512 devices in a mesh: dp: 4 (over z_hi), seq: 64 (over z_lo, y, x), chan: 2 (over core).
Axes of the slice: x: 4, y: 8, z: 8 (z_hi: 4, z_lo: 2; z = z_hi * 2 + z_lo), core: 2. Of those that a mesh axis runs over, the one named last changes fastest.
Arguments:
- signal: bfloat16 [4, 8192, 512], P('dp', 'seq', 'chan'), may hold values from -6 to 6
- gating: bfloat16 [4, 8192, 512], P('dp', 'seq', 'chan'), may hold values from -6 to 6
- cotangent: bfloat16 [4, 8192, 8192], P('dp', 'seq', 'chan'), may hold values from -6 to 6
- filt: float32 [8192, 512], P('seq', 'chan'), may hold values from -1 to 1
- skip: float32 [512], P('chan'), may hold values from -3 to 3
- output_projection: bfloat16 [512, 8192], P('chan', 'dp'), may hold values from -0.0625 to 0.0625
- adapter_down_bank: bfloat16 [2, 512, 16], P(None, 'chan'), may hold values from -0.25 to 0.25
- adapter_up_bank: bfloat16 [2, 16, 8192], P(None, None, 'chan'), may hold values from -0.0625 to 0.0625
- adapter_index: int32 [4], P('dp'), may hold values from 0 to 1
- sequence_rank: int32 [4], P('dp'), may hold values from 1 to 16, as said below
- real_length: int32 [4], P('dp'), may hold values from 4096 to 8192, as said below
Outputs:
- grad_signal: bfloat16 [4, 8192, 512], P('dp', 'seq', 'chan')
- grad_gating: bfloat16 [4, 8192, 512], P('dp', 'seq', 'chan')
- grad_filt: float32 [8192, 512], P('seq', 'chan')
- grad_skip: float32 [512], P('chan')
- grad_a: float32 [2, 512, 16], P(None, 'chan')
- grad_b: float32 [2, 16, 8192], P(None, None, 'chan')
The draws below stay inside these ranges and needn't reach their ends.
Inputs may be any that keep to these rules, and one draw needn't show every extreme that they name: `sequence_rank`: the first sequence uses all 16 ranks. Positions from real_length on are padding; the first sequence has none.
All inputs are finite; a program needn't handle non-finite values.
Results may differ from the reference program's by a relative error of at most 0.0052.
Values may be sent and summed in bfloat16 or wider, within the bound.
A program may use at most 64 MiB of HBM per device.

```python
import jax
import jax.numpy as jnp

MODEL_WIDTH = 8192
SLAB_CHANNELS = 512
MAX_RANK = 16
ADAPTER_COUNT = 2
L = 8192
BATCH = 4


def draw_filt(key, part):
    key = jax.random.fold_in(key, 7)
    rate_key, noise_key = jax.random.split(key)
    log_rates = jax.random.uniform(rate_key, (SLAB_CHANNELS,), jnp.float32, jnp.log(0.5 / L), jnp.log(1.0 / 40.0))
    noise = jnp.clip(jax.random.normal(noise_key, (L, SLAB_CHANNELS), jnp.float32), -4.0, 4.0)
    rates = jnp.exp(log_rates)
    steps_along = jnp.arange(L, dtype=jnp.float32)[:, None]
    return (jnp.sqrt(2.0 * rates) * noise * jnp.exp(-rates * steps_along)).astype(jnp.float32)


def draw_sequence_rank(key, part):
    key = jax.random.fold_in(key, 11)
    drawn = jax.random.randint(key, (BATCH,), 1, MAX_RANK + 1)
    return jnp.where(jnp.arange(BATCH) == 0, MAX_RANK, drawn).astype(jnp.int32)


def draw_real_length(key, part):
    key = jax.random.fold_in(key, 13)
    drawn = jax.random.randint(key, (BATCH,), L // 2, L + 1)
    return jnp.where(jnp.arange(BATCH) == 0, L, drawn).astype(jnp.int32)


def set_ends(values, key, least, top_value):
    longest = values.shape.index(max(values.shape))
    spots = []
    for shift in (0, 1):
        where = [jax.random.randint(jax.random.fold_in(key, axis), (), 0, length) for axis, length in enumerate(values.shape)]
        where[longest] = (where[longest] + shift) % values.shape[longest]
        spots.append(tuple(where))
    return values.at[spots[0]].set(least).at[spots[1]].set(top_value)


def level_of(stream_key, extent, cuts, least, largest):
    level, own = 1.0, jax.random.fold_in(stream_key, 6)
    for position, parts in cuts:
        heights = jnp.exp(jax.random.uniform(jax.random.fold_in(own, position), (parts,), jnp.float32, least / len(cuts), largest / len(cuts)))
        level = level * jnp.repeat(heights, extent[position] // parts).reshape([-1 if axis == position else 1 for axis in range(len(extent))])
    return level


def gaussian(key, shape, scale, bound, shards=(), kind=jnp.bfloat16):
    gain = level_of(key, shape, shards, -0.22, 0.18) if shards else 1.0
    values = jax.random.normal(key, shape, jnp.float32) * scale * gain
    return jnp.minimum(jnp.maximum(values, -bound), bound).astype(kind)


def setup_inputs(seed: int = 0) -> dict:
    key_list = jax.random.split(jax.random.key(seed), 12)
    signal = gaussian(key_list[0], (BATCH, L, SLAB_CHANNELS), 1.0, 6.0, ((0, 4), (1, 64), (2, 2)))
    gating = gaussian(key_list[1], (BATCH, L, SLAB_CHANNELS), 1.0, 6.0, ((0, 4), (1, 64), (2, 2)))
    cotangent = gaussian(key_list[2], (BATCH, L, MODEL_WIDTH), 1.0, 6.0, ((0, 4), (1, 64), (2, 2)))
    filt = draw_filt(jax.random.fold_in(key_list[11], 71), 0)
    skip = gaussian(key_list[4], (SLAB_CHANNELS,), 1.0, 3.0, ((0, 2),), jnp.float32)
    output_projection = gaussian(key_list[5], (SLAB_CHANNELS, MODEL_WIDTH), MODEL_WIDTH ** -0.5, 0.0625, ((0, 2), (1, 4)))
    adapter_down_bank = gaussian(key_list[6], (ADAPTER_COUNT, SLAB_CHANNELS, MAX_RANK), SLAB_CHANNELS ** -0.5, 0.25, ((1, 2),))
    adapter_up_bank = gaussian(key_list[7], (ADAPTER_COUNT, MAX_RANK, MODEL_WIDTH), MODEL_WIDTH ** -0.5, 0.0625, ((2, 2),))
    adapter_index = set_ends(jax.random.randint(key_list[8], (BATCH,), 0, ADAPTER_COUNT), jax.random.fold_in(key_list[8], 1), 0, ADAPTER_COUNT - 1).astype(jnp.int32)
    sequence_rank = draw_sequence_rank(jax.random.fold_in(key_list[11], 71), 0)
    real_length = draw_real_length(jax.random.fold_in(key_list[11], 71), 0)
    return {"signal": signal, "gating": gating, "cotangent": cotangent, "filt": filt, "skip": skip, "output_projection": output_projection, "adapter_down_bank": adapter_down_bank, "adapter_up_bank": adapter_up_bank, "adapter_index": adapter_index, "sequence_rank": sequence_rank, "real_length": real_length}


ADAPTER_SCALE = 2.0


def causal_conv(first, second):
    length = first.shape[0]
    spec = jnp.fft.rfft(first, n=2 * length, axis=0) * jnp.fft.rfft(second, n=2 * length, axis=0)
    return jnp.fft.irfft(spec, n=2 * length, axis=0)[:length]


def causal_corr(first, second):
    length = first.shape[0]
    spec = jnp.fft.rfft(first, n=2 * length, axis=0) * jnp.conj(jnp.fft.rfft(second, n=2 * length, axis=0))
    return jnp.fft.irfft(spec, n=2 * length, axis=0)[:length]


def reference(signal, gating, cotangent, filt, skip, output_projection, adapter_down_bank, adapter_up_bank, adapter_index, sequence_rank, real_length):
    positions = jnp.arange(L, dtype=jnp.int32)
    rank_index = jnp.arange(MAX_RANK, dtype=jnp.int32)
    grads_signal = []
    grads_gating = []
    grad_filt = jnp.zeros((L, SLAB_CHANNELS), jnp.float32)
    grad_skip = jnp.zeros((SLAB_CHANNELS,), jnp.float32)
    grad_a = jnp.zeros((ADAPTER_COUNT, SLAB_CHANNELS, MAX_RANK), jnp.float32)
    grad_b = jnp.zeros((ADAPTER_COUNT, MAX_RANK, MODEL_WIDTH), jnp.float32)
    for batch_entry in range(BATCH):
        source = signal[batch_entry].astype(jnp.float32)
        gate_row = gating[batch_entry].astype(jnp.float32)
        live = positions < real_length[batch_entry]
        masked = jnp.where(live[:, None], cotangent[batch_entry], jnp.zeros_like(cotangent[batch_entry]))
        chosen_down_maps = adapter_down_bank[adapter_index[batch_entry]]
        chosen_up_maps = adapter_up_bank[adapter_index[batch_entry]]
        rank_mask = (rank_index < sequence_rank[batch_entry]).astype(jnp.float32)
        inner = causal_conv(source, filt) + skip * source
        gated = (gate_row * inner).astype(jnp.bfloat16)
        down_projected = jnp.dot(masked, chosen_up_maps.T, preferred_element_type=jnp.float32)
        backward_rank = (ADAPTER_SCALE * down_projected * rank_mask).astype(jnp.bfloat16)
        grad_y = jnp.dot(masked, output_projection.T, preferred_element_type=jnp.float32) + jnp.dot(backward_rank, chosen_down_maps.T, preferred_element_type=jnp.float32)
        grads_gating.append((grad_y * inner).astype(jnp.bfloat16))
        grad_u = grad_y * gate_row
        grads_signal.append((causal_corr(grad_u, filt) + skip * grad_u).astype(jnp.bfloat16))
        grad_filt = grad_filt + causal_corr(grad_u, source)
        grad_skip = grad_skip + jnp.sum(grad_u * source, axis=0)
        up_projected = jnp.dot(gated, chosen_down_maps, preferred_element_type=jnp.float32)
        forward_rank = (ADAPTER_SCALE * up_projected * rank_mask).astype(jnp.bfloat16)
        selected_values = (jnp.arange(ADAPTER_COUNT, dtype=jnp.int32) == adapter_index[batch_entry]).astype(jnp.float32)
        grad_a = grad_a + selected_values[:, None, None] * jnp.dot(gated.T, backward_rank, preferred_element_type=jnp.float32)[None]
        grad_b = grad_b + selected_values[:, None, None] * jnp.dot(forward_rank.T, masked, preferred_element_type=jnp.float32)[None]
    return jnp.stack(grads_signal), jnp.stack(grads_gating), grad_filt, grad_skip, grad_a, grad_b
```

```python
import functools
import math

import jax
import jax.numpy as jnp
import ml_dtypes
import numpy as np
from jax import lax
from jax.experimental import pallas as pl
from jax.experimental.pallas import tpu as pltpu
from jax.sharding import PartitionSpec as P

MESH = pl.DeviceIdType.MESH
BF = jnp.bfloat16
F32 = jnp.float32
LANES = 128
PER = 4
HALF_ROWS = 8


def split3(table, axis, order):
    high = table.astype(ml_dtypes.bfloat16)
    low = (table - high.astype(np.float64)).astype(ml_dtypes.bfloat16)
    return np.concatenate([high if o else low for o in order], axis=axis)


def tables(n):
    rows = -(-(n + 1) // 8) * 8
    k1 = np.arange(rows)
    used = (k1 <= n).astype(np.float64)
    i = np.arange(n)
    a = np.arange(LANES)
    period = 2 * n * LANES
    th1 = 2 * math.pi * (k1[:, None] * i[None, :] % (2 * n)) / (2 * n)
    first = np.concatenate([np.cos(th1) * used[:, None], -np.sin(th1) * used[:, None]], 0)
    thw = 2 * math.pi * (k1[:, None] * a[None, :] % period) / period
    tw_cos, tw_sin = np.cos(thw), np.sin(thw)
    th2 = 2 * math.pi * (a[:, None] * a[None, :] % LANES) / LANES
    c2, s2 = np.cos(th2), np.sin(th2)
    second = np.block([[c2, -s2], [s2, c2]])
    second_back = np.block([[c2, s2], [-s2, c2]])
    weight = used * np.where((k1 == 0) | (k1 == n), 1.0, 2.0) / period
    last = np.concatenate([np.cos(th1).T * weight, -np.sin(th1).T * weight], 1)
    return (
        split3(first, 1, (1, 1, 0)),
        split3(second, 0, (1, 1, 0)),
        split3(second_back, 0, (1, 1, 0)),
        split3(last, 1, (1, 1, 0)),
        tw_cos.astype(np.float32),
        tw_sin.astype(np.float32),
    )


def split_data(x, axis):
    high = x.astype(BF)
    low = (x - high.astype(F32)).astype(BF)
    return jnp.concatenate([high, low, high], axis=axis)


def dot(a, b):
    return jnp.dot(a, b, preferred_element_type=F32)


def dot_t(a, b):
    return lax.dot_general(a, b, (((1,), (1,)), ((), ())), preferred_element_type=F32)


def dot_0(a, b):
    return lax.dot_general(a, b, (((0,), (0,)), ((), ())), preferred_element_type=F32)


def kernel(
    n,
    index_ref, rank_ref, length_ref,
    signal_ref, gating_ref, cot_ref, filt_ref, skip_ref, w_ref, down_ref, up_ref,
    t1_ref, t2_ref, t2b_ref, t1b_ref, tc_ref, ts_ref,
    gsig_ref, ggat_ref, gfilt_ref, gskip_ref, ga_ref, gb_ref,
    masked, sig_t, gate_t, grady_t, spec_s, spec_f, spec_g,
    sf_send, sf_recv, c_send, c_recv, u_send, u_recv, k_send, k_recv,
    m_recv, w_recv, pre_send, pre_recv, own_part, ret_send, ret_recv,
    d_send, d_recv, r_send, r_recv,
    b_send, b_recv, q_send, q_recv, g_send, g_recv, f_send, f_recv,
    a2a_send_sem, a2a_recv_sem, m_send_sem, m_recv_sem, w_sem, pre_send_sem, pre_recv_sem,
    ret_send_sem, ret_recv_sem, d_sem, r_sem, b_sem, q_send_sem, q_recv_sem, g_sem,
    f_send_sem, f_recv_sem,
):
    dp = lax.axis_index("dp")
    me = lax.axis_index("seq")
    ch = lax.axis_index("chan")
    other = 1 - ch
    width = w_ref.shape[0]
    cols = w_ref.shape[1] // 2
    half = cot_ref.shape[1]
    n_own = b_send.shape[1] // LANES
    rows = t1_ref.shape[0] // 2
    up_chunks = half // LANES
    a_chunks = -(-width // LANES)

    barrier = pltpu.get_barrier_semaphore()

    def greet(d, _):
        pl.semaphore_signal(
            barrier, inc=1, device_id=(dp, lax.rem(me + d, n), ch), device_id_type=MESH
        )
        return 0

    lax.fori_loop(1, n, greet, 0)
    for d in range(4):
        for c in range(2):
            if d or c:
                pl.semaphore_signal(
                    barrier, inc=1, device_id=(lax.rem(dp + d, 4), me, lax.rem(ch + c, 2)),
                    device_id_type=MESH,
                )

    sig_t[...] = signal_ref[...].astype(F32).T
    gate_t[...] = gating_ref[...].astype(F32).T
    filt_t = filt_ref[...].T
    for cc in range(PER):
        sf_send[pl.ds(cc, n, stride=8), :] = sig_t[cc * n:(cc + 1) * n, :]
        sf_send[pl.ds(PER + cc, n, stride=8), :] = filt_t[cc * n:(cc + 1) * n, :]
    real_length = length_ref[0]
    live_col = (me * LANES + lax.broadcasted_iota(jnp.int32, (LANES, 1), 0) < real_length).astype(F32)
    live_row = (me * LANES + lax.broadcasted_iota(jnp.int32, (1, LANES), 1) < real_length).astype(F32)
    masked[...] = (cot_ref[...].astype(F32) * live_col).astype(BF)
    pick1 = index_ref[0].astype(F32)
    pick0 = 1.0 - pick1
    up_sel = (up_ref[0].astype(F32) * pick0 + up_ref[1].astype(F32) * pick1).astype(BF)
    down_sel = (down_ref[0].astype(F32) * pick0 + down_ref[1].astype(F32) * pick1).astype(BF)
    max_rank = up_sel.shape[0]
    keep = (lax.broadcasted_iota(jnp.int32, (max_rank, LANES), 0) < rank_ref[0]).astype(F32)

    pl.semaphore_wait(barrier, n - 1 + 7)

    def cot_copy(qq, hh):
        return pltpu.make_async_remote_copy(
            src_ref=cot_ref.at[:, pl.ds((2 * qq + hh) * cols, cols)],
            dst_ref=m_recv.at[dp],
            send_sem=m_send_sem.at[2 * qq + hh],
            recv_sem=m_recv_sem.at[dp],
            device_id=(2 * ch + qq, me, hh),
            device_id_type=MESH,
        )

    def cot_self(qq, hh):
        return (2 * ch + qq == dp) & (ch == hh)

    for qq in range(2):
        for hh in range(2):
            @pl.when(jnp.logical_not(cot_self(qq, hh)))
            def _():
                cot_copy(qq, hh).start()

            @pl.when(cot_self(qq, hh))
            def _():
                pltpu.make_async_copy(
                    cot_ref.at[:, pl.ds((2 * qq + hh) * cols, cols)], m_recv.at[dp], m_recv_sem.at[dp]
                ).start()

    def a2a_start(k, src, dst, size):
        def body(d, _):
            j = lax.rem(me + d, n)
            pltpu.make_async_remote_copy(
                src_ref=src.at[pl.ds(pl.multiple_of(j * size, size), size), :],
                dst_ref=dst.at[pl.ds(pl.multiple_of(me * size, size), size), :],
                send_sem=a2a_send_sem.at[k],
                recv_sem=a2a_recv_sem.at[k],
                device_id=(dp, j, ch),
                device_id_type=MESH,
            ).start()
            return 0

        lax.fori_loop(1, n, body, 0)
        mine = pl.ds(pl.multiple_of(me * size, size), size)
        pltpu.make_async_copy(src.at[mine, :], dst.at[mine, :], a2a_recv_sem.at[k]).start()

    def a2a_wait(k, dst):
        pltpu.make_async_copy(dst, dst, a2a_recv_sem.at[k]).wait()

    def a2a_wait_send(k, src, size):
        part = src.at[pl.ds(0, (n - 1) * size), :]
        pltpu.make_async_copy(part, part, a2a_send_sem.at[k]).wait()

    a2a_start(0, sf_send, sf_recv, 8)

    def to_chan(src, dst, send_sem, recv_sem):
        return pltpu.make_async_remote_copy(
            src_ref=src, dst_ref=dst, send_sem=send_sem, recv_sem=recv_sem,
            device_id=(dp, me, other), device_id_type=MESH,
        )

    w_copy = to_chan(
        w_ref.at[:, pl.ds(pl.multiple_of(other * cols, LANES), cols)], w_recv, w_sem.at[0], w_sem.at[1]
    )
    w_copy.start()
    d_send[...] = dot_t(up_sel, masked[...])
    d_copy = to_chan(d_send, d_recv, d_sem.at[0], d_sem.at[1])
    d_copy.start()

    tc, ts = tc_ref[...], ts_ref[...]

    def forward(load, store):
        x = jnp.concatenate([load(cc) for cc in range(PER)], axis=1)
        y = dot(t1_ref[...], split_data(x, 0))
        parts = []
        for cc in range(PER):
            re = y[:rows, cc * LANES:(cc + 1) * LANES]
            im = y[rows:, cc * LANES:(cc + 1) * LANES]
            parts.append(jnp.concatenate([re * tc + im * ts, im * tc - re * ts], axis=1))
        store[...] = dot(split_data(jnp.concatenate(parts, axis=0), 1), t2_ref[...])

    def inverse(re, im):
        q = dot(split_data(jnp.concatenate([re, im], axis=1), 1), t2b_ref[...])
        parts = []
        for cc in range(PER):
            qr = q[cc * rows:(cc + 1) * rows, :LANES]
            qi = q[cc * rows:(cc + 1) * rows, LANES:]
            parts.append(jnp.concatenate([qr * tc - qi * ts, qi * tc + qr * ts], axis=0))
        return dot(t1b_ref[...], split_data(jnp.concatenate(parts, axis=1), 0))

    a2a_wait(0, sf_recv)
    forward(lambda cc: sf_recv[pl.ds(cc, n, stride=8), :], spec_s)
    forward(lambda cc: sf_recv[pl.ds(PER + cc, n, stride=8), :], spec_f)
    s_re, s_im = spec_s[:, :LANES], spec_s[:, LANES:]
    f_re, f_im = spec_f[:, :LANES], spec_f[:, LANES:]
    conv = inverse(s_re * f_re - s_im * f_im, s_re * f_im + s_im * f_re)
    for cc in range(PER):
        c_send[pl.ds(cc, n, stride=HALF_ROWS), :] = conv[:, cc * LANES:(cc + 1) * LANES]
    a2a_start(1, c_send, c_recv, HALF_ROWS)

    d_copy.wait()
    back_rank = (2.0 * (d_send[...] + d_recv[...]) * keep).astype(BF)

    w_copy.wait_recv()
    order = (0, 1, 3, 2)
    own_cols = pl.ds(pl.multiple_of(ch * cols, LANES), cols)
    pre_copies, ret_copies = [], []

    def finish(slot):
        b = lax.rem(dp + order[slot], 4)
        pre_copies[slot].wait_recv()
        total = own_part[slot] + pre_recv[slot].astype(F32)
        if slot == 0:
            grady_t[...] = total
            return
        ret_send[slot] = total.astype(BF)
        copy = pltpu.make_async_remote_copy(
            src_ref=ret_send.at[slot], dst_ref=ret_recv.at[dp],
            send_sem=ret_send_sem.at[slot], recv_sem=ret_recv_sem.at[dp],
            device_id=(b, me, ch), device_id_type=MESH,
        )
        copy.start()
        ret_copies.append(copy)

    for slot in range(4):
        b = lax.rem(dp + order[slot], 4)
        pltpu.make_async_copy(m_recv.at[b], m_recv.at[b], m_recv_sem.at[b]).wait()
        piece = m_recv[b]
        pre_send[slot] = dot_t(w_recv[...], piece).astype(BF)
        copy = to_chan(pre_send.at[slot], pre_recv.at[slot], pre_send_sem.at[slot], pre_recv_sem.at[slot])
        copy.start()
        pre_copies.append(copy)
        own_part[slot] = dot_t(w_ref[:, own_cols], piece)
        if slot:
            finish(slot - 1)
    finish(3)

    skip_t = jnp.broadcast_to(skip_ref[...], (LANES, width)).T
    a2a_wait(1, c_recv)
    conv_t = jnp.concatenate(
        [c_recv[pl.ds(cc, n, stride=HALF_ROWS), :] for cc in range(PER)], axis=0
    )
    inner_t = conv_t + skip_t * sig_t[...]
    gated_t = (gate_t[...] * inner_t).astype(BF)
    r_send[...] = dot_0(down_sel, gated_t)
    r_copy = to_chan(r_send, r_recv, r_sem.at[0], r_sem.at[1])
    r_copy.start()

    total = grady_t[...]
    for step in (1, 3, 2):
        q = lax.rem(dp + step, 4)
        pltpu.make_async_copy(ret_recv.at[q], ret_recv.at[q], ret_recv_sem.at[q]).wait()
        total = total + ret_recv[q].astype(F32)
    grad_y = total * live_row + dot(down_sel, back_rank)
    grad_u = grad_y * gate_t[...]
    grady_t[...] = grad_u
    for cc in range(PER):
        u_send[pl.ds(cc, n, stride=HALF_ROWS), :] = grady_t[cc * n:(cc + 1) * n, :]
    a2a_start(2, u_send, u_recv, HALF_ROWS)
    ggat_ref[...] = (grad_y * inner_t).T.astype(BF)

    r_copy.wait()
    fwd_rank = (2.0 * (r_send[...] + r_recv[...]) * keep).astype(BF)
    b_send[:, :half] = dot(fwd_rank, masked[...]).astype(BF)
    b_send[:, half:half + width] = dot_t(back_rank, gated_t).astype(BF)
    product = grad_u * sig_t[...]
    high = product.astype(BF)
    low = (product - high.astype(F32)).astype(BF)
    ones = jnp.ones((max_rank, LANES), BF)
    b_send[:, half + a_chunks * LANES:half + a_chunks * LANES + width] = (
        dot_t(ones, high) + dot_t(ones, low)
    ).astype(BF)

    def share(d, _):
        p = lax.rem(me + d, n_own)
        src = b_send.at[:, pl.ds(pl.multiple_of(p * LANES, LANES), LANES)]
        dst = b_recv.at[pl.ds(pl.multiple_of(me * 16, 16), 16), :]

        @pl.when(p != me)
        def _():
            pltpu.make_async_remote_copy(
                src_ref=src, dst_ref=dst, send_sem=b_sem.at[0], recv_sem=b_sem.at[1],
                device_id=(dp, p, ch), device_id_type=MESH,
            ).start()

        @pl.when(p == me)
        def _():
            pltpu.make_async_copy(src, dst, b_sem.at[1]).start()
        return 0

    lax.fori_loop(0, n_own, share, 0)

    a2a_wait(2, u_recv)
    forward(lambda cc: u_recv[pl.ds(cc, n, stride=HALF_ROWS), :], spec_g)
    g_re, g_im = spec_g[:, :LANES], spec_g[:, LANES:]
    s_re, s_im = spec_s[:, :LANES], spec_s[:, LANES:]
    f_re, f_im = spec_f[:, :LANES], spec_f[:, LANES:]
    corr_f = inverse(g_re * f_re + g_im * f_im, g_im * f_re - g_re * f_im)
    corr_s = inverse(g_re * s_re + g_im * s_im, g_im * s_re - g_re * s_im)
    for cc in range(PER):
        k_send[pl.ds(cc, n, stride=8), :] = corr_f[:, cc * LANES:(cc + 1) * LANES]
        k_send[pl.ds(PER + cc, n, stride=8), :] = corr_s[:, cc * LANES:(cc + 1) * LANES]
    a2a_start(3, k_send, k_recv, 8)

    is_owner = me < n_own

    def q_copy(step):
        return pltpu.make_async_remote_copy(
            src_ref=q_send, dst_ref=q_recv.at[dp], send_sem=q_send_sem.at[step], recv_sem=q_recv_sem.at[dp],
            device_id=(lax.rem(dp + step, 4), me, ch), device_id_type=MESH,
        )

    @pl.when(is_owner)
    def _():
        pltpu.make_async_copy(b_recv, b_recv, b_sem.at[1]).wait()
        acc = b_recv[0:16, :].astype(F32)
        for i in range(1, n):
            acc = acc + b_recv[16 * i:16 * (i + 1), :].astype(F32)
        q_send[...] = jnp.concatenate([acc * pick0, acc * pick1], axis=0)
        for step in (1, 3, 2):
            q_copy(step).start()

    a2a_wait(3, k_recv)
    corr_st = jnp.concatenate(
        [k_recv[pl.ds(PER + cc, n, stride=8), :] for cc in range(PER)], axis=0
    )
    f_send[...] = corr_st.astype(BF)
    f_copies = []
    for step in (1, 3, 2):
        copy = pltpu.make_async_remote_copy(
            src_ref=f_send, dst_ref=f_recv.at[dp], send_sem=f_send_sem.at[step], recv_sem=f_recv_sem.at[dp],
            device_id=(lax.rem(dp + step, 4), me, ch), device_id_type=MESH,
        )
        copy.start()
        f_copies.append(copy)

    g_size = 2 * max_rank

    @pl.when(is_owner)
    def _():
        sums = q_send[...]
        for step in (1, 3, 2):
            q = lax.rem(dp + step, 4)
            pltpu.make_async_copy(q_recv.at[q], q_recv.at[q], q_recv_sem.at[q]).wait()
            sums = sums + q_recv[q]
        g_send[...] = sums.astype(BF)
        mine = pl.ds(pl.multiple_of(me * g_size, g_size), g_size)

        def spread(d, _):
            pltpu.make_async_remote_copy(
                src_ref=g_send, dst_ref=g_recv.at[mine, :], send_sem=g_sem.at[0], recv_sem=g_sem.at[1],
                device_id=(dp, lax.rem(me + d, n), ch), device_id_type=MESH,
            ).start()
            return 0

        lax.fori_loop(1, n, spread, 0)
        pltpu.make_async_copy(g_send, g_recv.at[mine, :], g_sem.at[1]).start()

    corr_ft = jnp.concatenate(
        [k_recv[pl.ds(cc, n, stride=8), :] for cc in range(PER)], axis=0
    )
    gsig_ref[...] = (corr_ft + skip_t * grady_t[...]).T.astype(BF)

    sums = corr_st
    for step in (1, 3, 2):
        q = lax.rem(dp + step, 4)
        pltpu.make_async_copy(f_recv.at[q], f_recv.at[q], f_recv_sem.at[q]).wait()
        sums = sums + f_recv[q].astype(F32)
    gfilt_ref[...] = sums.T

    pltpu.make_async_copy(g_recv, g_recv, g_sem.at[1]).wait()

    def place(p, _):
        block = g_recv[pl.ds(pl.multiple_of(p * g_size, g_size), g_size), :].astype(F32)
        where = pl.ds(pl.multiple_of(p * LANES, LANES), LANES)
        gb_ref[0, :, where] = block[:max_rank]
        gb_ref[1, :, where] = block[max_rank:]
        return 0

    lax.fori_loop(0, up_chunks, place, 0)
    for k in range(a_chunks):
        size = min(LANES, width)
        at = (up_chunks + k) * g_size
        block = g_recv[at:at + g_size, :].astype(F32)
        ga_ref[0, :, k * size:(k + 1) * size] = block[:max_rank, :size]
        ga_ref[1, :, k * size:(k + 1) * size] = block[max_rank:, :size]
        at = (up_chunks + a_chunks + k) * g_size
        block = g_recv[at:at + g_size, :].astype(F32)
        gskip_ref[:, k * size:(k + 1) * size] = (block[:max_rank] + block[max_rank:])[:8, :size]

    for qq in range(2):
        for hh in range(2):
            @pl.when(jnp.logical_not(cot_self(qq, hh)))
            def _():
                cot_copy(qq, hh).wait_send()
    a2a_wait_send(0, sf_send, 8)
    a2a_wait_send(1, c_send, HALF_ROWS)
    a2a_wait_send(2, u_send, HALF_ROWS)
    a2a_wait_send(3, k_send, 8)
    w_copy.wait_send()
    for copy in pre_copies + ret_copies + f_copies:
        copy.wait_send()

    def b_sent(count):
        part = b_send.at[:, pl.ds(0, count * LANES)]
        pltpu.make_async_copy(part, part, b_sem.at[0]).wait()

    @pl.when(is_owner)
    def _():
        b_sent(n_own - 1)
        for step in (1, 3, 2):
            q_copy(step).wait_send()

        def sent(d, _):
            pltpu.make_async_copy(g_send, g_send, g_sem.at[0]).wait()
            return 0

        lax.fori_loop(1, n, sent, 0)

    @pl.when(jnp.logical_not(is_owner))
    def _():
        b_sent(n_own)


def local(
    signal, gating, cotangent, filt, skip, output_projection,
    adapter_down_bank, adapter_up_bank, adapter_index, sequence_rank, real_length,
):
    n = lax.axis_size("seq")
    width = signal.shape[2]
    half = cotangent.shape[2]
    cols = output_projection.shape[1] // 2
    max_rank = adapter_up_bank.shape[1]
    a_chunks = -(-width // LANES)
    n_own = half // LANES + 2 * a_chunks
    consts = [jnp.asarray(t) for t in tables(n)]
    rows = consts[4].shape[0]
    vmem = pl.BlockSpec(memory_space=pltpu.VMEM)
    smem = pl.BlockSpec(memory_space=pltpu.SMEM)
    dma = pltpu.SemaphoreType.DMA
    outs = pl.pallas_call(
        functools.partial(kernel, n),
        out_shape=(
            jax.ShapeDtypeStruct((LANES, width), BF),
            jax.ShapeDtypeStruct((LANES, width), BF),
            jax.ShapeDtypeStruct((LANES, width), F32),
            jax.ShapeDtypeStruct((8, width), F32),
            jax.ShapeDtypeStruct((2, max_rank, width), F32),
            jax.ShapeDtypeStruct((2, max_rank, half), F32),
        ),
        in_specs=[smem] * 3 + [vmem] * 14,
        out_specs=(vmem,) * 6,
        scratch_shapes=[
            pltpu.VMEM((LANES, half), BF),
            pltpu.VMEM((width, LANES), F32),
            pltpu.VMEM((width, LANES), F32),
            pltpu.VMEM((width, LANES), F32),
            pltpu.VMEM((PER * rows, 2 * LANES), F32),
            pltpu.VMEM((PER * rows, 2 * LANES), F32),
            pltpu.VMEM((PER * rows, 2 * LANES), F32),
            pltpu.VMEM((8 * n, LANES), F32),
            pltpu.VMEM((8 * n, LANES), F32),
            pltpu.VMEM((HALF_ROWS * n, LANES), F32),
            pltpu.VMEM((HALF_ROWS * n, LANES), F32),
            pltpu.VMEM((HALF_ROWS * n, LANES), F32),
            pltpu.VMEM((HALF_ROWS * n, LANES), F32),
            pltpu.VMEM((8 * n, LANES), F32),
            pltpu.VMEM((8 * n, LANES), F32),
            pltpu.VMEM((4, LANES, cols), BF),
            pltpu.VMEM((width, cols), BF),
            pltpu.VMEM((4, width, LANES), BF),
            pltpu.VMEM((4, width, LANES), BF),
            pltpu.VMEM((4, width, LANES), F32),
            pltpu.VMEM((4, width, LANES), BF),
            pltpu.VMEM((4, width, LANES), BF),
            pltpu.VMEM((max_rank, LANES), F32),
            pltpu.VMEM((max_rank, LANES), F32),
            pltpu.VMEM((max_rank, LANES), F32),
            pltpu.VMEM((max_rank, LANES), F32),
            pltpu.VMEM((max_rank, n_own * LANES), BF),
            pltpu.VMEM((16 * n, LANES), BF),
            pltpu.VMEM((2 * max_rank, LANES), F32),
            pltpu.VMEM((4, 2 * max_rank, LANES), F32),
            pltpu.VMEM((2 * max_rank, LANES), BF),
            pltpu.VMEM((2 * max_rank * n_own, LANES), BF),
            pltpu.VMEM((width, LANES), BF),
            pltpu.VMEM((4, width, LANES), BF),
            dma((4,)), dma((4,)), dma((4,)), dma((4,)), dma((2,)), dma((4,)), dma((4,)),
            dma((4,)), dma((4,)), dma((2,)), dma((2,)), dma((2,)), dma((4,)), dma((4,)), dma((2,)),
            dma((4,)), dma((4,)),
        ],
        compiler_params=pltpu.CompilerParams(
            collective_id=0, has_side_effects=True, vmem_limit_bytes=40 * 1024 * 1024
        ),
    )(
        adapter_index, sequence_rank, real_length,
        signal[0], gating[0], cotangent[0], filt, skip[None], output_projection,
        adapter_down_bank, adapter_up_bank, *consts,
    )
    grad_signal, grad_gating, grad_filt, grad_skip, grad_a, grad_b = outs
    return (
        grad_signal[None], grad_gating[None], grad_filt, grad_skip[0],
        jnp.swapaxes(grad_a, 1, 2), grad_b,
    )


def solution(mesh):
    placed = (
        P("dp", "seq", "chan"), P("dp", "seq", "chan"), P("dp", "seq", "chan"), P("seq", "chan"),
        P("chan"), P("chan", "dp"), P(None, "chan", None), P(None, None, "chan"),
        P("dp"), P("dp"), P("dp"),
    )
    return jax.shard_map(
        local,
        mesh=mesh,
        in_specs=placed,
        out_specs=(
            P("dp", "seq", "chan"), P("dp", "seq", "chan"), P("seq", "chan"), P("chan"),
            P(None, "chan", None), P(None, None, "chan"),
        ),
        check_vma=False,
    )
```

```python
import functools
import math

import jax
import jax.numpy as jnp
import ml_dtypes
import numpy as np
from jax import lax
from jax.experimental import pallas as pl
from jax.experimental.pallas import tpu as pltpu
from jax.sharding import PartitionSpec as P

MESH = pl.DeviceIdType.MESH
BF = jnp.bfloat16
F32 = jnp.float32
LANES = 128
PER = 4
VMEM_LIMIT = 62 * 1024 * 1024
SUB = 2


def split3(table, axis, order):
    high = table.astype(ml_dtypes.bfloat16)
    low = (table - high.astype(np.float64)).astype(ml_dtypes.bfloat16)
    return np.concatenate([high if o else low for o in order], axis=axis)


def tables(n):
    rows = -(-(n + 1) // 8) * 8
    k1 = np.arange(rows)
    used = (k1 <= n).astype(np.float64)
    i = np.arange(n)
    a = np.arange(LANES)
    period = 2 * n * LANES
    th1 = 2 * math.pi * (k1[:, None] * i[None, :] % (2 * n)) / (2 * n)
    first = np.concatenate([np.cos(th1) * used[:, None], -np.sin(th1) * used[:, None]], 0)
    thw = 2 * math.pi * (k1[:, None] * a[None, :] % period) / period
    tw_cos, tw_sin = np.cos(thw), np.sin(thw)
    th2 = 2 * math.pi * (a[:, None] * a[None, :] % LANES) / LANES
    c2, s2 = np.cos(th2), np.sin(th2)
    second = np.block([[c2, -s2], [s2, c2]])
    second_back = np.block([[c2, s2], [-s2, c2]])
    weight = used * np.where((k1 == 0) | (k1 == n), 1.0, 2.0) / period
    last = np.concatenate([np.cos(th1).T * weight, -np.sin(th1).T * weight], 1)
    return (
        split3(first, 1, (1, 1, 0)),
        split3(second, 0, (1, 1, 0)),
        split3(second_back, 0, (1, 1, 0)),
        split3(last, 1, (1, 1, 0)),
        tw_cos.astype(np.float32),
        tw_sin.astype(np.float32),
    )


def split_data(x, axis):
    high = x.astype(BF)
    low = (x - high.astype(F32)).astype(BF)
    return jnp.concatenate([high, low, high], axis=axis)


def dot(a, b):
    return jnp.dot(a, b, preferred_element_type=F32)


def dot_t(a, b):
    return lax.dot_general(a, b, (((1,), (1,)), ((), ())), preferred_element_type=F32)


def dot_0(a, b):
    return lax.dot_general(a, b, (((0,), (0,)), ((), ())), preferred_element_type=F32)


def kernel(
    n,
    index_ref, rank_ref, length_ref,
    signal_hbm, gating_hbm, cot_hbm, filt_hbm, skip_hbm, w_hbm, down_hbm, up_hbm,
    t1_hbm, t2_hbm, t2b_hbm, t1b_hbm, tc_hbm, ts_hbm,
    gsig_hbm, ggat_hbm, gfilt_hbm, gbank_hbm, gskip_hbm,
    gsig_ref, ggat_ref, gfilt_ref, gskip_ref,
    signal_ref, gating_ref, cot_ref, filt_ref, skip_ref, w_ref, down_ref, up_ref,
    t1_ref, t2_ref, t2b_ref, t1b_ref, tc_ref, ts_ref,
    masked, sig_t, gate_t, gradu_t, spec_s, spec_f, spec_g,
    sf_send, sf_recv, c_send, c_recv, u_send, u_recv, ks_send, ks_recv, kf_send, kf_recv,
    m_own, m_recv, w_recv, pre0_send, pre0_recv, pre_send, pre_recv, ret_send, ret_recv,
    d_send, d_recv, r_send, r_recv,
    b_send, b_recv, q_send, q_recv, g_send, g_recv, f_send, f_recv, e_send, e_recv,
    in_sem, out_sem, a2a_send_sem, a2a_recv_sem, m_send_sem, m_recv_sem, own_sem, w_sem, pre0_sem,
    pre_send_sem, pre_recv_sem, ret_send_sem, ret_recv_sem, d_sem, r_sem, b_sem,
    q_send_sem, q_recv_sem, g_sem, f_send_sem, f_recv_sem, e_send_sem, e_recv_sem,
):
    dp = lax.axis_index("dp")
    me = lax.axis_index("seq")
    ch = lax.axis_index("chan")
    other = 1 - ch
    plane = n // 2
    zl, spot = lax.div(me, plane), lax.rem(me, plane)
    width = w_ref.shape[0]
    cols = w_ref.shape[1] // 2
    half = cot_ref.shape[1]
    piece = LANES // SUB
    n_own = b_send.shape[1] // LANES
    rows = t1_ref.shape[0] // 2
    a_chunks = -(-width // LANES)

    barrier = pltpu.get_barrier_semaphore()
    for d in range(4):
        for z in range(2):
            for c in range(2):
                if d or c:
                    pl.semaphore_signal(
                        barrier, inc=1,
                        device_id=(lax.rem(dp + d, 4), lax.rem(zl + z, 2) * plane + spot, lax.rem(ch + c, 2)),
                        device_id_type=MESH,
                    )

    def greet(d, _):
        pl.semaphore_signal(
            barrier, inc=1, device_id=(dp, lax.rem(me + d, n), ch), device_id_type=MESH
        )
        return 0

    lax.fori_loop(1, n, greet, 0, unroll=9 if n == 64 else 1)

    pairs = (
        (signal_hbm, signal_ref), (filt_hbm, filt_ref), (cot_hbm, cot_ref), (up_hbm, up_ref),
        (w_hbm, w_ref), (t1_hbm, t1_ref), (t2_hbm, t2_ref), (t2b_hbm, t2b_ref), (t1b_hbm, t1b_ref),
        (tc_hbm, tc_ref), (ts_hbm, ts_ref), (gating_hbm, gating_ref), (down_hbm, down_ref),
        (skip_hbm, skip_ref),
    )
    loads = [pltpu.make_async_copy(s, d, in_sem.at[i]) for i, (s, d) in enumerate(pairs)]
    for load in loads:
        load.start()

    loads[0].wait()
    loads[1].wait()
    sig_t[...] = signal_ref[...].astype(F32).T
    filt_t = filt_ref[...].T
    for cc in range(PER):
        sf_send[pl.ds(cc, n, stride=8), :] = sig_t[cc * n:(cc + 1) * n, :]
        sf_send[pl.ds(PER + cc, n, stride=8), :] = filt_t[cc * n:(cc + 1) * n, :]
    real_length = length_ref[0]
    live_col = (me * LANES + lax.broadcasted_iota(jnp.int32, (LANES, 1), 0) < real_length).astype(F32)
    live_row = (me * LANES + lax.broadcasted_iota(jnp.int32, (1, LANES), 1) < real_length).astype(F32)
    pick1 = index_ref[0].astype(F32)
    pick0 = 1.0 - pick1

    pl.semaphore_wait(barrier, n - 1 + 14)

    def cot_copy(sub, qq, hh):
        q = 2 * ch + qq
        step = lax.rem(q - dp + 4, 4)
        odd = lax.rem(step, 2)
        to_z = lax.div(step, 3) + (1 - odd) * (1 - zl)
        return pltpu.make_async_remote_copy(
            src_ref=cot_hbm.at[pl.ds(sub * piece, piece), pl.ds((2 * qq + hh) * cols, cols)],
            dst_ref=m_recv.at[sub, odd * zl + (1 - odd) * 2],
            send_sem=m_send_sem.at[sub, 2 * qq + hh],
            recv_sem=m_recv_sem.at[sub],
            device_id=(q, to_z * plane + spot, hh),
            device_id_type=MESH,
        )

    def own_copy(qq, hh):
        return pltpu.make_async_remote_copy(
            src_ref=cot_hbm.at[:, pl.ds((2 * qq + hh) * cols, cols)],
            dst_ref=m_own,
            send_sem=own_sem.at[0],
            recv_sem=own_sem.at[1],
            device_id=(dp, me, hh),
            device_id_type=MESH,
        )

    def to_other(qq):
        return 2 * ch + qq != dp

    for sub in range(SUB):
        for qq in range(2):
            for hh in range(2):
                @pl.when(to_other(qq))
                def _():
                    cot_copy(sub, qq, hh).start()
    for qq in range(2):
        for hh in range(2):
            @pl.when((2 * ch + qq == dp) & (ch != hh))
            def _():
                own_copy(qq, hh).start()

            @pl.when((2 * ch + qq == dp) & (ch == hh))
            def _():
                pltpu.make_async_copy(
                    cot_hbm.at[:, pl.ds((2 * qq + hh) * cols, cols)], m_own, own_sem.at[1]
                ).start()

    def to_chan(src, dst, send_sem, recv_sem):
        return pltpu.make_async_remote_copy(
            src_ref=src, dst_ref=dst, send_sem=send_sem, recv_sem=recv_sem,
            device_id=(dp, me, other), device_id_type=MESH,
        )

    w_copy = to_chan(
        w_hbm.at[:, pl.ds(pl.multiple_of(other * cols, LANES), cols)], w_recv, w_sem.at[0], w_sem.at[1]
    )
    w_copy.start()

    def a2a_start(k, src, dst, at):
        def body(d, _):
            j = lax.rem(me + d, n)
            pltpu.make_async_remote_copy(
                src_ref=src.at[at(j)],
                dst_ref=dst.at[at(me)],
                send_sem=a2a_send_sem.at[k],
                recv_sem=a2a_recv_sem.at[k],
                device_id=(dp, j, ch),
                device_id_type=MESH,
            ).start()
            return 0

        lax.fori_loop(1, n, body, 0, unroll=9 if n == 64 else 1)
        pltpu.make_async_copy(src.at[at(me)], dst.at[at(me)], a2a_recv_sem.at[k]).start()

    def a2a_wait(k, dst):
        pltpu.make_async_copy(dst, dst, a2a_recv_sem.at[k]).wait()

    def a2a_wait_send(k, src, size):
        part = src.at[pl.ds(0, (n - 1) * size)]
        pltpu.make_async_copy(part, part, a2a_send_sem.at[k]).wait()

    def eight(j):
        return pl.ds(pl.multiple_of(j * 8, 8), 8)

    def block(j):
        return j

    a2a_start(0, sf_send, sf_recv, eight)

    for load in loads[2:]:
        load.wait()
    masked[...] = (cot_ref[...].astype(F32) * live_col).astype(BF)
    up_sel = (up_ref[0].astype(F32) * pick0 + up_ref[1].astype(F32) * pick1).astype(BF)
    down_sel = (down_ref[0].astype(F32) * pick0 + down_ref[1].astype(F32) * pick1).astype(BF)
    max_rank = up_sel.shape[0]
    keep = (lax.broadcasted_iota(jnp.int32, (max_rank, LANES), 0) < rank_ref[0]).astype(F32)
    d_send[...] = dot_t(up_sel, masked[...])
    d_copy = to_chan(d_send, d_recv, d_sem.at[0], d_sem.at[1])
    d_copy.start()
    gate_t[...] = gating_ref[...].astype(F32).T
    skip_t = jnp.broadcast_to(skip_ref[...], (LANES, width)).T

    own_cols = pl.ds(pl.multiple_of(ch * cols, LANES), cols)
    pltpu.make_async_copy(m_own, m_own, own_sem.at[1]).wait()
    w_copy.wait_recv()
    pre0_send[...] = dot_t(m_own[...], w_recv[...]).astype(BF)
    pre0_copy = to_chan(pre0_send, pre0_recv, pre0_sem.at[0], pre0_sem.at[1])
    pre0_copy.start()
    own_part = dot_t(m_own[...], w_ref[:, own_cols])

    pre_copies, ret_copies = [], []

    def project(sub):
        pltpu.make_async_copy(m_recv.at[sub], m_recv.at[sub], m_recv_sem.at[sub]).wait()
        part = m_recv[sub].reshape(3 * piece, cols)
        pre_send[sub] = dot_t(part, w_recv[...]).astype(BF)
        copy = to_chan(pre_send.at[sub], pre_recv.at[sub], pre_send_sem.at[sub], pre_recv_sem.at[sub])
        copy.start()
        pre_copies.append(copy)
        return dot_t(part, w_ref[:, own_cols])

    def give_back(sub, mine):
        pre_copies[sub].wait_recv()
        ret_send[sub] = (mine + pre_recv[sub].astype(F32)).astype(BF)
        near, far = lax.rem(dp + 3 - 2 * zl, 4), lax.rem(dp + 2, 4)
        for slot, (b, z, back) in enumerate(((near, 0, zl), (near, 1, zl), (far, 1 - zl, 2))):
            copy = pltpu.make_async_remote_copy(
                src_ref=ret_send.at[sub, pl.ds(slot * piece, piece)],
                dst_ref=ret_recv.at[back, pl.ds(sub * piece, piece)],
                send_sem=ret_send_sem.at[sub, slot], recv_sem=ret_recv_sem,
                device_id=(b, z * plane + spot, ch), device_id_type=MESH,
            )
            copy.start()
            ret_copies.append(copy)

    tc, ts = tc_ref[...], ts_ref[...]

    def forward(load, store):
        x = jnp.concatenate([load(cc) for cc in range(PER)], axis=1)
        y = dot(t1_ref[...], split_data(x, 0))
        parts = []
        for cc in range(PER):
            re = y[:rows, cc * LANES:(cc + 1) * LANES]
            im = y[rows:, cc * LANES:(cc + 1) * LANES]
            parts.append(jnp.concatenate([re * tc + im * ts, im * tc - re * ts], axis=1))
        store[...] = dot(split_data(jnp.concatenate(parts, axis=0), 1), t2_ref[...])

    def inverse(re, im):
        q = dot(split_data(jnp.concatenate([re, im], axis=1), 1), t2b_ref[...])
        parts = []
        for cc in range(PER):
            qr = q[cc * rows:(cc + 1) * rows, :LANES]
            qi = q[cc * rows:(cc + 1) * rows, LANES:]
            parts.append(jnp.concatenate([qr * tc - qi * ts, qi * tc + qr * ts], axis=0))
        return dot(t1b_ref[...], split_data(jnp.concatenate(parts, axis=1), 0))

    def spread_channels(dst, values):
        for cc in range(PER):
            dst[:, cc, :] = values[:, cc * LANES:(cc + 1) * LANES]

    def gather_channels(src):
        return jnp.concatenate([src[:, cc, :] for cc in range(PER)], axis=0)

    a2a_wait(0, sf_recv)
    forward(lambda cc: sf_recv[pl.ds(cc, n, stride=8), :], spec_s)
    forward(lambda cc: sf_recv[pl.ds(PER + cc, n, stride=8), :], spec_f)
    s_re, s_im = spec_s[:, :LANES], spec_s[:, LANES:]
    f_re, f_im = spec_f[:, :LANES], spec_f[:, LANES:]
    spread_channels(c_send, inverse(s_re * f_re - s_im * f_im, s_re * f_im + s_im * f_re))
    a2a_start(1, c_send, c_recv, block)

    d_copy.wait()
    back_rank = (2.0 * (d_send[...] + d_recv[...]) * keep).astype(BF)

    a2a_wait(1, c_recv)
    inner_t = gather_channels(c_recv) + skip_t * sig_t[...]
    gated_t = (gate_t[...] * inner_t).astype(BF)
    r_send[...] = dot(down_sel, gated_t)
    r_copy = to_chan(r_send, r_recv, r_sem.at[0], r_sem.at[1])
    r_copy.start()
    b_send[:, half:half + width] = dot_t(back_rank, gated_t).astype(BF)

    r_copy.wait()
    fwd_rank = (2.0 * (r_send[...] + r_recv[...]) * keep).astype(BF)
    b_send[:, :half] = dot(fwd_rank, masked[...]).astype(BF)

    def share_copy(p):
        return pltpu.make_async_remote_copy(
            src_ref=b_send.at[:, pl.ds(pl.multiple_of(p * LANES, LANES), LANES)],
            dst_ref=b_recv.at[pl.ds(pl.multiple_of(me * 16, 16), 16), :],
            send_sem=b_sem.at[0], recv_sem=b_sem.at[1], device_id=(dp, p, ch), device_id_type=MESH,
        )

    def share(d, _):
        p = lax.rem(me + d, n_own)

        @pl.when(p != me)
        def _():
            share_copy(p).start()

        @pl.when(p == me)
        def _():
            pltpu.make_async_copy(
                b_send.at[:, pl.ds(pl.multiple_of(p * LANES, LANES), LANES)],
                b_recv.at[pl.ds(pl.multiple_of(me * 16, 16), 16), :],
                b_sem.at[1],
            ).start()
        return 0

    lax.fori_loop(0, n_own, share, 0)

    mine = project(0)
    for sub in range(1, SUB):
        after = project(sub)
        give_back(sub - 1, mine)
        mine = after
    give_back(SUB - 1, mine)

    is_owner = me < n_own

    def q_copy(step):
        return pltpu.make_async_remote_copy(
            src_ref=q_send, dst_ref=q_recv.at[step - 1], send_sem=q_send_sem.at[step],
            recv_sem=q_recv_sem, device_id=(lax.rem(dp + step, 4), me, ch), device_id_type=MESH,
        )

    @pl.when(is_owner)
    def _():
        pltpu.make_async_copy(b_recv, b_recv, b_sem.at[1]).wait()
        acc = b_recv[0:16, :].astype(F32)
        for i in range(1, n):
            acc = acc + b_recv[16 * i:16 * (i + 1), :].astype(F32)
        q_send[...] = jnp.concatenate([acc * pick0, acc * pick1], axis=0)
        for step in (1, 3, 2):
            q_copy(step).start()

    grad_y = own_part + received(pre0_copy, pre0_recv)
    pltpu.make_async_copy(ret_recv, ret_recv, ret_recv_sem).wait()
    for k in range(3):
        grad_y = grad_y + ret_recv[k].astype(F32)
    grad_y = grad_y.T * live_row + dot_0(down_sel, back_rank)
    grad_u = grad_y * gate_t[...]
    gradu_t[...] = grad_u
    for cc in range(PER):
        u_send[:, cc, :] = gradu_t[cc * n:(cc + 1) * n, :]
    a2a_start(2, u_send, u_recv, block)
    ggat_ref[...] = (grad_y * inner_t).T.astype(BF)
    outs = [
        pltpu.make_async_copy(s, d, out_sem.at[i])
        for i, (s, d) in enumerate((
            (ggat_ref, ggat_hbm), (gsig_ref, gsig_hbm), (gfilt_ref, gfilt_hbm), (g_recv, gbank_hbm),
            (gskip_ref, gskip_hbm),
        ))
    ]
    outs[0].start()

    g_size = 2 * max_rank

    @pl.when(is_owner)
    def _():
        pltpu.make_async_copy(q_recv, q_recv, q_recv_sem).wait()
        g_send[...] = (q_send[...] + q_recv[0] + q_recv[1] + q_recv[2]).astype(BF)
        at = pl.ds(pl.multiple_of(me * g_size, g_size), g_size)

        def spread(d, _):
            pltpu.make_async_remote_copy(
                src_ref=g_send, dst_ref=g_recv.at[at, :], send_sem=g_sem.at[0], recv_sem=g_sem.at[1],
                device_id=(dp, lax.rem(me + d, n), ch), device_id_type=MESH,
            ).start()
            return 0

        lax.fori_loop(1, n, spread, 0, unroll=9 if n == 64 else 1)
        pltpu.make_async_copy(g_send, g_recv.at[at, :], g_sem.at[1]).start()

    a2a_wait(2, u_recv)
    forward(lambda cc: u_recv[:, cc, :], spec_g)
    g_re, g_im = spec_g[:, :LANES], spec_g[:, LANES:]
    s_re, s_im = spec_s[:, :LANES], spec_s[:, LANES:]
    spread_channels(ks_send, inverse(g_re * s_re + g_im * s_im, g_im * s_re - g_re * s_im))
    a2a_start(3, ks_send, ks_recv, block)
    f_re, f_im = spec_f[:, :LANES], spec_f[:, LANES:]
    spread_channels(kf_send, inverse(g_re * f_re + g_im * f_im, g_im * f_re - g_re * f_im))
    for cc in range(PER):
        value = jnp.sum(u_recv[:, cc, :] * sf_recv[pl.ds(cc, n, stride=8), :], axis=(0, 1), keepdims=True)
        kf_send[:, PER + cc, :] = jnp.broadcast_to(value, (n, LANES))
    a2a_start(4, kf_send, kf_recv, block)

    def to_peers(src, dst, send_sem, recv_sem):
        copies = []
        for step in (1, 3, 2):
            copy = pltpu.make_async_remote_copy(
                src_ref=src, dst_ref=dst.at[step - 1], send_sem=send_sem.at[step], recv_sem=recv_sem,
                device_id=(lax.rem(dp + step, 4), me, ch), device_id_type=MESH,
            )
            copy.start()
            copies.append(copy)
        return copies

    a2a_wait(3, ks_recv)
    corr_st = gather_channels(ks_recv)
    f_send[...] = corr_st.astype(BF)
    f_copies = to_peers(f_send, f_recv, f_send_sem, f_recv_sem)

    a2a_wait(4, kf_recv)
    skips = jnp.concatenate([kf_recv[:, PER + cc, :] for cc in range(PER)], axis=0)
    e_send[...] = skips.T[:8]
    e_copies = to_peers(e_send, e_recv, e_send_sem, e_recv_sem)
    gsig_ref[...] = (gather_channels(kf_recv) + skip_t * gradu_t[...]).T.astype(BF)
    outs[1].start()

    pltpu.make_async_copy(g_recv, g_recv, g_sem.at[1]).wait()
    outs[3].start()

    pltpu.make_async_copy(f_recv, f_recv, f_recv_sem).wait()
    sums = corr_st
    for k in range(3):
        sums = sums + f_recv[k].astype(F32)
    gfilt_ref[...] = sums.T
    outs[2].start()

    pltpu.make_async_copy(e_recv, e_recv, e_recv_sem).wait()
    gskip_ref[...] = e_send[...] + e_recv[0] + e_recv[1] + e_recv[2]
    outs[4].start()

    for sub in range(SUB):
        for qq in range(2):
            for hh in range(2):
                @pl.when(to_other(qq))
                def _():
                    cot_copy(sub, qq, hh).wait_send()
    for qq in range(2):
        for hh in range(2):
            @pl.when((2 * ch + qq == dp) & (ch != hh))
            def _():
                own_copy(qq, hh).wait_send()
    a2a_wait_send(0, sf_send, 8)
    for k, src in ((1, c_send), (2, u_send), (3, ks_send), (4, kf_send)):
        a2a_wait_send(k, src, 1)
    w_copy.wait_send()
    pre0_copy.wait_send()
    for copy in pre_copies + ret_copies + f_copies + e_copies:
        copy.wait_send()

    def b_sent(count):
        part = b_send.at[:, pl.ds(0, count * LANES)]
        pltpu.make_async_copy(part, part, b_sem.at[0]).wait()

    @pl.when(me < n_own)
    def _():
        b_sent(n_own - 1)
        for step in (1, 3, 2):
            q_copy(step).wait_send()

        def sent(d, _):
            pltpu.make_async_copy(g_send, g_send, g_sem.at[0]).wait()
            return 0

        lax.fori_loop(1, n, sent, 0)

    @pl.when(me >= n_own)
    def _():
        b_sent(n_own)

    for out in outs:
        out.wait()


def received(copy, ref):
    copy.wait_recv()
    return ref[...].astype(F32)


def finish_kernel(
    gsig_in, ggat_in, gfilt_in, gbank_in, gskip_in,
    gsig_out, ggat_out, gfilt_out, gskip_out, ga_out, gb_out,
    gsig_ref, ggat_ref, gfilt_ref, gbank_ref, gskip_ref, ga_ref, gb_ref, in_sem, out_sem,
):
    max_rank, half = gb_ref.shape[1:]
    width = ga_ref.shape[2]
    g_size = 2 * max_rank
    up_chunks = half // LANES
    a_chunks = -(-width // LANES)
    pairs = (
        (gbank_in, gbank_ref), (gfilt_in, gfilt_ref), (gsig_in, gsig_ref), (ggat_in, ggat_ref),
        (gskip_in.at[pl.ds(0, 1)], gskip_ref),
    )
    loads = [pltpu.make_async_copy(s, d, in_sem.at[i]) for i, (s, d) in enumerate(pairs)]
    for load in loads:
        load.start()
    pairs = (
        (gb_ref, gb_out), (gfilt_ref, gfilt_out), (gsig_ref, gsig_out), (ggat_ref, ggat_out),
        (gskip_ref, gskip_out), (ga_ref, ga_out),
    )
    stores = [pltpu.make_async_copy(s, d, out_sem.at[i]) for i, (s, d) in enumerate(pairs)]
    loads[0].wait()

    def place(p, _):
        block = gbank_ref[pl.ds(pl.multiple_of(p * g_size, g_size), g_size), :].astype(F32)
        where = pl.ds(pl.multiple_of(p * LANES, LANES), LANES)
        gb_ref[0, :, where] = block[:max_rank]
        gb_ref[1, :, where] = block[max_rank:]
        return 0

    lax.fori_loop(0, up_chunks, place, 0, unroll=4)
    stores[0].start()
    for k in range(1, 5):
        loads[k].wait()
        stores[k].start()
    size = min(LANES, width)
    for k in range(a_chunks):
        at = (up_chunks + k) * g_size
        block = gbank_ref[at:at + g_size, :].astype(F32)
        ga_ref[0, :, k * size:(k + 1) * size] = block[:max_rank, :size]
        ga_ref[1, :, k * size:(k + 1) * size] = block[max_rank:, :size]
    stores[5].start()
    for store in stores:
        store.wait()


def local(
    signal, gating, cotangent, filt, skip, output_projection,
    adapter_down_bank, adapter_up_bank, adapter_index, sequence_rank, real_length,
):
    n = lax.axis_size("seq")
    width = signal.shape[2]
    half = cotangent.shape[2]
    cols = output_projection.shape[1] // 2
    max_rank = adapter_up_bank.shape[1]
    a_chunks = -(-width // LANES)
    n_own = half // LANES + a_chunks
    piece = LANES // SUB
    consts = [jnp.asarray(t) for t in tables(n)]
    rows = consts[4].shape[0]
    vmem = pl.BlockSpec(memory_space=pltpu.VMEM)
    smem = pl.BlockSpec(memory_space=pltpu.SMEM)
    hbm = pl.BlockSpec(memory_space=pltpu.HBM)
    dma = pltpu.SemaphoreType.DMA
    arrays = [
        signal[0], gating[0], cotangent[0], filt, skip[None], output_projection,
        jnp.swapaxes(adapter_down_bank, 1, 2), adapter_up_bank, *consts,
    ]
    block = pltpu.VMEM((n, PER, LANES), F32)
    eight = pltpu.VMEM((8 * n, LANES), F32)
    two = pltpu.VMEM((n, 2 * PER, LANES), F32)
    wide = pltpu.VMEM((width, LANES), F32)
    spec = pltpu.VMEM((PER * rows, 2 * LANES), F32)
    rank = pltpu.VMEM((max_rank, LANES), F32)
    outs = pl.pallas_call(
        functools.partial(kernel, n),
        out_shape=(
            jax.ShapeDtypeStruct((LANES, width), BF),
            jax.ShapeDtypeStruct((LANES, width), BF),
            jax.ShapeDtypeStruct((LANES, width), F32),
            jax.ShapeDtypeStruct((2 * max_rank * n_own, LANES), BF),
            jax.ShapeDtypeStruct((8, width), F32),
        ),
        in_specs=[smem] * 3 + [hbm] * len(arrays),
        out_specs=(hbm,) * 5,
        scratch_shapes=[
            pltpu.VMEM((LANES, width), BF),
            pltpu.VMEM((LANES, width), BF),
            pltpu.VMEM((LANES, width), F32),
            pltpu.VMEM((8, width), F32),
        ] + [pltpu.VMEM(a.shape, a.dtype) for a in arrays] + [
            pltpu.VMEM((LANES, half), BF),
            wide, wide, wide, spec, spec, spec,
            eight, eight, block, block, block, block, block, block, two, two,
            pltpu.VMEM((LANES, cols), BF),
            pltpu.VMEM((SUB, 3, piece, cols), BF),
            pltpu.VMEM((width, cols), BF),
            pltpu.VMEM((LANES, width), BF),
            pltpu.VMEM((LANES, width), BF),
            pltpu.VMEM((SUB, 3 * piece, width), BF),
            pltpu.VMEM((SUB, 3 * piece, width), BF),
            pltpu.VMEM((SUB, 3 * piece, width), BF),
            pltpu.VMEM((3, LANES, width), BF),
            rank, rank, rank, rank,
            pltpu.VMEM((max_rank, n_own * LANES), BF),
            pltpu.VMEM((16 * n, LANES), BF),
            pltpu.VMEM((2 * max_rank, LANES), F32),
            pltpu.VMEM((3, 2 * max_rank, LANES), F32),
            pltpu.VMEM((2 * max_rank, LANES), BF),
            pltpu.VMEM((2 * max_rank * n_own, LANES), BF),
            pltpu.VMEM((width, LANES), BF),
            pltpu.VMEM((3, width, LANES), BF),
            pltpu.VMEM((8, width), F32),
            pltpu.VMEM((3, 8, width), F32),
            dma((len(arrays),)), dma((5,)), dma((5,)), dma((5,)), dma((SUB, 4)), dma((SUB,)), dma((2,)), dma((2,)),
            dma((2,)), dma((SUB,)), dma((SUB,)), dma((SUB, 4)), dma, dma((2,)), dma((2,)), dma((2,)),
            dma((4,)), dma, dma((2,)), dma((4,)), dma, dma((4,)), dma,
        ],
        compiler_params=pltpu.CompilerParams(
            collective_id=0, has_side_effects=True, vmem_limit_bytes=VMEM_LIMIT
        ),
    )(adapter_index, sequence_rank, real_length, *arrays)
    grad_signal, grad_gating, grad_filt, grad_skip, grad_a, grad_b = pl.pallas_call(
        finish_kernel,
        out_shape=(
            jax.ShapeDtypeStruct((LANES, width), BF),
            jax.ShapeDtypeStruct((LANES, width), BF),
            jax.ShapeDtypeStruct((LANES, width), F32),
            jax.ShapeDtypeStruct((1, width), F32),
            jax.ShapeDtypeStruct((2, max_rank, width), F32),
            jax.ShapeDtypeStruct((2, max_rank, half), F32),
        ),
        in_specs=[hbm] * 5,
        out_specs=(hbm,) * 6,
        scratch_shapes=[
            pltpu.VMEM((LANES, width), BF), pltpu.VMEM((LANES, width), BF), pltpu.VMEM((LANES, width), F32),
            pltpu.VMEM((2 * max_rank * n_own, LANES), BF), pltpu.VMEM((1, width), F32),
            pltpu.VMEM((2, max_rank, width), F32), pltpu.VMEM((2, max_rank, half), F32),
            dma((5,)), dma((6,)),
        ],
        compiler_params=pltpu.CompilerParams(vmem_limit_bytes=VMEM_LIMIT),
    )(*outs)
    return (grad_signal[None], grad_gating[None], grad_filt, grad_skip[0], jnp.swapaxes(grad_a, 1, 2), grad_b)


def solution(mesh):
    placed = (
        P("dp", "seq", "chan"), P("dp", "seq", "chan"), P("dp", "seq", "chan"), P("seq", "chan"),
        P("chan"), P("chan", "dp"), P(None, "chan", None), P(None, None, "chan"),
        P("dp"), P("dp"), P("dp"),
    )
    return jax.shard_map(
        local,
        mesh=mesh,
        in_specs=placed,
        out_specs=(
            P("dp", "seq", "chan"), P("dp", "seq", "chan"), P("seq", "chan"), P("chan"),
            P(None, "chan", None), P(None, None, "chan"),
        ),
        check_vma=False,
    )
```

```python
import functools
import math

import jax
import jax.numpy as jnp
import ml_dtypes
import numpy as np
from jax import lax
from jax.experimental import pallas as pl
from jax.experimental.pallas import tpu as pltpu
from jax.sharding import PartitionSpec as P

MESH = pl.DeviceIdType.MESH
BF = jnp.bfloat16
F32 = jnp.float32
LANES = 128
PER = 4
VMEM_LIMIT = 62 * 1024 * 1024
SUB = 2


def split3(table, axis, order):
    high = table.astype(ml_dtypes.bfloat16)
    low = (table - high.astype(np.float64)).astype(ml_dtypes.bfloat16)
    return np.concatenate([high if o else low for o in order], axis=axis)


def tables(n):
    rows = -(-(n + 1) // 8) * 8
    k1 = np.arange(rows)
    used = (k1 <= n).astype(np.float64)
    i = np.arange(n)
    a = np.arange(LANES)
    period = 2 * n * LANES
    th1 = 2 * math.pi * (k1[:, None] * i[None, :] % (2 * n)) / (2 * n)
    first = np.concatenate([np.cos(th1) * used[:, None], -np.sin(th1) * used[:, None]], 0)
    thw = 2 * math.pi * (k1[:, None] * a[None, :] % period) / period
    tw_cos, tw_sin = np.cos(thw), np.sin(thw)
    th2 = 2 * math.pi * (a[:, None] * a[None, :] % LANES) / LANES
    c2, s2 = np.cos(th2), np.sin(th2)
    second = np.block([[c2, -s2], [s2, c2]])
    second_back = np.block([[c2, s2], [-s2, c2]])
    weight = used * np.where((k1 == 0) | (k1 == n), 1.0, 2.0) / period
    last = np.concatenate([np.cos(th1).T * weight, -np.sin(th1).T * weight], 1)
    return (
        split3(first, 1, (1, 1, 0)),
        split3(second, 0, (1, 1, 0)),
        split3(second_back, 0, (1, 1, 0)),
        split3(last, 1, (1, 1, 0)),
        tw_cos.astype(np.float32),
        tw_sin.astype(np.float32),
    )


def split_data(x, axis):
    high = x.astype(BF)
    low = (x - high.astype(F32)).astype(BF)
    return jnp.concatenate([high, low, high], axis=axis)


def dot(a, b):
    return jnp.dot(a, b, preferred_element_type=F32)


def dot_t(a, b):
    return lax.dot_general(a, b, (((1,), (1,)), ((), ())), preferred_element_type=F32)


def dot_0(a, b):
    return lax.dot_general(a, b, (((0,), (0,)), ((), ())), preferred_element_type=F32)


def kernel(
    n,
    index_ref, rank_ref, length_ref,
    signal_hbm, gating_hbm, cot_hbm, filt_hbm, skip_hbm, w_hbm, down_hbm, up_hbm,
    t1_hbm, t2_hbm, t2b_hbm, t1b_hbm, tc_hbm, ts_hbm,
    gsig_hbm, ggat_hbm, gfilt_hbm, gbank_hbm, gskip_hbm,
    gsig_ref, ggat_ref, gfilt_ref, gskip_ref,
    signal_ref, gating_ref, cot_ref, filt_ref, skip_ref, w_ref, down_ref, up_ref,
    t1_ref, t2_ref, t2b_ref, t1b_ref, tc_ref, ts_ref,
    masked, sig_t, gate_t, gradu_t, spec_s, spec_f, spec_g,
    sf_send, sf_recv, c_send, c_recv, u_send, u_recv, ks_send, ks_recv, kf_send, kf_recv,
    m_own, m_recv, m_far, w_far, far_send, far_recv, w_recv, pre0_send, pre0_recv, pre_send, pre_recv, ret_send, ret_recv,
    d_send, d_recv, r_send, r_recv,
    b_send, b_recv, q_send, q_recv, g_send, g_recv, f_send, f_recv, corr_st, h_send, h_recv, e_send, e_recv,
    in_sem, out_sem, a2a_send_sem, a2a_recv_sem, m_send_sem, m_recv_sem, own_sem, w_sem, pre0_sem,
    pre_send_sem, pre_recv_sem, ret_send_sem, ret_recv_sem, d_sem, r_sem, b_sem,
    q_send_sem, q_recv_sem, g_sem, f_send_sem, f_recv_sem, e_send_sem, e_recv_sem,
    h_send_sem, h_recv_sem, far_sem, wf_sem, wy_send_sem, wy_recv_sem, fr_send_sem, fr_recv_sem,
):
    dp = lax.axis_index("dp")
    me = lax.axis_index("seq")
    ch = lax.axis_index("chan")
    other = 1 - ch
    plane = n // 2
    zl, spot = lax.div(me, plane), lax.rem(me, plane)
    group = m_far.shape[0]
    nx = group // 2
    ny = plane // nx
    y, x = lax.div(spot, nx), lax.rem(spot, nx)
    g = zl * nx + x
    far_cols = m_far.shape[2]

    def member(k):
        return lax.div(k, nx) * plane + y * nx + lax.rem(k, nx)

    width = w_ref.shape[0]
    cols = w_ref.shape[1] // 2
    half = cot_ref.shape[1]
    piece = LANES // SUB
    n_own = b_send.shape[1] // LANES
    rows = t1_ref.shape[0] // 2
    a_chunks = -(-width // LANES)

    barrier = pltpu.get_barrier_semaphore()
    for d in range(4):
        for z in range(2):
            for c in range(2):
                if d or c:
                    pl.semaphore_signal(
                        barrier, inc=1,
                        device_id=(lax.rem(dp + d, 4), lax.rem(zl + z, 2) * plane + spot, lax.rem(ch + c, 2)),
                        device_id_type=MESH,
                    )

    def greet(d, _):
        pl.semaphore_signal(
            barrier, inc=1, device_id=(dp, lax.rem(me + d, n), ch), device_id_type=MESH
        )
        return 0

    lax.fori_loop(1, n, greet, 0, unroll=9 if n == 64 else 1)
    for z in range(2):
        for k in range(1, nx):
            pl.semaphore_signal(
                barrier, inc=1, device_id=(dp, member(z * nx + lax.rem(x + k, nx)), other),
                device_id_type=MESH,
            )

    pairs = (
        (signal_hbm, signal_ref), (filt_hbm, filt_ref), (cot_hbm, cot_ref), (up_hbm, up_ref),
        (w_hbm, w_ref), (t1_hbm, t1_ref), (t2_hbm, t2_ref), (t2b_hbm, t2b_ref), (t1b_hbm, t1b_ref),
        (tc_hbm, tc_ref), (ts_hbm, ts_ref), (gating_hbm, gating_ref), (down_hbm, down_ref),
        (skip_hbm, skip_ref),
    )
    loads = [pltpu.make_async_copy(s, d, in_sem.at[i]) for i, (s, d) in enumerate(pairs)]
    for load in loads:
        load.start()

    loads[0].wait()
    loads[1].wait()
    sig_t[...] = signal_ref[...].astype(F32).T
    filt_t = filt_ref[...].T
    for cc in range(PER):
        sf_send[pl.ds(cc, n, stride=8), :] = sig_t[cc * n:(cc + 1) * n, :]
        sf_send[pl.ds(PER + cc, n, stride=8), :] = filt_t[cc * n:(cc + 1) * n, :]
    real_length = length_ref[0]
    live_col = (me * LANES + lax.broadcasted_iota(jnp.int32, (LANES, 1), 0) < real_length).astype(F32)
    live_row = (me * LANES + lax.broadcasted_iota(jnp.int32, (1, LANES), 1) < real_length).astype(F32)
    pick1 = index_ref[0].astype(F32)
    pick0 = 1.0 - pick1

    pl.semaphore_wait(barrier, n - 1 + 14 + 2 * (nx - 1))

    def cot_copy(sub, qq, hh):
        q = 2 * ch + qq
        return pltpu.make_async_remote_copy(
            src_ref=cot_hbm.at[pl.ds(sub * piece, piece), pl.ds((2 * qq + hh) * cols, cols)],
            dst_ref=m_recv.at[sub, zl],
            send_sem=m_send_sem.at[sub, 2 * qq + hh],
            recv_sem=m_recv_sem.at[sub],
            device_id=(q, lax.div(lax.rem(q - dp + 4, 4), 3) * plane + spot, hh),
            device_id_type=MESH,
        )

    def own_copy(qq, hh):
        return pltpu.make_async_remote_copy(
            src_ref=cot_hbm.at[:, pl.ds((2 * qq + hh) * cols, cols)],
            dst_ref=m_own,
            send_sem=own_sem.at[0],
            recv_sem=own_sem.at[1],
            device_id=(dp, me, hh),
            device_id_type=MESH,
        )

    def to_other(qq):
        return lax.rem(2 * ch + qq - dp + 4, 2) == 1

    for sub in range(SUB):
        for qq in range(2):
            for hh in range(2):
                @pl.when(to_other(qq))
                def _():
                    cot_copy(sub, qq, hh).start()
    for qq in range(2):
        for hh in range(2):
            @pl.when((2 * ch + qq == dp) & (ch != hh))
            def _():
                own_copy(qq, hh).start()

            @pl.when((2 * ch + qq == dp) & (ch == hh))
            def _():
                pltpu.make_async_copy(
                    cot_hbm.at[:, pl.ds((2 * qq + hh) * cols, cols)], m_own, own_sem.at[1]
                ).start()

    far = lax.rem(dp + 2, 4)
    slice_rows = width // ny
    my_slice = pl.ds(pl.multiple_of(y * slice_rows, slice_rows), slice_rows)

    wf_copy = pltpu.make_async_remote_copy(
        src_ref=w_hbm.at[my_slice, pl.ds(pl.multiple_of(g * far_cols, far_cols), far_cols)],
        dst_ref=w_far.at[my_slice, :],
        send_sem=wf_sem.at[0], recv_sem=wf_sem.at[1], device_id=(far, me, ch), device_id_type=MESH,
    )
    wf_copy.start()

    def far_copy(d, c):
        k = lax.rem(g + d, group)
        at = lax.rem(far, 2) * 2 * cols + k * far_cols
        src = cot_hbm.at[:, pl.ds(pl.multiple_of(at, far_cols), far_cols)]
        if d == 0 and c == 0:
            return pltpu.make_async_copy(src, m_far.at[d], far_sem.at[1])
        return pltpu.make_async_remote_copy(
            src_ref=src, dst_ref=m_far.at[d], send_sem=far_sem.at[0], recv_sem=far_sem.at[1],
            device_id=(dp, member(k), lax.rem(ch + c, 2)), device_id_type=MESH,
        )

    holds_far = ch == lax.div(far, 2)

    @pl.when(holds_far)
    def _():
        for d in range(group):
            for c in range(2):
                far_copy(d, c).start()

    def to_chan(src, dst, send_sem, recv_sem):
        return pltpu.make_async_remote_copy(
            src_ref=src, dst_ref=dst, send_sem=send_sem, recv_sem=recv_sem,
            device_id=(dp, me, other), device_id_type=MESH,
        )

    w_copy = to_chan(
        w_hbm.at[:, pl.ds(pl.multiple_of(other * cols, LANES), cols)], w_recv, w_sem.at[0], w_sem.at[1]
    )
    w_copy.start()

    def a2a_start(k, src, dst, at):
        def body(d, _):
            j = lax.rem(me + d, n)
            pltpu.make_async_remote_copy(
                src_ref=src.at[at(j)],
                dst_ref=dst.at[at(me)],
                send_sem=a2a_send_sem.at[k],
                recv_sem=a2a_recv_sem.at[k],
                device_id=(dp, j, ch),
                device_id_type=MESH,
            ).start()
            return 0

        lax.fori_loop(1, n, body, 0, unroll=9 if n == 64 else 1)
        pltpu.make_async_copy(src.at[at(me)], dst.at[at(me)], a2a_recv_sem.at[k]).start()

    def a2a_wait(k, dst):
        pltpu.make_async_copy(dst, dst, a2a_recv_sem.at[k]).wait()

    def a2a_wait_send(k, src, size):
        part = src.at[pl.ds(0, (n - 1) * size)]
        pltpu.make_async_copy(part, part, a2a_send_sem.at[k]).wait()

    def eight(j):
        return pl.ds(pl.multiple_of(j * 8, 8), 8)

    def block(j):
        return j

    a2a_start(0, sf_send, sf_recv, eight)

    wf_copy.wait_recv()
    wy_copies = []
    for k in range(1, ny):
        copy = pltpu.make_async_remote_copy(
            src_ref=w_far.at[my_slice, :], dst_ref=w_far.at[my_slice, :],
            send_sem=wy_send_sem.at[k], recv_sem=wy_recv_sem,
            device_id=(dp, zl * plane + lax.rem(y + k, ny) * nx + x, ch), device_id_type=MESH,
        )
        copy.start()
        wy_copies.append(copy)

    for load in loads[2:]:
        load.wait()
    masked[...] = (cot_ref[...].astype(F32) * live_col).astype(BF)
    up_sel = (up_ref[0].astype(F32) * pick0 + up_ref[1].astype(F32) * pick1).astype(BF)
    down_sel = (down_ref[0].astype(F32) * pick0 + down_ref[1].astype(F32) * pick1).astype(BF)
    max_rank = up_sel.shape[0]
    keep = (lax.broadcasted_iota(jnp.int32, (max_rank, LANES), 0) < rank_ref[0]).astype(F32)
    d_send[...] = dot_t(up_sel, masked[...])
    d_copy = to_chan(d_send, d_recv, d_sem.at[0], d_sem.at[1])
    d_copy.start()
    gate_t[...] = gating_ref[...].astype(F32).T
    skip_t = jnp.broadcast_to(skip_ref[...], (LANES, width)).T

    own_cols = pl.ds(pl.multiple_of(ch * cols, LANES), cols)
    pltpu.make_async_copy(m_own, m_own, own_sem.at[1]).wait()
    w_copy.wait_recv()
    pre0_send[...] = dot_t(m_own[...], w_recv[...]).astype(BF)
    pre0_copy = to_chan(pre0_send, pre0_recv, pre0_sem.at[0], pre0_sem.at[1])
    pre0_copy.start()
    own_part = dot_t(m_own[...], w_ref[:, own_cols])

    pre_copies, ret_copies = [], []

    def project(sub):
        pltpu.make_async_copy(m_recv.at[sub], m_recv.at[sub], m_recv_sem.at[sub]).wait()
        part = m_recv[sub].reshape(2 * piece, cols)
        pre_send[sub] = dot_t(part, w_recv[...]).astype(BF)
        copy = to_chan(pre_send.at[sub], pre_recv.at[sub], pre_send_sem.at[sub], pre_recv_sem.at[sub])
        copy.start()
        pre_copies.append(copy)
        return dot_t(part, w_ref[:, own_cols])

    def give_back(sub, mine):
        pre_copies[sub].wait_recv()
        ret_send[sub] = (mine + pre_recv[sub].astype(F32)).astype(BF)
        for slot in range(2):
            copy = pltpu.make_async_remote_copy(
                src_ref=ret_send.at[sub, pl.ds(slot * piece, piece)],
                dst_ref=ret_recv.at[zl, pl.ds(sub * piece, piece)],
                send_sem=ret_send_sem.at[sub, slot], recv_sem=ret_recv_sem,
                device_id=(lax.rem(dp + 3 - 2 * zl, 4), slot * plane + spot, ch), device_id_type=MESH,
            )
            copy.start()
            ret_copies.append(copy)

    tc, ts = tc_ref[...], ts_ref[...]

    def forward(load, store):
        x = jnp.concatenate([load(cc) for cc in range(PER)], axis=1)
        y = dot(t1_ref[...], split_data(x, 0))
        parts = []
        for cc in range(PER):
            re = y[:rows, cc * LANES:(cc + 1) * LANES]
            im = y[rows:, cc * LANES:(cc + 1) * LANES]
            parts.append(jnp.concatenate([re * tc + im * ts, im * tc - re * ts], axis=1))
        store[...] = dot(split_data(jnp.concatenate(parts, axis=0), 1), t2_ref[...])

    def inverse(re, im):
        q = dot(split_data(jnp.concatenate([re, im], axis=1), 1), t2b_ref[...])
        parts = []
        for cc in range(PER):
            qr = q[cc * rows:(cc + 1) * rows, :LANES]
            qi = q[cc * rows:(cc + 1) * rows, LANES:]
            parts.append(jnp.concatenate([qr * tc - qi * ts, qi * tc + qr * ts], axis=0))
        return dot(t1b_ref[...], split_data(jnp.concatenate(parts, axis=1), 0))

    def spread_channels(dst, values):
        for cc in range(PER):
            dst[:, cc, :] = values[:, cc * LANES:(cc + 1) * LANES]

    def gather_channels(src):
        return jnp.concatenate([src[:, cc, :] for cc in range(PER)], axis=0)

    a2a_wait(0, sf_recv)
    forward(lambda cc: sf_recv[pl.ds(cc, n, stride=8), :], spec_s)
    forward(lambda cc: sf_recv[pl.ds(PER + cc, n, stride=8), :], spec_f)
    s_re, s_im = spec_s[:, :LANES], spec_s[:, LANES:]
    f_re, f_im = spec_f[:, :LANES], spec_f[:, LANES:]
    spread_channels(c_send, inverse(s_re * f_re - s_im * f_im, s_re * f_im + s_im * f_re))
    a2a_start(1, c_send, c_recv, block)

    d_copy.wait()
    back_rank = (2.0 * (d_send[...] + d_recv[...]) * keep).astype(BF)

    pltpu.make_async_copy(m_far, m_far, far_sem.at[1]).wait()
    if ny > 1:
        rest = w_far.at[pl.ds(0, (ny - 1) * slice_rows), :]
        pltpu.make_async_copy(rest, rest, wy_recv_sem).wait()
    far_part = dot_t(m_far[...].reshape(group * LANES, far_cols), w_far[...])
    far_send[...] = far_part[LANES:].astype(BF)
    own_part = own_part + far_part[:LANES]
    far_copies = []
    for d in range(1, group):
        copy = pltpu.make_async_remote_copy(
            src_ref=far_send.at[pl.ds((d - 1) * LANES, LANES), :], dst_ref=far_recv.at[d - 1],
            send_sem=fr_send_sem.at[d], recv_sem=fr_recv_sem,
            device_id=(dp, member(lax.rem(g + group - d, group)), ch), device_id_type=MESH,
        )
        copy.start()
        far_copies.append(copy)

    mine = project(0)
    for sub in range(1, SUB):
        after = project(sub)
        give_back(sub - 1, mine)
        mine = after
    give_back(SUB - 1, mine)

    a2a_wait(1, c_recv)
    inner_t = gather_channels(c_recv) + skip_t * sig_t[...]
    gated_t = (gate_t[...] * inner_t).astype(BF)
    r_send[...] = dot(down_sel, gated_t)
    r_copy = to_chan(r_send, r_recv, r_sem.at[0], r_sem.at[1])
    r_copy.start()
    b_send[:, half:half + width] = dot_t(back_rank, gated_t).astype(BF)

    grad_y = own_part + received(pre0_copy, pre0_recv)
    pltpu.make_async_copy(ret_recv, ret_recv, ret_recv_sem).wait()
    pltpu.make_async_copy(far_recv, far_recv, fr_recv_sem).wait()
    for k in range(2):
        grad_y = grad_y + ret_recv[k].astype(F32)
    for k in range(group - 1):
        grad_y = grad_y + far_recv[k].astype(F32)
    grad_y = grad_y.T * live_row + dot_0(down_sel, back_rank)
    grad_u = grad_y * gate_t[...]
    gradu_t[...] = grad_u
    for cc in range(PER):
        u_send[:, cc, :] = gradu_t[cc * n:(cc + 1) * n, :]
    a2a_start(2, u_send, u_recv, block)
    r_copy.wait()
    fwd_rank = (2.0 * (r_send[...] + r_recv[...]) * keep).astype(BF)
    b_send[:, :half] = dot(fwd_rank, masked[...]).astype(BF)

    def share_copy(p):
        return pltpu.make_async_remote_copy(
            src_ref=b_send.at[:, pl.ds(pl.multiple_of(p * LANES, LANES), LANES)],
            dst_ref=b_recv.at[pl.ds(pl.multiple_of(me * 16, 16), 16), :],
            send_sem=b_sem.at[0], recv_sem=b_sem.at[1], device_id=(dp, p, ch), device_id_type=MESH,
        )

    def share(d, _):
        p = lax.rem(me + d, n_own)

        @pl.when(p != me)
        def _():
            share_copy(p).start()

        @pl.when(p == me)
        def _():
            pltpu.make_async_copy(
                b_send.at[:, pl.ds(pl.multiple_of(p * LANES, LANES), LANES)],
                b_recv.at[pl.ds(pl.multiple_of(me * 16, 16), 16), :],
                b_sem.at[1],
            ).start()
        return 0

    lax.fori_loop(0, n_own, share, 0)

    ggat_ref[...] = (grad_y * inner_t).T.astype(BF)
    outs = [
        pltpu.make_async_copy(s, d, out_sem.at[i])
        for i, (s, d) in enumerate((
            (ggat_ref, ggat_hbm), (gsig_ref, gsig_hbm), (gfilt_ref, gfilt_hbm), (g_recv, gbank_hbm),
            (gskip_ref, gskip_hbm),
        ))
    ]
    outs[0].start()

    is_owner = me < n_own

    def q_copy(step):
        return pltpu.make_async_remote_copy(
            src_ref=q_send, dst_ref=q_recv.at[step - 1], send_sem=q_send_sem.at[step],
            recv_sem=q_recv_sem, device_id=(lax.rem(dp + step, 4), me, ch), device_id_type=MESH,
        )

    @pl.when(is_owner)
    def _():
        pltpu.make_async_copy(b_recv, b_recv, b_sem.at[1]).wait()
        acc = b_recv[0:16, :].astype(F32)
        for i in range(1, n):
            acc = acc + b_recv[16 * i:16 * (i + 1), :].astype(F32)
        q_send[...] = jnp.concatenate([acc * pick0, acc * pick1], axis=0)
        for step in (1, 3, 2):
            q_copy(step).start()

    a2a_wait(2, u_recv)
    forward(lambda cc: u_recv[:, cc, :], spec_g)
    g_re, g_im = spec_g[:, :LANES], spec_g[:, LANES:]
    s_re, s_im = spec_s[:, :LANES], spec_s[:, LANES:]
    spread_channels(ks_send, inverse(g_re * s_re + g_im * s_im, g_im * s_re - g_re * s_im))
    a2a_start(3, ks_send, ks_recv, block)
    f_re, f_im = spec_f[:, :LANES], spec_f[:, LANES:]
    spread_channels(kf_send, inverse(g_re * f_re + g_im * f_im, g_im * f_re - g_re * f_im))
    for cc in range(PER):
        value = jnp.sum(u_recv[:, cc, :] * sf_recv[pl.ds(cc, n, stride=8), :], axis=(0, 1), keepdims=True)
        kf_send[:, PER + cc, :] = jnp.broadcast_to(value, (n, LANES))
    a2a_start(4, kf_send, kf_recv, block)

    g_size = 2 * max_rank

    @pl.when(is_owner)
    def _():
        pltpu.make_async_copy(q_recv, q_recv, q_recv_sem).wait()
        g_send[...] = (q_send[...] + q_recv[0] + q_recv[1] + q_recv[2]).astype(BF)
        at = pl.ds(pl.multiple_of(me * g_size, g_size), g_size)

        def spread(d, _):
            pltpu.make_async_remote_copy(
                src_ref=g_send, dst_ref=g_recv.at[at, :], send_sem=g_sem.at[0], recv_sem=g_sem.at[1],
                device_id=(dp, lax.rem(me + d, n), ch), device_id_type=MESH,
            ).start()
            return 0

        lax.fori_loop(1, n, spread, 0, unroll=9 if n == 64 else 1)
        pltpu.make_async_copy(g_send, g_recv.at[at, :], g_sem.at[1]).start()

    def to_peers(src, dst, send_sem, recv_sem):
        copies = []
        for step in (1, 3, 2):
            copy = pltpu.make_async_remote_copy(
                src_ref=src, dst_ref=dst.at[step - 1], send_sem=send_sem.at[step], recv_sem=recv_sem,
                device_id=(lax.rem(dp + step, 4), me, ch), device_id_type=MESH,
            )
            copy.start()
            copies.append(copy)
        return copies

    a2a_wait(3, ks_recv)
    quarter = width // 4
    corr_st[...] = gather_channels(ks_recv)
    f_send[...] = corr_st[...].astype(BF)
    f_copies = []
    for step in (1, 3, 2):
        q = lax.rem(dp + step, 4)
        copy = pltpu.make_async_remote_copy(
            src_ref=f_send.at[pl.ds(pl.multiple_of(q * quarter, quarter), quarter), :],
            dst_ref=f_recv.at[step - 1], send_sem=f_send_sem.at[step], recv_sem=f_recv_sem,
            device_id=(q, me, ch), device_id_type=MESH,
        )
        copy.start()
        f_copies.append(copy)

    a2a_wait(4, kf_recv)
    skips = jnp.concatenate([kf_recv[:, PER + cc, :] for cc in range(PER)], axis=0)
    e_send[...] = skips.T[:8]
    e_copies = to_peers(e_send, e_recv, e_send_sem, e_recv_sem)

    pltpu.make_async_copy(f_recv, f_recv, f_recv_sem).wait()
    my_quarter = pl.ds(pl.multiple_of(dp * quarter, quarter), quarter)
    sums = corr_st[my_quarter, :]
    for k in range(3):
        sums = sums + f_recv[k].astype(F32)
    h_send[...] = sums.astype(BF)
    h_copies = []
    for step in (1, 3, 2):
        copy = pltpu.make_async_remote_copy(
            src_ref=h_send, dst_ref=h_recv.at[my_quarter, :], send_sem=h_send_sem.at[step],
            recv_sem=h_recv_sem, device_id=(lax.rem(dp + step, 4), me, ch), device_id_type=MESH,
        )
        copy.start()
        h_copies.append(copy)
    pltpu.make_async_copy(h_send, h_recv.at[my_quarter, :], h_recv_sem).start()
    gsig_ref[...] = (gather_channels(kf_recv) + skip_t * gradu_t[...]).T.astype(BF)
    outs[1].start()

    pltpu.make_async_copy(g_recv, g_recv, g_sem.at[1]).wait()
    outs[3].start()

    pltpu.make_async_copy(h_recv, h_recv, h_recv_sem).wait()
    gfilt_ref[...] = h_recv[...].astype(F32).T
    outs[2].start()

    pltpu.make_async_copy(e_recv, e_recv, e_recv_sem).wait()
    gskip_ref[...] = e_send[...] + e_recv[0] + e_recv[1] + e_recv[2]
    outs[4].start()

    for sub in range(SUB):
        for qq in range(2):
            for hh in range(2):
                @pl.when(to_other(qq))
                def _():
                    cot_copy(sub, qq, hh).wait_send()
    for qq in range(2):
        for hh in range(2):
            @pl.when((2 * ch + qq == dp) & (ch != hh))
            def _():
                own_copy(qq, hh).wait_send()
    a2a_wait_send(0, sf_send, 8)
    for k, src in ((1, c_send), (2, u_send), (3, ks_send), (4, kf_send)):
        a2a_wait_send(k, src, 1)
    w_copy.wait_send()
    pre0_copy.wait_send()
    wf_copy.wait_send()
    for copy in wy_copies + far_copies + pre_copies + ret_copies + f_copies + h_copies + e_copies:
        copy.wait_send()

    @pl.when(holds_far)
    def _():
        def sent(d, _):
            pltpu.make_async_copy(m_far.at[0], m_far.at[0], far_sem.at[0]).wait()
            return 0

        lax.fori_loop(1, 2 * group, sent, 0)

    def b_sent(count):
        part = b_send.at[:, pl.ds(0, count * LANES)]
        pltpu.make_async_copy(part, part, b_sem.at[0]).wait()

    @pl.when(me < n_own)
    def _():
        b_sent(n_own - 1)
        for step in (1, 3, 2):
            q_copy(step).wait_send()

        def sent(d, _):
            pltpu.make_async_copy(g_send, g_send, g_sem.at[0]).wait()
            return 0

        lax.fori_loop(1, n, sent, 0)

    @pl.when(me >= n_own)
    def _():
        b_sent(n_own)

    for out in outs:
        out.wait()


def received(copy, ref):
    copy.wait_recv()
    return ref[...].astype(F32)


def finish_kernel(
    gsig_in, ggat_in, gfilt_in, gbank_in, gskip_in,
    gsig_out, ggat_out, gfilt_out, gskip_out, ga_out, gb_out,
    gsig_ref, ggat_ref, gfilt_ref, gbank_ref, gskip_ref, ga_ref, gb_ref, in_sem, out_sem,
):
    max_rank, half = gb_ref.shape[1:]
    width = ga_ref.shape[2]
    g_size = 2 * max_rank
    up_chunks = half // LANES
    a_chunks = -(-width // LANES)
    pairs = (
        (gbank_in, gbank_ref), (gfilt_in, gfilt_ref), (gsig_in, gsig_ref), (ggat_in, ggat_ref),
        (gskip_in.at[pl.ds(0, 1)], gskip_ref),
    )
    loads = [pltpu.make_async_copy(s, d, in_sem.at[i]) for i, (s, d) in enumerate(pairs)]
    for load in loads:
        load.start()
    pairs = (
        (gb_ref, gb_out), (gfilt_ref, gfilt_out), (gsig_ref, gsig_out), (ggat_ref, ggat_out),
        (gskip_ref, gskip_out), (ga_ref, ga_out),
    )
    stores = [pltpu.make_async_copy(s, d, out_sem.at[i]) for i, (s, d) in enumerate(pairs)]
    loads[0].wait()

    def place(p, _):
        block = gbank_ref[pl.ds(pl.multiple_of(p * g_size, g_size), g_size), :].astype(F32)
        where = pl.ds(pl.multiple_of(p * LANES, LANES), LANES)
        gb_ref[0, :, where] = block[:max_rank]
        gb_ref[1, :, where] = block[max_rank:]
        return 0

    lax.fori_loop(0, up_chunks, place, 0, unroll=4)
    stores[0].start()
    for k in range(1, 5):
        loads[k].wait()
        stores[k].start()
    size = min(LANES, width)
    for k in range(a_chunks):
        at = (up_chunks + k) * g_size
        block = gbank_ref[at:at + g_size, :].astype(F32)
        ga_ref[0, :, k * size:(k + 1) * size] = block[:max_rank, :size]
        ga_ref[1, :, k * size:(k + 1) * size] = block[max_rank:, :size]
    stores[5].start()
    for store in stores:
        store.wait()


def local(
    signal, gating, cotangent, filt, skip, output_projection,
    adapter_down_bank, adapter_up_bank, adapter_index, sequence_rank, real_length,
):
    n = lax.axis_size("seq")
    width = signal.shape[2]
    half = cotangent.shape[2]
    cols = output_projection.shape[1] // 2
    max_rank = adapter_up_bank.shape[1]
    a_chunks = -(-width // LANES)
    n_own = half // LANES + a_chunks
    piece = LANES // SUB
    group = 2 * min(4, n // 2)
    far_cols = 2 * cols // group
    consts = [jnp.asarray(t) for t in tables(n)]
    rows = consts[4].shape[0]
    vmem = pl.BlockSpec(memory_space=pltpu.VMEM)
    smem = pl.BlockSpec(memory_space=pltpu.SMEM)
    hbm = pl.BlockSpec(memory_space=pltpu.HBM)
    dma = pltpu.SemaphoreType.DMA
    arrays = [
        signal[0], gating[0], cotangent[0], filt, skip[None], output_projection,
        jnp.swapaxes(adapter_down_bank, 1, 2), adapter_up_bank, *consts,
    ]
    block = pltpu.VMEM((n, PER, LANES), F32)
    eight = pltpu.VMEM((8 * n, LANES), F32)
    two = pltpu.VMEM((n, 2 * PER, LANES), F32)
    wide = pltpu.VMEM((width, LANES), F32)
    spec = pltpu.VMEM((PER * rows, 2 * LANES), F32)
    rank = pltpu.VMEM((max_rank, LANES), F32)
    outs = pl.pallas_call(
        functools.partial(kernel, n),
        out_shape=(
            jax.ShapeDtypeStruct((LANES, width), BF),
            jax.ShapeDtypeStruct((LANES, width), BF),
            jax.ShapeDtypeStruct((LANES, width), F32),
            jax.ShapeDtypeStruct((2 * max_rank * n_own, LANES), BF),
            jax.ShapeDtypeStruct((8, width), F32),
        ),
        in_specs=[smem] * 3 + [hbm] * len(arrays),
        out_specs=(hbm,) * 5,
        scratch_shapes=[
            pltpu.VMEM((LANES, width), BF),
            pltpu.VMEM((LANES, width), BF),
            pltpu.VMEM((LANES, width), F32),
            pltpu.VMEM((8, width), F32),
        ] + [pltpu.VMEM(a.shape, a.dtype) for a in arrays] + [
            pltpu.VMEM((LANES, half), BF),
            wide, wide, wide, spec, spec, spec,
            eight, eight, block, block, block, block, block, block, two, two,
            pltpu.VMEM((LANES, cols), BF),
            pltpu.VMEM((SUB, 2, piece, cols), BF),
            pltpu.VMEM((group, LANES, far_cols), BF),
            pltpu.VMEM((width, far_cols), BF),
            pltpu.VMEM(((group - 1) * LANES, width), BF),
            pltpu.VMEM((group - 1, LANES, width), BF),
            pltpu.VMEM((width, cols), BF),
            pltpu.VMEM((LANES, width), BF),
            pltpu.VMEM((LANES, width), BF),
            pltpu.VMEM((SUB, 2 * piece, width), BF),
            pltpu.VMEM((SUB, 2 * piece, width), BF),
            pltpu.VMEM((SUB, 2 * piece, width), BF),
            pltpu.VMEM((2, LANES, width), BF),
            rank, rank, rank, rank,
            pltpu.VMEM((max_rank, n_own * LANES), BF),
            pltpu.VMEM((16 * n, LANES), BF),
            pltpu.VMEM((2 * max_rank, LANES), F32),
            pltpu.VMEM((3, 2 * max_rank, LANES), F32),
            pltpu.VMEM((2 * max_rank, LANES), BF),
            pltpu.VMEM((2 * max_rank * n_own, LANES), BF),
            pltpu.VMEM((width, LANES), BF),
            pltpu.VMEM((3, width // 4, LANES), BF),
            wide,
            pltpu.VMEM((width // 4, LANES), BF),
            pltpu.VMEM((width, LANES), BF),
            pltpu.VMEM((8, width), F32),
            pltpu.VMEM((3, 8, width), F32),
            dma((len(arrays),)), dma((5,)), dma((5,)), dma((5,)), dma((SUB, 4)), dma((SUB,)), dma((2,)), dma((2,)),
            dma((2,)), dma((SUB,)), dma((SUB,)), dma((SUB, 4)), dma, dma((2,)), dma((2,)), dma((2,)),
            dma((4,)), dma, dma((2,)), dma((4,)), dma, dma((4,)), dma,
            dma((4,)), dma, dma((2,)), dma((2,)), dma((8,)), dma, dma((group,)), dma,
        ],
        compiler_params=pltpu.CompilerParams(
            collective_id=0, has_side_effects=True, vmem_limit_bytes=VMEM_LIMIT
        ),
    )(adapter_index, sequence_rank, real_length, *arrays)
    grad_signal, grad_gating, grad_filt, grad_skip, grad_a, grad_b = pl.pallas_call(
        finish_kernel,
        out_shape=(
            jax.ShapeDtypeStruct((LANES, width), BF),
            jax.ShapeDtypeStruct((LANES, width), BF),
            jax.ShapeDtypeStruct((LANES, width), F32),
            jax.ShapeDtypeStruct((1, width), F32),
            jax.ShapeDtypeStruct((2, max_rank, width), F32),
            jax.ShapeDtypeStruct((2, max_rank, half), F32),
        ),
        in_specs=[hbm] * 5,
        out_specs=(hbm,) * 6,
        scratch_shapes=[
            pltpu.VMEM((LANES, width), BF), pltpu.VMEM((LANES, width), BF), pltpu.VMEM((LANES, width), F32),
            pltpu.VMEM((2 * max_rank * n_own, LANES), BF), pltpu.VMEM((1, width), F32),
            pltpu.VMEM((2, max_rank, width), F32), pltpu.VMEM((2, max_rank, half), F32),
            dma((5,)), dma((6,)),
        ],
        compiler_params=pltpu.CompilerParams(vmem_limit_bytes=VMEM_LIMIT),
    )(*outs)
    return (grad_signal[None], grad_gating[None], grad_filt, grad_skip[0], jnp.swapaxes(grad_a, 1, 2), grad_b)


def solution(mesh):
    placed = (
        P("dp", "seq", "chan"), P("dp", "seq", "chan"), P("dp", "seq", "chan"), P("seq", "chan"),
        P("chan"), P("chan", "dp"), P(None, "chan", None), P(None, None, "chan"),
        P("dp"), P("dp"), P("dp"),
    )
    return jax.shard_map(
        local,
        mesh=mesh,
        in_specs=placed,
        out_specs=(
            P("dp", "seq", "chan"), P("dp", "seq", "chan"), P("seq", "chan"), P("chan"),
            P(None, "chan", None), P(None, None, "chan"),
        ),
        check_vma=False,
    )
```

```python
import functools
import math

import jax
import jax.numpy as jnp
import ml_dtypes
import numpy as np
from jax import lax
from jax.experimental import pallas as pl
from jax.experimental.pallas import tpu as pltpu
from jax.sharding import PartitionSpec as P

MESH = pl.DeviceIdType.MESH
BF = jnp.bfloat16
F32 = jnp.float32
LANES = 128
PER = 4
VMEM_LIMIT = 62 * 1024 * 1024
SUB = 2


def split3(table, axis, order):
    high = table.astype(ml_dtypes.bfloat16)
    low = (table - high.astype(np.float64)).astype(ml_dtypes.bfloat16)
    return np.concatenate([high if o else low for o in order], axis=axis)


def tables(n):
    rows = -(-(n + 1) // 8) * 8
    k1 = np.arange(rows)
    used = (k1 <= n).astype(np.float64)
    i = np.arange(n)
    a = np.arange(LANES)
    period = 2 * n * LANES
    th1 = 2 * math.pi * (k1[:, None] * i[None, :] % (2 * n)) / (2 * n)
    first = np.concatenate([np.cos(th1) * used[:, None], -np.sin(th1) * used[:, None]], 0)
    thw = 2 * math.pi * (k1[:, None] * a[None, :] % period) / period
    tw_cos, tw_sin = np.cos(thw), np.sin(thw)
    th2 = 2 * math.pi * (a[:, None] * a[None, :] % LANES) / LANES
    c2, s2 = np.cos(th2), np.sin(th2)
    second = np.block([[c2, -s2], [s2, c2]])
    second_back = np.block([[c2, s2], [-s2, c2]])
    weight = used * np.where((k1 == 0) | (k1 == n), 1.0, 2.0) / period
    last = np.concatenate([np.cos(th1).T * weight, -np.sin(th1).T * weight], 1)
    return (
        split3(first, 1, (1, 1, 0)),
        split3(second, 0, (1, 1, 0)),
        split3(second_back, 0, (1, 1, 0)),
        split3(last, 1, (1, 1, 0)),
        tw_cos.astype(np.float32),
        tw_sin.astype(np.float32),
    )


def split_data(x, axis):
    high = x.astype(BF)
    low = (x - high.astype(F32)).astype(BF)
    return jnp.concatenate([high, low, high], axis=axis)


def dot(a, b):
    return jnp.dot(a, b, preferred_element_type=F32)


def dot_t(a, b):
    return lax.dot_general(a, b, (((1,), (1,)), ((), ())), preferred_element_type=F32)


def dot_0(a, b):
    return lax.dot_general(a, b, (((0,), (0,)), ((), ())), preferred_element_type=F32)


def kernel(
    n,
    index_ref, rank_ref, length_ref,
    signal_hbm, gating_hbm, cot_hbm, filt_hbm, skip_hbm, w_hbm, down_hbm, up_hbm,
    t1_hbm, t2_hbm, t2b_hbm, t1b_hbm, tc_hbm, ts_hbm,
    gsig_hbm, ggat_hbm, gfilt_hbm, gbank_hbm,
    gsig_ref, ggat_ref, gfilt_ref,
    signal_ref, gating_ref, cot_ref, filt_ref, skip_ref, w_ref, down_ref, up_ref,
    t1_ref, t2_ref, t2b_ref, t1b_ref, tc_ref, ts_ref,
    masked, sig_t, gate_t, gradu_t, spec_s, spec_f, spec_g,
    sf_send, sf_recv, c_send, c_recv, u_send, u_recv, ks_send, ks_recv, kf_send, kf_recv,
    m_own, m_recv, m_far, w_far, far_send, far_recv, w_recv, pre0_send, pre0_recv, pre_send, pre_recv, ret_send, ret_recv,
    d_send, d_recv, r_send, r_recv,
    b_send, b_recv, q_send, q_recv, g_send, g_recv, f_send, f_recv, corr_st, h_send, h_recv,
    in_sem, out_sem, a2a_send_sem, a2a_recv_sem, m_send_sem, m_recv_sem, own_sem, w_sem, pre0_sem,
    pre_send_sem, pre_recv_sem, ret_send_sem, ret_recv_sem, d_sem, r_sem, b_sem,
    q_send_sem, q_recv_sem, g_sem, f_send_sem, f_recv_sem,
    h_send_sem, h_recv_sem, far_sem, wf_sem, wy_send_sem, wy_recv_sem, fr_send_sem, fr_recv_sem,
):
    dp = lax.axis_index("dp")
    me = lax.axis_index("seq")
    ch = lax.axis_index("chan")
    other = 1 - ch
    plane = n // 2
    zl, spot = lax.div(me, plane), lax.rem(me, plane)
    group = m_far.shape[0]
    nx = group // 2
    ny = plane // nx
    y, x = lax.div(spot, nx), lax.rem(spot, nx)
    g = zl * nx + x
    far_cols = m_far.shape[2]

    def member(k):
        return lax.div(k, nx) * plane + y * nx + lax.rem(k, nx)

    width = w_ref.shape[0]
    cols = w_ref.shape[1] // 2
    half = cot_ref.shape[1]
    piece = LANES // SUB
    n_own = b_send.shape[1] // LANES
    extras = n_own - n // 2
    rows = t1_ref.shape[0] // 2
    a_chunks = -(-width // LANES)

    barrier = pltpu.get_barrier_semaphore()
    for d in range(4):
        for z in range(2):
            for c in range(2):
                if d or c:
                    pl.semaphore_signal(
                        barrier, inc=1,
                        device_id=(lax.rem(dp + d, 4), lax.rem(zl + z, 2) * plane + spot, lax.rem(ch + c, 2)),
                        device_id_type=MESH,
                    )

    def greet(d, _):
        pl.semaphore_signal(
            barrier, inc=1, device_id=(dp, lax.rem(me + d, n), ch), device_id_type=MESH
        )
        return 0

    lax.fori_loop(1, n, greet, 0, unroll=9 if n == 64 else 1)
    for z in range(2):
        for k in range(1, nx):
            pl.semaphore_signal(
                barrier, inc=1, device_id=(dp, member(z * nx + lax.rem(x + k, nx)), other),
                device_id_type=MESH,
            )

    pairs = (
        (signal_hbm, signal_ref), (filt_hbm, filt_ref), (cot_hbm, cot_ref), (up_hbm, up_ref),
        (w_hbm, w_ref), (t1_hbm, t1_ref), (t2_hbm, t2_ref), (t2b_hbm, t2b_ref), (t1b_hbm, t1b_ref),
        (tc_hbm, tc_ref), (ts_hbm, ts_ref), (gating_hbm, gating_ref), (down_hbm, down_ref),
        (skip_hbm, skip_ref),
    )
    loads = [pltpu.make_async_copy(s, d, in_sem.at[i]) for i, (s, d) in enumerate(pairs)]
    for load in loads:
        load.start()

    loads[0].wait()
    loads[1].wait()
    sig_t[...] = signal_ref[...].astype(F32).T
    filt_t = filt_ref[...].T
    for cc in range(PER):
        sf_send[pl.ds(cc, n, stride=8), :] = sig_t[cc * n:(cc + 1) * n, :]
        sf_send[pl.ds(PER + cc, n, stride=8), :] = filt_t[cc * n:(cc + 1) * n, :]
    real_length = length_ref[0]
    live_col = (me * LANES + lax.broadcasted_iota(jnp.int32, (LANES, 1), 0) < real_length).astype(F32)
    live_row = (me * LANES + lax.broadcasted_iota(jnp.int32, (1, LANES), 1) < real_length).astype(F32)
    pick1 = index_ref[0].astype(F32)
    pick0 = 1.0 - pick1

    pl.semaphore_wait(barrier, n - 1 + 14 + 2 * (nx - 1))

    def a2a_start(k, src, dst, at):
        def body(d, _):
            j = lax.rem(me + d, n)
            pltpu.make_async_remote_copy(
                src_ref=src.at[at(j)],
                dst_ref=dst.at[at(me)],
                send_sem=a2a_send_sem.at[k],
                recv_sem=a2a_recv_sem.at[k],
                device_id=(dp, j, ch),
                device_id_type=MESH,
            ).start()
            return 0

        lax.fori_loop(1, n, body, 0, unroll=9 if n == 64 else 1)
        pltpu.make_async_copy(src.at[at(me)], dst.at[at(me)], a2a_recv_sem.at[k]).start()

    def a2a_wait(k, dst):
        pltpu.make_async_copy(dst, dst, a2a_recv_sem.at[k]).wait()

    def a2a_wait_send(k, src, size):
        part = src.at[pl.ds(0, (n - 1) * size)]
        pltpu.make_async_copy(part, part, a2a_send_sem.at[k]).wait()

    def eight(j):
        return pl.ds(pl.multiple_of(j * 8, 8), 8)

    def block(j):
        return j

    a2a_start(0, sf_send, sf_recv, eight)

    def cot_copy(sub, qq, hh):
        q = 2 * ch + qq
        return pltpu.make_async_remote_copy(
            src_ref=cot_hbm.at[pl.ds(sub * piece, piece), pl.ds((2 * qq + hh) * cols, cols)],
            dst_ref=m_recv.at[sub, zl],
            send_sem=m_send_sem.at[sub, 2 * qq + hh],
            recv_sem=m_recv_sem.at[sub],
            device_id=(q, lax.div(lax.rem(q - dp + 4, 4), 3) * plane + spot, hh),
            device_id_type=MESH,
        )

    def own_copy(qq, hh):
        return pltpu.make_async_remote_copy(
            src_ref=cot_hbm.at[:, pl.ds((2 * qq + hh) * cols, cols)],
            dst_ref=m_own,
            send_sem=own_sem.at[0],
            recv_sem=own_sem.at[1],
            device_id=(dp, me, hh),
            device_id_type=MESH,
        )

    def to_other(qq):
        return lax.rem(2 * ch + qq - dp + 4, 2) == 1

    for sub in range(SUB):
        for qq in range(2):
            for hh in range(2):
                @pl.when(to_other(qq))
                def _():
                    cot_copy(sub, qq, hh).start()
    for qq in range(2):
        for hh in range(2):
            @pl.when((2 * ch + qq == dp) & (ch != hh))
            def _():
                own_copy(qq, hh).start()

            @pl.when((2 * ch + qq == dp) & (ch == hh))
            def _():
                pltpu.make_async_copy(
                    cot_hbm.at[:, pl.ds((2 * qq + hh) * cols, cols)], m_own, own_sem.at[1]
                ).start()

    far = lax.rem(dp + 2, 4)
    slice_rows = width // ny
    my_slice = pl.ds(pl.multiple_of(y * slice_rows, slice_rows), slice_rows)

    wf_copy = pltpu.make_async_remote_copy(
        src_ref=w_hbm.at[my_slice, pl.ds(pl.multiple_of(g * far_cols, far_cols), far_cols)],
        dst_ref=w_far.at[my_slice, :],
        send_sem=wf_sem.at[0], recv_sem=wf_sem.at[1], device_id=(far, me, ch), device_id_type=MESH,
    )
    wf_copy.start()

    def far_copy(d, c):
        k = lax.rem(g + d, group)
        at = lax.rem(far, 2) * 2 * cols + k * far_cols
        src = cot_hbm.at[:, pl.ds(pl.multiple_of(at, far_cols), far_cols)]
        if d == 0 and c == 0:
            return pltpu.make_async_copy(src, m_far.at[d], far_sem.at[1])
        return pltpu.make_async_remote_copy(
            src_ref=src, dst_ref=m_far.at[d], send_sem=far_sem.at[0], recv_sem=far_sem.at[1],
            device_id=(dp, member(k), lax.rem(ch + c, 2)), device_id_type=MESH,
        )

    holds_far = ch == lax.div(far, 2)

    @pl.when(holds_far)
    def _():
        for d in range(group):
            for c in range(2):
                far_copy(d, c).start()

    def to_chan(src, dst, send_sem, recv_sem):
        return pltpu.make_async_remote_copy(
            src_ref=src, dst_ref=dst, send_sem=send_sem, recv_sem=recv_sem,
            device_id=(dp, me, other), device_id_type=MESH,
        )

    w_copy = to_chan(
        w_hbm.at[:, pl.ds(pl.multiple_of(other * cols, LANES), cols)], w_recv, w_sem.at[0], w_sem.at[1]
    )
    w_copy.start()

    wf_copy.wait_recv()
    wy_copies = []
    for k in range(1, ny):
        copy = pltpu.make_async_remote_copy(
            src_ref=w_far.at[my_slice, :], dst_ref=w_far.at[my_slice, :],
            send_sem=wy_send_sem.at[k], recv_sem=wy_recv_sem,
            device_id=(dp, zl * plane + lax.rem(y + k, ny) * nx + x, ch), device_id_type=MESH,
        )
        copy.start()
        wy_copies.append(copy)

    for load in loads[2:]:
        load.wait()
    masked[...] = (cot_ref[...].astype(F32) * live_col).astype(BF)
    up_sel = (up_ref[0].astype(F32) * pick0 + up_ref[1].astype(F32) * pick1).astype(BF)
    down_sel = (down_ref[0].astype(F32) * pick0 + down_ref[1].astype(F32) * pick1).astype(BF)
    max_rank = up_sel.shape[0]
    keep = (lax.broadcasted_iota(jnp.int32, (max_rank, LANES), 0) < rank_ref[0]).astype(F32)
    d_send[...] = dot_t(up_sel, masked[...])
    d_copy = to_chan(d_send, d_recv, d_sem.at[0], d_sem.at[1])
    d_copy.start()
    gate_t[...] = gating_ref[...].astype(F32).T
    skip_t = jnp.broadcast_to(skip_ref[...], (LANES, width)).T

    own_cols = pl.ds(pl.multiple_of(ch * cols, LANES), cols)
    pltpu.make_async_copy(m_own, m_own, own_sem.at[1]).wait()
    w_copy.wait_recv()
    pre0_send[...] = dot_t(m_own[...], w_recv[...]).astype(BF)
    pre0_copy = to_chan(pre0_send, pre0_recv, pre0_sem.at[0], pre0_sem.at[1])
    pre0_copy.start()
    own_part = dot_t(m_own[...], w_ref[:, own_cols])

    pre_copies, ret_copies = [], []

    def project(sub):
        pltpu.make_async_copy(m_recv.at[sub], m_recv.at[sub], m_recv_sem.at[sub]).wait()
        part = m_recv[sub].reshape(2 * piece, cols)
        pre_send[sub] = dot_t(part, w_recv[...]).astype(BF)
        copy = to_chan(pre_send.at[sub], pre_recv.at[sub], pre_send_sem.at[sub], pre_recv_sem.at[sub])
        copy.start()
        pre_copies.append(copy)
        return dot_t(part, w_ref[:, own_cols])

    def give_back(sub, mine):
        pre_copies[sub].wait_recv()
        ret_send[sub] = (mine + pre_recv[sub].astype(F32)).astype(BF)
        for slot in range(2):
            copy = pltpu.make_async_remote_copy(
                src_ref=ret_send.at[sub, pl.ds(slot * piece, piece)],
                dst_ref=ret_recv.at[zl, pl.ds(sub * piece, piece)],
                send_sem=ret_send_sem.at[sub, slot], recv_sem=ret_recv_sem,
                device_id=(lax.rem(dp + 3 - 2 * zl, 4), slot * plane + spot, ch), device_id_type=MESH,
            )
            copy.start()
            ret_copies.append(copy)

    tc, ts = tc_ref[...], ts_ref[...]

    def forward(load, store):
        x = jnp.concatenate([load(cc) for cc in range(PER)], axis=1)
        y = dot(t1_ref[...], split_data(x, 0))
        parts = []
        for cc in range(PER):
            re = y[:rows, cc * LANES:(cc + 1) * LANES]
            im = y[rows:, cc * LANES:(cc + 1) * LANES]
            parts.append(jnp.concatenate([re * tc + im * ts, im * tc - re * ts], axis=1))
        store[...] = dot(split_data(jnp.concatenate(parts, axis=0), 1), t2_ref[...])

    def inverse(re, im):
        q = dot(split_data(jnp.concatenate([re, im], axis=1), 1), t2b_ref[...])
        parts = []
        for cc in range(PER):
            qr = q[cc * rows:(cc + 1) * rows, :LANES]
            qi = q[cc * rows:(cc + 1) * rows, LANES:]
            parts.append(jnp.concatenate([qr * tc - qi * ts, qi * tc + qr * ts], axis=0))
        return dot(t1b_ref[...], split_data(jnp.concatenate(parts, axis=1), 0))

    def spread_channels(dst, values):
        for cc in range(PER):
            dst[:, cc, :] = values[:, cc * LANES:(cc + 1) * LANES]

    def gather_channels(src):
        return jnp.concatenate([src[:, cc, :] for cc in range(PER)], axis=0)

    a2a_wait(0, sf_recv)
    forward(lambda cc: sf_recv[pl.ds(cc, n, stride=8), :], spec_s)
    forward(lambda cc: sf_recv[pl.ds(PER + cc, n, stride=8), :], spec_f)
    s_re, s_im = spec_s[:, :LANES], spec_s[:, LANES:]
    f_re, f_im = spec_f[:, :LANES], spec_f[:, LANES:]
    spread_channels(c_send, inverse(s_re * f_re - s_im * f_im, s_re * f_im + s_im * f_re))
    a2a_start(1, c_send, c_recv, block)

    d_copy.wait()
    back_rank = (2.0 * (d_send[...] + d_recv[...]) * keep).astype(BF)

    pltpu.make_async_copy(m_far, m_far, far_sem.at[1]).wait()
    if ny > 1:
        rest = w_far.at[pl.ds(0, (ny - 1) * slice_rows), :]
        pltpu.make_async_copy(rest, rest, wy_recv_sem).wait()
    far_part = dot_t(m_far[...].reshape(group * LANES, far_cols), w_far[...])
    far_send[...] = far_part[LANES:].astype(BF)
    own_part = own_part + far_part[:LANES]
    far_copies = []
    for d in range(1, group):
        copy = pltpu.make_async_remote_copy(
            src_ref=far_send.at[pl.ds((d - 1) * LANES, LANES), :], dst_ref=far_recv.at[d - 1],
            send_sem=fr_send_sem.at[d], recv_sem=fr_recv_sem,
            device_id=(dp, member(lax.rem(g + group - d, group)), ch), device_id_type=MESH,
        )
        copy.start()
        far_copies.append(copy)

    mine = project(0)
    for sub in range(1, SUB):
        after = project(sub)
        give_back(sub - 1, mine)
        mine = after
    give_back(SUB - 1, mine)

    a2a_wait(1, c_recv)
    inner_t = gather_channels(c_recv) + skip_t * sig_t[...]
    gated_t = (gate_t[...] * inner_t).astype(BF)
    r_send[...] = dot(down_sel, gated_t)
    r_copy = to_chan(r_send, r_recv, r_sem.at[0], r_sem.at[1])
    r_copy.start()
    b_send[:, half:half + width] = dot_t(back_rank, gated_t).astype(BF)

    grad_y = own_part + received(pre0_copy, pre0_recv)
    pltpu.make_async_copy(ret_recv, ret_recv, ret_recv_sem).wait()
    pltpu.make_async_copy(far_recv, far_recv, fr_recv_sem).wait()
    for k in range(2):
        grad_y = grad_y + ret_recv[k].astype(F32)
    for k in range(group - 1):
        grad_y = grad_y + far_recv[k].astype(F32)
    grad_y = grad_y.T * live_row + dot_0(down_sel, back_rank)
    grad_u = grad_y * gate_t[...]
    gradu_t[...] = grad_u
    for cc in range(PER):
        u_send[:, cc, :] = gradu_t[cc * n:(cc + 1) * n, :]
    a2a_start(2, u_send, u_recv, block)
    r_copy.wait()
    fwd_rank = (2.0 * (r_send[...] + r_recv[...]) * keep).astype(BF)
    b_send[:, :half] = dot(fwd_rank, masked[...]).astype(BF)

    product = grad_u * sig_t[...]
    high = product.astype(BF)
    low = (product - high.astype(F32)).astype(BF)
    ones = jnp.ones((max_rank, LANES), BF)
    at = half + a_chunks * LANES
    b_send[:, at:at + width] = (dot_t(ones, high) + dot_t(ones, low)).astype(BF)

    def share(p, owner):
        src = b_send.at[:, pl.ds(pl.multiple_of(p * LANES, LANES), LANES)]
        dst = b_recv.at[pl.ds(pl.multiple_of(me * 16, 16), 16), :]

        @pl.when(owner != me)
        def _():
            pltpu.make_async_remote_copy(
                src_ref=src, dst_ref=dst, send_sem=b_sem.at[0], recv_sem=b_sem.at[1],
                device_id=(dp, owner, ch), device_id_type=MESH,
            ).start()

        @pl.when(owner == me)
        def _():
            pltpu.make_async_copy(src, dst, b_sem.at[1]).start()

    def share_main(d, _):
        p = lax.rem(me + d, plane)
        share(p, p)
        return 0

    for k in range(extras):
        share(plane + k, plane + (k % ny) * nx + k // ny)
    lax.fori_loop(0, plane, share_main, 0, unroll=4 if n == 64 else 1)

    ggat_ref[...] = (grad_y * inner_t).T.astype(BF)
    outs = [
        pltpu.make_async_copy(s, d, out_sem.at[i])
        for i, (s, d) in enumerate((
            (ggat_ref, ggat_hbm), (gsig_ref, gsig_hbm), (gfilt_ref, gfilt_hbm), (g_recv, gbank_hbm),
        ))
    ]
    outs[0].start()

    a2a_wait(2, u_recv)
    forward(lambda cc: u_recv[:, cc, :], spec_g)
    g_re, g_im = spec_g[:, :LANES], spec_g[:, LANES:]
    s_re, s_im = spec_s[:, :LANES], spec_s[:, LANES:]
    spread_channels(ks_send, inverse(g_re * s_re + g_im * s_im, g_im * s_re - g_re * s_im))
    a2a_start(3, ks_send, ks_recv, block)
    f_re, f_im = spec_f[:, :LANES], spec_f[:, LANES:]
    spread_channels(kf_send, inverse(g_re * f_re + g_im * f_im, g_im * f_re - g_re * f_im))
    a2a_start(4, kf_send, kf_recv, block)

    column = zl * plane + x * ny
    is_owner = column + y < n_own

    def q_copy(step):
        return pltpu.make_async_remote_copy(
            src_ref=q_send, dst_ref=q_recv.at[step - 1], send_sem=q_send_sem.at[step],
            recv_sem=q_recv_sem, device_id=(lax.rem(dp + step, 4), me, ch), device_id_type=MESH,
        )

    @pl.when(is_owner)
    def _():
        pltpu.make_async_copy(b_recv, b_recv, b_sem.at[1]).wait()
        acc = b_recv[0:16, :].astype(F32)
        for i in range(1, n):
            acc = acc + b_recv[16 * i:16 * (i + 1), :].astype(F32)
        q_send[...] = jnp.concatenate([acc * pick0, acc * pick1], axis=0)
        for step in (1, 3, 2):
            q_copy(step).start()

    a2a_wait(3, ks_recv)
    quarter = width // 4
    corr_st[...] = gather_channels(ks_recv)
    f_send[...] = corr_st[...].astype(BF)
    f_copies = []
    for step in (1, 3, 2):
        q = lax.rem(dp + step, 4)
        copy = pltpu.make_async_remote_copy(
            src_ref=f_send.at[pl.ds(pl.multiple_of(q * quarter, quarter), quarter), :],
            dst_ref=f_recv.at[step - 1], send_sem=f_send_sem.at[step], recv_sem=f_recv_sem,
            device_id=(q, me, ch), device_id_type=MESH,
        )
        copy.start()
        f_copies.append(copy)

    g_size = 2 * max_rank
    bank_rows = pl.ds(pl.multiple_of((column + y) * g_size, g_size), g_size)

    @pl.when(is_owner)
    def _():
        pltpu.make_async_copy(q_recv, q_recv, q_recv_sem).wait()
        g_send[...] = (q_send[...] + q_recv[0] + q_recv[1] + q_recv[2]).astype(BF)
        for k in range(1, ny):
            pltpu.make_async_remote_copy(
                src_ref=g_send, dst_ref=g_recv.at[bank_rows, :], send_sem=g_sem.at[0], recv_sem=g_sem.at[1],
                device_id=(dp, zl * plane + lax.rem(y + k, ny) * nx + x, ch), device_id_type=MESH,
            ).start()
        pltpu.make_async_copy(g_send, g_recv.at[bank_rows, :], g_sem.at[1]).start()

    a2a_wait(4, kf_recv)
    gsig_ref[...] = (gather_channels(kf_recv) + skip_t * gradu_t[...]).T.astype(BF)
    outs[1].start()

    pltpu.make_async_copy(f_recv, f_recv, f_recv_sem).wait()
    my_quarter = pl.ds(pl.multiple_of(dp * quarter, quarter), quarter)
    sums = corr_st[my_quarter, :]
    for k in range(3):
        sums = sums + f_recv[k].astype(F32)
    h_send[...] = sums.astype(BF)
    h_copies = []
    for step in (1, 3, 2):
        copy = pltpu.make_async_remote_copy(
            src_ref=h_send, dst_ref=h_recv.at[my_quarter, :], send_sem=h_send_sem.at[step],
            recv_sem=h_recv_sem, device_id=(lax.rem(dp + step, 4), me, ch), device_id_type=MESH,
        )
        copy.start()
        h_copies.append(copy)
    pltpu.make_async_copy(h_send, h_recv.at[my_quarter, :], h_recv_sem).start()

    columns = [(zl == 0, ny)] + [
        ((zl == 1) & (x == k), max(0, min(ny, extras - k * ny))) for k in range(nx)
    ]

    def block_copy(k, count):
        rows_of = pl.ds(pl.multiple_of(column * g_size, g_size), count * g_size)
        return pltpu.make_async_remote_copy(
            src_ref=g_recv.at[rows_of, :], dst_ref=g_recv.at[rows_of, :],
            send_sem=g_sem.at[2], recv_sem=g_sem.at[3],
            device_id=(dp, member(lax.rem(g + k, group)), ch), device_id_type=MESH,
        )

    for here, count in columns:
        if count:
            @pl.when(here)
            def _():
                part = g_recv.at[pl.ds(0, count * g_size), :]
                pltpu.make_async_copy(part, part, g_sem.at[1]).wait()
                for k in range(1, group):
                    block_copy(k, count).start()

    pltpu.make_async_copy(h_recv, h_recv, h_recv_sem).wait()
    gfilt_ref[...] = h_recv[...].astype(F32).T
    outs[2].start()

    for here, count in columns:
        @pl.when(here)
        def _():
            part = g_recv.at[pl.ds(0, (n_own - count) * g_size), :]
            pltpu.make_async_copy(part, part, g_sem.at[3]).wait()
    outs[3].start()

    for sub in range(SUB):
        for qq in range(2):
            for hh in range(2):
                @pl.when(to_other(qq))
                def _():
                    cot_copy(sub, qq, hh).wait_send()
    for qq in range(2):
        for hh in range(2):
            @pl.when((2 * ch + qq == dp) & (ch != hh))
            def _():
                own_copy(qq, hh).wait_send()
    a2a_wait_send(0, sf_send, 8)
    for k, src in ((1, c_send), (2, u_send), (3, ks_send), (4, kf_send)):
        a2a_wait_send(k, src, 1)
    w_copy.wait_send()
    pre0_copy.wait_send()
    wf_copy.wait_send()
    for copy in wy_copies + far_copies + pre_copies + ret_copies + f_copies + h_copies:
        copy.wait_send()

    @pl.when(holds_far)
    def _():
        def sent(d, _):
            pltpu.make_async_copy(m_far.at[0], m_far.at[0], far_sem.at[0]).wait()
            return 0

        lax.fori_loop(1, 2 * group, sent, 0)

    def b_sent(count):
        part = b_send.at[:, pl.ds(0, count * LANES)]
        pltpu.make_async_copy(part, part, b_sem.at[0]).wait()

    @pl.when(is_owner)
    def _():
        b_sent(n_own - 1)
        for step in (1, 3, 2):
            q_copy(step).wait_send()
        for _ in range(1, ny):
            pltpu.make_async_copy(g_send, g_send, g_sem.at[0]).wait()

    @pl.when(jnp.logical_not(is_owner))
    def _():
        b_sent(n_own)

    for here, count in columns:
        if count:
            @pl.when(here)
            def _():
                for k in range(1, group):
                    block_copy(k, count).wait_send()

    for out in outs:
        out.wait()


def received(copy, ref):
    copy.wait_recv()
    return ref[...].astype(F32)


def finish_kernel(
    ny,
    gsig_in, ggat_in, gfilt_in, gbank_in,
    gsig_out, ggat_out, gfilt_out, gskip_out, ga_out, gb_out,
    gsig_ref, ggat_ref, gfilt_ref, gbank_ref, gskip_ref, ga_ref, gb_ref, in_sem, out_sem,
):
    max_rank, half = gb_ref.shape[1:]
    width = ga_ref.shape[2]
    g_size = 2 * max_rank
    up_chunks = half // LANES
    nx = up_chunks // ny
    a_chunks = -(-width // LANES)
    pairs = ((gbank_in, gbank_ref), (gfilt_in, gfilt_ref), (gsig_in, gsig_ref), (ggat_in, ggat_ref))
    loads = [pltpu.make_async_copy(s, d, in_sem.at[i]) for i, (s, d) in enumerate(pairs)]
    for load in loads:
        load.start()
    pairs = (
        (gb_ref, gb_out), (gfilt_ref, gfilt_out), (gsig_ref, gsig_out), (ggat_ref, ggat_out),
        (gskip_ref, gskip_out), (ga_ref, ga_out),
    )
    stores = [pltpu.make_async_copy(s, d, out_sem.at[i]) for i, (s, d) in enumerate(pairs)]
    loads[0].wait()
    for p in range(up_chunks):
        at = ((p % nx) * ny + p // nx) * g_size
        block = gbank_ref[at:at + g_size, :].astype(F32)
        gb_ref[0, :, p * LANES:(p + 1) * LANES] = block[:max_rank]
        gb_ref[1, :, p * LANES:(p + 1) * LANES] = block[max_rank:]
    stores[0].start()
    for k in range(1, 4):
        loads[k].wait()
        stores[k].start()
    size = min(LANES, width)
    for k in range(a_chunks):
        at = (up_chunks + k) * g_size
        block = gbank_ref[at:at + g_size, :].astype(F32)
        ga_ref[0, :, k * size:(k + 1) * size] = block[:max_rank, :size]
        ga_ref[1, :, k * size:(k + 1) * size] = block[max_rank:, :size]
        at = (up_chunks + a_chunks + k) * g_size
        block = gbank_ref[at:at + g_size, :].astype(F32)
        gskip_ref[:, k * size:(k + 1) * size] = (block[0:1] + block[max_rank:max_rank + 1])[:, :size]
    stores[4].start()
    stores[5].start()
    for store in stores:
        store.wait()


def local(
    signal, gating, cotangent, filt, skip, output_projection,
    adapter_down_bank, adapter_up_bank, adapter_index, sequence_rank, real_length,
):
    n = lax.axis_size("seq")
    width = signal.shape[2]
    half = cotangent.shape[2]
    cols = output_projection.shape[1] // 2
    max_rank = adapter_up_bank.shape[1]
    a_chunks = -(-width // LANES)
    n_own = half // LANES + 2 * a_chunks
    piece = LANES // SUB
    group = 2 * min(4, n // 2)
    far_cols = 2 * cols // group
    consts = [jnp.asarray(t) for t in tables(n)]
    rows = consts[4].shape[0]
    vmem = pl.BlockSpec(memory_space=pltpu.VMEM)
    smem = pl.BlockSpec(memory_space=pltpu.SMEM)
    hbm = pl.BlockSpec(memory_space=pltpu.HBM)
    dma = pltpu.SemaphoreType.DMA
    arrays = [
        signal[0], gating[0], cotangent[0], filt, skip[None], output_projection,
        jnp.swapaxes(adapter_down_bank, 1, 2), adapter_up_bank, *consts,
    ]
    block = pltpu.VMEM((n, PER, LANES), F32)
    eight = pltpu.VMEM((8 * n, LANES), F32)
    wide = pltpu.VMEM((width, LANES), F32)
    spec = pltpu.VMEM((PER * rows, 2 * LANES), F32)
    rank = pltpu.VMEM((max_rank, LANES), F32)
    outs = pl.pallas_call(
        functools.partial(kernel, n),
        out_shape=(
            jax.ShapeDtypeStruct((LANES, width), BF),
            jax.ShapeDtypeStruct((LANES, width), BF),
            jax.ShapeDtypeStruct((LANES, width), F32),
            jax.ShapeDtypeStruct((2 * max_rank * n_own, LANES), BF),
        ),
        in_specs=[smem] * 3 + [hbm] * len(arrays),
        out_specs=(hbm,) * 4,
        scratch_shapes=[
            pltpu.VMEM((LANES, width), BF),
            pltpu.VMEM((LANES, width), BF),
            pltpu.VMEM((LANES, width), F32),
        ] + [pltpu.VMEM(a.shape, a.dtype) for a in arrays] + [
            pltpu.VMEM((LANES, half), BF),
            wide, wide, wide, spec, spec, spec,
            eight, eight, block, block, block, block, block, block, block, block,
            pltpu.VMEM((LANES, cols), BF),
            pltpu.VMEM((SUB, 2, piece, cols), BF),
            pltpu.VMEM((group, LANES, far_cols), BF),
            pltpu.VMEM((width, far_cols), BF),
            pltpu.VMEM(((group - 1) * LANES, width), BF),
            pltpu.VMEM((group - 1, LANES, width), BF),
            pltpu.VMEM((width, cols), BF),
            pltpu.VMEM((LANES, width), BF),
            pltpu.VMEM((LANES, width), BF),
            pltpu.VMEM((SUB, 2 * piece, width), BF),
            pltpu.VMEM((SUB, 2 * piece, width), BF),
            pltpu.VMEM((SUB, 2 * piece, width), BF),
            pltpu.VMEM((2, LANES, width), BF),
            rank, rank, rank, rank,
            pltpu.VMEM((max_rank, n_own * LANES), BF),
            pltpu.VMEM((16 * n, LANES), BF),
            pltpu.VMEM((2 * max_rank, LANES), F32),
            pltpu.VMEM((3, 2 * max_rank, LANES), F32),
            pltpu.VMEM((2 * max_rank, LANES), BF),
            pltpu.VMEM((2 * max_rank * n_own, LANES), BF),
            pltpu.VMEM((width, LANES), BF),
            pltpu.VMEM((3, width // 4, LANES), BF),
            wide,
            pltpu.VMEM((width // 4, LANES), BF),
            pltpu.VMEM((width, LANES), BF),
            dma((len(arrays),)), dma((4,)), dma((5,)), dma((5,)), dma((SUB, 4)), dma((SUB,)), dma((2,)), dma((2,)),
            dma((2,)), dma((SUB,)), dma((SUB,)), dma((SUB, 4)), dma, dma((2,)), dma((2,)), dma((2,)),
            dma((4,)), dma, dma((4,)), dma((4,)), dma,
            dma((4,)), dma, dma((2,)), dma((2,)), dma((8,)), dma, dma((group,)), dma,
        ],
        compiler_params=pltpu.CompilerParams(
            collective_id=0, has_side_effects=True, vmem_limit_bytes=VMEM_LIMIT
        ),
    )(adapter_index, sequence_rank, real_length, *arrays)
    grad_signal, grad_gating, grad_filt, grad_skip, grad_a, grad_b = pl.pallas_call(
        functools.partial(finish_kernel, n // group),
        out_shape=(
            jax.ShapeDtypeStruct((LANES, width), BF),
            jax.ShapeDtypeStruct((LANES, width), BF),
            jax.ShapeDtypeStruct((LANES, width), F32),
            jax.ShapeDtypeStruct((1, width), F32),
            jax.ShapeDtypeStruct((2, max_rank, width), F32),
            jax.ShapeDtypeStruct((2, max_rank, half), F32),
        ),
        in_specs=[hbm] * 4,
        out_specs=(hbm,) * 6,
        scratch_shapes=[
            pltpu.VMEM((LANES, width), BF), pltpu.VMEM((LANES, width), BF), pltpu.VMEM((LANES, width), F32),
            pltpu.VMEM((2 * max_rank * n_own, LANES), BF), pltpu.VMEM((1, width), F32),
            pltpu.VMEM((2, max_rank, width), F32), pltpu.VMEM((2, max_rank, half), F32),
            dma((4,)), dma((6,)),
        ],
        compiler_params=pltpu.CompilerParams(vmem_limit_bytes=VMEM_LIMIT),
    )(*outs)
    return (grad_signal[None], grad_gating[None], grad_filt, grad_skip[0], jnp.swapaxes(grad_a, 1, 2), grad_b)


def solution(mesh):
    placed = (
        P("dp", "seq", "chan"), P("dp", "seq", "chan"), P("dp", "seq", "chan"), P("seq", "chan"),
        P("chan"), P("chan", "dp"), P(None, "chan", None), P(None, None, "chan"),
        P("dp"), P("dp"), P("dp"),
    )
    return jax.shard_map(
        local,
        mesh=mesh,
        in_specs=placed,
        out_specs=(
            P("dp", "seq", "chan"), P("dp", "seq", "chan"), P("seq", "chan"), P("chan"),
            P(None, "chan", None), P(None, None, "chan"),
        ),
        check_vma=False,
    )
```

```python
import functools
import math

import jax
import jax.numpy as jnp
import ml_dtypes
import numpy as np
from jax import lax
from jax.experimental import pallas as pl
from jax.experimental.pallas import tpu as pltpu
from jax.sharding import PartitionSpec as P

MESH = pl.DeviceIdType.MESH
BF = jnp.bfloat16
F32 = jnp.float32
LANES = 128
PER = 4
VMEM_LIMIT = 62 * 1024 * 1024
SUB = 2


def split3(table, axis, order):
    high = table.astype(ml_dtypes.bfloat16)
    low = (table - high.astype(np.float64)).astype(ml_dtypes.bfloat16)
    return np.concatenate([high if o else low for o in order], axis=axis)


def tables(n):
    rows = -(-(n + 1) // 8) * 8
    k1 = np.arange(rows)
    used = (k1 <= n).astype(np.float64)
    i = np.arange(n)
    a = np.arange(LANES)
    period = 2 * n * LANES
    th1 = 2 * math.pi * (k1[:, None] * i[None, :] % (2 * n)) / (2 * n)
    first = np.concatenate([np.cos(th1) * used[:, None], -np.sin(th1) * used[:, None]], 0)
    thw = 2 * math.pi * (k1[:, None] * a[None, :] % period) / period
    tw_cos, tw_sin = np.cos(thw), np.sin(thw)
    th2 = 2 * math.pi * (a[:, None] * a[None, :] % LANES) / LANES
    c2, s2 = np.cos(th2), np.sin(th2)
    second = np.block([[c2, -s2], [s2, c2]])
    second_back = np.block([[c2, s2], [-s2, c2]])
    weight = used * np.where((k1 == 0) | (k1 == n), 1.0, 2.0) / period
    last = np.concatenate([np.cos(th1).T * weight, -np.sin(th1).T * weight], 1)
    return (
        split3(first, 1, (1, 1, 0)),
        split3(second, 0, (1, 1, 0)),
        split3(second_back, 0, (1, 1, 0)),
        split3(last, 1, (1, 1, 0)),
        tw_cos.astype(np.float32),
        tw_sin.astype(np.float32),
    )


def split_data(x, axis):
    high = x.astype(BF)
    low = (x - high.astype(F32)).astype(BF)
    return jnp.concatenate([high, low, high], axis=axis)


def dot(a, b):
    return jnp.dot(a, b, preferred_element_type=F32)


def dot_t(a, b):
    return lax.dot_general(a, b, (((1,), (1,)), ((), ())), preferred_element_type=F32)


def dot_0(a, b):
    return lax.dot_general(a, b, (((0,), (0,)), ((), ())), preferred_element_type=F32)


def kernel(
    n,
    index_ref, rank_ref, length_ref,
    signal_hbm, gating_hbm, cot_hbm, filt_hbm, skip_hbm, w_hbm, down_hbm, up_hbm,
    t1_hbm, t2_hbm, t2b_hbm, t1b_hbm, tc_hbm, ts_hbm,
    gsig_hbm, ggat_hbm, gfilt_hbm, gbank_hbm,
    gsig_ref, ggat_ref, gfilt_ref,
    signal_ref, gating_ref, cot_ref, filt_ref, skip_ref, w_ref, down_ref, up_ref,
    t1_ref, t2_ref, t2b_ref, t1b_ref, tc_ref, ts_ref,
    masked, sig_t, gate_t, gradu_t, spec_s, spec_f, spec_g,
    sf_send, sf_recv, c_send, c_recv, u_send, u_recv, ks_send, ks_recv, kf_send, kf_recv,
    u_stage, u_back, ks_stage, ks_back, kf_stage, kf_back,
    m_own, m_recv, m_far, w_far, far_send, far_recv, w_recv, pre0_send, pre0_recv, pre_send, pre_recv, ret_send, ret_recv,
    d_send, d_recv, r_send, r_recv,
    b_send, b_recv, q_send, q_recv, g_send, g_recv, f_send, f_recv, corr_st, h_send, h_recv,
    in_sem, out_sem, a2a_send_sem, a2a_recv_sem, m_send_sem, m_recv_sem, own_sem, w_sem, pre0_sem,
    pre_send_sem, pre_recv_sem, ret_send_sem, ret_recv_sem, d_sem, r_sem, b_sem,
    q_send_sem, q_recv_sem, g_sem, f_send_sem, f_recv_sem,
    h_send_sem, h_recv_sem, far_sem, wf_sem, wy_send_sem, wy_recv_sem, fr_send_sem, fr_recv_sem,
):
    dp = lax.axis_index("dp")
    me = lax.axis_index("seq")
    ch = lax.axis_index("chan")
    other = 1 - ch
    plane = n // 2
    zl, spot = lax.div(me, plane), lax.rem(me, plane)
    group = m_far.shape[0]
    nx = group // 2
    ny = plane // nx
    y, x = lax.div(spot, nx), lax.rem(spot, nx)
    g = zl * nx + x
    far_cols = m_far.shape[2]

    def member(k):
        return lax.div(k, nx) * plane + y * nx + lax.rem(k, nx)

    width = w_ref.shape[0]
    cols = w_ref.shape[1] // 2
    half = cot_ref.shape[1]
    piece = LANES // SUB
    n_own = b_send.shape[1] // LANES
    extras = n_own - n // 2
    rows = t1_ref.shape[0] // 2
    a_chunks = -(-width // LANES)

    pairs = (
        (signal_hbm, signal_ref), (filt_hbm, filt_ref), (cot_hbm, cot_ref), (up_hbm, up_ref),
        (w_hbm, w_ref), (t1_hbm, t1_ref), (t2_hbm, t2_ref), (t2b_hbm, t2b_ref), (t1b_hbm, t1b_ref),
        (tc_hbm, tc_ref), (ts_hbm, ts_ref), (gating_hbm, gating_ref), (down_hbm, down_ref),
        (skip_hbm, skip_ref),
    )
    loads = [pltpu.make_async_copy(s, d, in_sem.at[i]) for i, (s, d) in enumerate(pairs)]
    for load in loads:
        load.start()

    barrier = pltpu.get_barrier_semaphore()
    for d in range(4):
        for z in range(2):
            for c in range(2):
                if d or c:
                    pl.semaphore_signal(
                        barrier, inc=1,
                        device_id=(lax.rem(dp + d, 4), lax.rem(zl + z, 2) * plane + spot, lax.rem(ch + c, 2)),
                        device_id_type=MESH,
                    )

    def greet(d, _):
        pl.semaphore_signal(
            barrier, inc=1, device_id=(dp, lax.rem(me + d, n), ch), device_id_type=MESH
        )
        return 0

    lax.fori_loop(1, n, greet, 0, unroll=9 if n == 64 else 1)
    for z in range(2):
        for k in range(1, nx):
            pl.semaphore_signal(
                barrier, inc=1, device_id=(dp, member(z * nx + lax.rem(x + k, nx)), other),
                device_id_type=MESH,
            )

    loads[0].wait()
    loads[1].wait()
    sig_t[...] = signal_ref[...].astype(F32).T
    filt_t = filt_ref[...].T
    for cc in range(PER):
        sf_send[pl.ds(cc, n, stride=8), :] = sig_t[cc * n:(cc + 1) * n, :]
        sf_send[pl.ds(PER + cc, n, stride=8), :] = filt_t[cc * n:(cc + 1) * n, :]
    real_length = length_ref[0]
    live_col = (me * LANES + lax.broadcasted_iota(jnp.int32, (LANES, 1), 0) < real_length).astype(F32)
    live_row = (me * LANES + lax.broadcasted_iota(jnp.int32, (1, LANES), 1) < real_length).astype(F32)
    pick1 = index_ref[0].astype(F32)
    pick0 = 1.0 - pick1

    pl.semaphore_wait(barrier, n - 1 + 14 + 2 * (nx - 1))

    def a2a_start(k, src, dst, at):
        def body(d, _):
            j = lax.rem(me + d, n)
            pltpu.make_async_remote_copy(
                src_ref=src.at[at(j)],
                dst_ref=dst.at[at(me)],
                send_sem=a2a_send_sem.at[k],
                recv_sem=a2a_recv_sem.at[k],
                device_id=(dp, j, ch),
                device_id_type=MESH,
            ).start()
            return 0

        lax.fori_loop(1, n, body, 0, unroll=9 if n == 64 else 1)
        pltpu.make_async_copy(src.at[at(me)], dst.at[at(me)], a2a_recv_sem.at[k]).start()

    def a2a_wait(k, dst):
        pltpu.make_async_copy(dst, dst, a2a_recv_sem.at[k]).wait()

    def a2a_wait_send(k, src, size):
        part = src.at[pl.ds(0, (n - 1) * size)]
        pltpu.make_async_copy(part, part, a2a_send_sem.at[k]).wait()

    def eight(j):
        return pl.ds(pl.multiple_of(j * 8, 8), 8)

    def block(j):
        return j

    a2a_start(0, sf_send, sf_recv, eight)

    def cot_copy(sub, qq, hh):
        q = 2 * ch + qq
        return pltpu.make_async_remote_copy(
            src_ref=cot_hbm.at[pl.ds(sub * piece, piece), pl.ds((2 * qq + hh) * cols, cols)],
            dst_ref=m_recv.at[sub, zl],
            send_sem=m_send_sem.at[sub, 2 * qq + hh],
            recv_sem=m_recv_sem.at[sub],
            device_id=(q, lax.div(lax.rem(q - dp + 4, 4), 3) * plane + spot, hh),
            device_id_type=MESH,
        )

    def own_copy(qq, hh):
        return pltpu.make_async_remote_copy(
            src_ref=cot_hbm.at[:, pl.ds((2 * qq + hh) * cols, cols)],
            dst_ref=m_own,
            send_sem=own_sem.at[0],
            recv_sem=own_sem.at[1],
            device_id=(dp, me, hh),
            device_id_type=MESH,
        )

    def to_other(qq):
        return lax.rem(2 * ch + qq - dp + 4, 2) == 1

    for sub in range(SUB):
        for qq in range(2):
            for hh in range(2):
                @pl.when(to_other(qq))
                def _():
                    cot_copy(sub, qq, hh).start()
    for qq in range(2):
        for hh in range(2):
            @pl.when((2 * ch + qq == dp) & (ch != hh))
            def _():
                own_copy(qq, hh).start()

            @pl.when((2 * ch + qq == dp) & (ch == hh))
            def _():
                pltpu.make_async_copy(
                    cot_hbm.at[:, pl.ds((2 * qq + hh) * cols, cols)], m_own, own_sem.at[1]
                ).start()

    far = lax.rem(dp + 2, 4)
    slice_rows = width // ny
    my_slice = pl.ds(pl.multiple_of(y * slice_rows, slice_rows), slice_rows)

    wf_copy = pltpu.make_async_remote_copy(
        src_ref=w_hbm.at[my_slice, pl.ds(pl.multiple_of(g * far_cols, far_cols), far_cols)],
        dst_ref=w_far.at[my_slice, :],
        send_sem=wf_sem.at[0], recv_sem=wf_sem.at[1], device_id=(far, me, ch), device_id_type=MESH,
    )
    wf_copy.start()

    def far_copy(d, c):
        k = lax.rem(g + d, group)
        at = lax.rem(far, 2) * 2 * cols + k * far_cols
        src = cot_hbm.at[:, pl.ds(pl.multiple_of(at, far_cols), far_cols)]
        if d == 0 and c == 0:
            return pltpu.make_async_copy(src, m_far.at[d], far_sem.at[1])
        return pltpu.make_async_remote_copy(
            src_ref=src, dst_ref=m_far.at[d], send_sem=far_sem.at[0], recv_sem=far_sem.at[1],
            device_id=(dp, member(k), lax.rem(ch + c, 2)), device_id_type=MESH,
        )

    holds_far = ch == lax.div(far, 2)

    @pl.when(holds_far)
    def _():
        for d in range(group):
            for c in range(2):
                far_copy(d, c).start()

    def to_chan(src, dst, send_sem, recv_sem):
        return pltpu.make_async_remote_copy(
            src_ref=src, dst_ref=dst, send_sem=send_sem, recv_sem=recv_sem,
            device_id=(dp, me, other), device_id_type=MESH,
        )

    w_copy = to_chan(
        w_hbm.at[:, pl.ds(pl.multiple_of(other * cols, LANES), cols)], w_recv, w_sem.at[0], w_sem.at[1]
    )
    w_copy.start()

    wf_copy.wait_recv()
    wy_copies = []
    for k in range(1, ny):
        copy = pltpu.make_async_remote_copy(
            src_ref=w_far.at[my_slice, :], dst_ref=w_far.at[my_slice, :],
            send_sem=wy_send_sem.at[k], recv_sem=wy_recv_sem,
            device_id=(dp, zl * plane + lax.rem(y + k, ny) * nx + x, ch), device_id_type=MESH,
        )
        copy.start()
        wy_copies.append(copy)

    for load in loads[2:]:
        load.wait()
    masked[...] = (cot_ref[...].astype(F32) * live_col).astype(BF)
    up_sel = (up_ref[0].astype(F32) * pick0 + up_ref[1].astype(F32) * pick1).astype(BF)
    down_sel = (down_ref[0].astype(F32) * pick0 + down_ref[1].astype(F32) * pick1).astype(BF)
    max_rank = up_sel.shape[0]
    keep = (lax.broadcasted_iota(jnp.int32, (max_rank, LANES), 0) < rank_ref[0]).astype(F32)
    d_send[...] = dot_t(up_sel, masked[...])
    d_copy = to_chan(d_send, d_recv, d_sem.at[0], d_sem.at[1])
    d_copy.start()
    gate_t[...] = gating_ref[...].astype(F32).T
    skip_t = jnp.broadcast_to(skip_ref[...], (LANES, width)).T

    own_cols = pl.ds(pl.multiple_of(ch * cols, LANES), cols)
    pltpu.make_async_copy(m_own, m_own, own_sem.at[1]).wait()
    w_copy.wait_recv()
    pre0_send[...] = dot_t(m_own[...], w_recv[...]).astype(BF)
    pre0_copy = to_chan(pre0_send, pre0_recv, pre0_sem.at[0], pre0_sem.at[1])
    pre0_copy.start()
    own_part = dot_t(m_own[...], w_ref[:, own_cols])

    pre_copies, ret_copies = [], []

    def project(sub):
        pltpu.make_async_copy(m_recv.at[sub], m_recv.at[sub], m_recv_sem.at[sub]).wait()
        part = m_recv[sub].reshape(2 * piece, cols)
        pre_send[sub] = dot_t(part, w_recv[...]).astype(BF)
        copy = to_chan(pre_send.at[sub], pre_recv.at[sub], pre_send_sem.at[sub], pre_recv_sem.at[sub])
        copy.start()
        pre_copies.append(copy)
        return dot_t(part, w_ref[:, own_cols])

    def give_back(sub, mine):
        pre_copies[sub].wait_recv()
        ret_send[sub] = (mine + pre_recv[sub].astype(F32)).astype(BF)
        for slot in range(2):
            copy = pltpu.make_async_remote_copy(
                src_ref=ret_send.at[sub, pl.ds(slot * piece, piece)],
                dst_ref=ret_recv.at[zl, pl.ds(sub * piece, piece)],
                send_sem=ret_send_sem.at[sub, slot], recv_sem=ret_recv_sem,
                device_id=(lax.rem(dp + 3 - 2 * zl, 4), slot * plane + spot, ch), device_id_type=MESH,
            )
            copy.start()
            ret_copies.append(copy)

    tc, ts = tc_ref[...], ts_ref[...]

    def forward(load, store):
        x = jnp.concatenate([load(cc) for cc in range(PER)], axis=1)
        y = dot(t1_ref[...], split_data(x, 0))
        parts = []
        for cc in range(PER):
            re = y[:rows, cc * LANES:(cc + 1) * LANES]
            im = y[rows:, cc * LANES:(cc + 1) * LANES]
            parts.append(jnp.concatenate([re * tc + im * ts, im * tc - re * ts], axis=1))
        store[...] = dot(split_data(jnp.concatenate(parts, axis=0), 1), t2_ref[...])

    def inverse(re, im):
        q = dot(split_data(jnp.concatenate([re, im], axis=1), 1), t2b_ref[...])
        parts = []
        for cc in range(PER):
            qr = q[cc * rows:(cc + 1) * rows, :LANES]
            qi = q[cc * rows:(cc + 1) * rows, LANES:]
            parts.append(jnp.concatenate([qr * tc - qi * ts, qi * tc + qr * ts], axis=0))
        return dot(t1b_ref[...], split_data(jnp.concatenate(parts, axis=1), 0))

    def spread_channels(dst, values):
        for cc in range(PER):
            dst[:, cc, :] = values[:, cc * LANES:(cc + 1) * LANES]

    def gather_channels(src):
        return jnp.concatenate([src[:, cc, :] for cc in range(PER)], axis=0)

    a2a_wait(0, sf_recv)
    forward(lambda cc: sf_recv[pl.ds(cc, n, stride=8), :], spec_s)
    forward(lambda cc: sf_recv[pl.ds(PER + cc, n, stride=8), :], spec_f)
    s_re, s_im = spec_s[:, :LANES], spec_s[:, LANES:]
    f_re, f_im = spec_f[:, :LANES], spec_f[:, LANES:]
    spread_channels(c_send, inverse(s_re * f_re - s_im * f_im, s_re * f_im + s_im * f_re))
    a2a_start(1, c_send, c_recv, block)

    d_copy.wait()
    back_rank = (2.0 * (d_send[...] + d_recv[...]) * keep).astype(BF)

    pltpu.make_async_copy(m_far, m_far, far_sem.at[1]).wait()
    if ny > 1:
        rest = w_far.at[pl.ds(0, (ny - 1) * slice_rows), :]
        pltpu.make_async_copy(rest, rest, wy_recv_sem).wait()
    far_part = dot_t(m_far[...].reshape(group * LANES, far_cols), w_far[...])
    far_send[...] = far_part[LANES:].astype(BF)
    own_part = own_part + far_part[:LANES]
    far_copies = []
    for d in range(1, group):
        copy = pltpu.make_async_remote_copy(
            src_ref=far_send.at[pl.ds((d - 1) * LANES, LANES), :], dst_ref=far_recv.at[d - 1],
            send_sem=fr_send_sem.at[d], recv_sem=fr_recv_sem,
            device_id=(dp, member(lax.rem(g + group - d, group)), ch), device_id_type=MESH,
        )
        copy.start()
        far_copies.append(copy)

    mine = project(0)
    for sub in range(1, SUB):
        after = project(sub)
        give_back(sub - 1, mine)
        mine = after
    give_back(SUB - 1, mine)

    a2a_wait(1, c_recv)
    inner_t = gather_channels(c_recv) + skip_t * sig_t[...]
    gated_t = (gate_t[...] * inner_t).astype(BF)
    r_send[...] = dot(down_sel, gated_t)
    r_copy = to_chan(r_send, r_recv, r_sem.at[0], r_sem.at[1])
    r_copy.start()
    b_send[:, half:half + width] = dot_t(back_rank, gated_t).astype(BF)

    grad_y = own_part + received(pre0_copy, pre0_recv)
    pltpu.make_async_copy(ret_recv, ret_recv, ret_recv_sem).wait()
    pltpu.make_async_copy(far_recv, far_recv, fr_recv_sem).wait()
    for k in range(2):
        grad_y = grad_y + ret_recv[k].astype(F32)
    for k in range(group - 1):
        grad_y = grad_y + far_recv[k].astype(F32)
    grad_y = grad_y.T * live_row + dot_0(down_sel, back_rank)
    grad_u = grad_y * gate_t[...]
    gradu_t[...] = grad_u
    for cc in range(PER):
        u_stage[:, cc, :] = gradu_t[cc * n:(cc + 1) * n, :]
    u_send[...] = u_stage[...].astype(BF)
    a2a_start(2, u_send, u_recv, block)
    r_copy.wait()
    fwd_rank = (2.0 * (r_send[...] + r_recv[...]) * keep).astype(BF)
    b_send[:, :half] = dot(fwd_rank, masked[...]).astype(BF)

    product = grad_u * sig_t[...]
    high = product.astype(BF)
    low = (product - high.astype(F32)).astype(BF)
    ones = jnp.ones((max_rank, LANES), BF)
    at = half + a_chunks * LANES
    b_send[:, at:at + width] = (dot_t(ones, high) + dot_t(ones, low)).astype(BF)

    def share(p, owner):
        src = b_send.at[:, pl.ds(pl.multiple_of(p * LANES, LANES), LANES)]
        dst = b_recv.at[pl.ds(pl.multiple_of(me * 16, 16), 16), :]

        @pl.when(owner != me)
        def _():
            pltpu.make_async_remote_copy(
                src_ref=src, dst_ref=dst, send_sem=b_sem.at[0], recv_sem=b_sem.at[1],
                device_id=(dp, owner, ch), device_id_type=MESH,
            ).start()

        @pl.when(owner == me)
        def _():
            pltpu.make_async_copy(src, dst, b_sem.at[1]).start()

    def share_main(d, _):
        p = lax.rem(me + d, plane)
        share(p, p)
        return 0

    for k in range(extras):
        share(plane + k, plane + (k % ny) * nx + k // ny)
    lax.fori_loop(0, plane, share_main, 0, unroll=4 if n == 64 else 1)

    ggat_ref[...] = (grad_y * inner_t).T.astype(BF)
    outs = [
        pltpu.make_async_copy(s, d, out_sem.at[i])
        for i, (s, d) in enumerate((
            (ggat_ref, ggat_hbm), (gsig_ref, gsig_hbm), (gfilt_ref, gfilt_hbm), (g_recv, gbank_hbm),
        ))
    ]
    outs[0].start()

    a2a_wait(2, u_recv)
    u_back[...] = u_recv[...].astype(F32)
    forward(lambda cc: u_back[:, cc, :], spec_g)
    g_re, g_im = spec_g[:, :LANES], spec_g[:, LANES:]
    s_re, s_im = spec_s[:, :LANES], spec_s[:, LANES:]
    spread_channels(ks_stage, inverse(g_re * s_re + g_im * s_im, g_im * s_re - g_re * s_im))
    ks_send[...] = ks_stage[...].astype(BF)
    a2a_start(3, ks_send, ks_recv, block)
    f_re, f_im = spec_f[:, :LANES], spec_f[:, LANES:]
    spread_channels(kf_stage, inverse(g_re * f_re + g_im * f_im, g_im * f_re - g_re * f_im))
    kf_send[...] = kf_stage[...].astype(BF)
    a2a_start(4, kf_send, kf_recv, block)

    column = zl * plane + x * ny
    is_owner = column + y < n_own

    def q_copy(step):
        return pltpu.make_async_remote_copy(
            src_ref=q_send, dst_ref=q_recv.at[step - 1], send_sem=q_send_sem.at[step],
            recv_sem=q_recv_sem, device_id=(lax.rem(dp + step, 4), me, ch), device_id_type=MESH,
        )

    @pl.when(is_owner)
    def _():
        pltpu.make_async_copy(b_recv, b_recv, b_sem.at[1]).wait()
        acc = b_recv[0:16, :].astype(F32)
        for i in range(1, n):
            acc = acc + b_recv[16 * i:16 * (i + 1), :].astype(F32)
        q_send[...] = jnp.concatenate([acc * pick0, acc * pick1], axis=0)
        for step in (1, 3, 2):
            q_copy(step).start()

    a2a_wait(3, ks_recv)
    quarter = width // 4
    ks_back[...] = ks_recv[...].astype(F32)
    corr_st[...] = gather_channels(ks_back)
    f_send[...] = corr_st[...].astype(BF)
    f_copies = []
    for step in (1, 3, 2):
        q = lax.rem(dp + step, 4)
        copy = pltpu.make_async_remote_copy(
            src_ref=f_send.at[pl.ds(pl.multiple_of(q * quarter, quarter), quarter), :],
            dst_ref=f_recv.at[step - 1], send_sem=f_send_sem.at[step], recv_sem=f_recv_sem,
            device_id=(q, me, ch), device_id_type=MESH,
        )
        copy.start()
        f_copies.append(copy)

    g_size = 2 * max_rank
    bank_rows = pl.ds(pl.multiple_of((column + y) * g_size, g_size), g_size)

    @pl.when(is_owner)
    def _():
        pltpu.make_async_copy(q_recv, q_recv, q_recv_sem).wait()
        g_send[...] = (q_send[...] + q_recv[0] + q_recv[1] + q_recv[2]).astype(BF)
        for k in range(1, ny):
            pltpu.make_async_remote_copy(
                src_ref=g_send, dst_ref=g_recv.at[bank_rows, :], send_sem=g_sem.at[0], recv_sem=g_sem.at[1],
                device_id=(dp, zl * plane + lax.rem(y + k, ny) * nx + x, ch), device_id_type=MESH,
            ).start()
        pltpu.make_async_copy(g_send, g_recv.at[bank_rows, :], g_sem.at[1]).start()

    a2a_wait(4, kf_recv)
    kf_back[...] = kf_recv[...].astype(F32)
    gsig_ref[...] = (gather_channels(kf_back) + skip_t * gradu_t[...]).T.astype(BF)
    outs[1].start()

    pltpu.make_async_copy(f_recv, f_recv, f_recv_sem).wait()
    my_quarter = pl.ds(pl.multiple_of(dp * quarter, quarter), quarter)
    sums = corr_st[my_quarter, :]
    for k in range(3):
        sums = sums + f_recv[k].astype(F32)
    h_send[...] = sums.astype(BF)
    h_copies = []
    for step in (1, 3, 2):
        copy = pltpu.make_async_remote_copy(
            src_ref=h_send, dst_ref=h_recv.at[my_quarter, :], send_sem=h_send_sem.at[step],
            recv_sem=h_recv_sem, device_id=(lax.rem(dp + step, 4), me, ch), device_id_type=MESH,
        )
        copy.start()
        h_copies.append(copy)
    pltpu.make_async_copy(h_send, h_recv.at[my_quarter, :], h_recv_sem).start()

    columns = [(zl == 0, ny)] + [
        ((zl == 1) & (x == k), max(0, min(ny, extras - k * ny))) for k in range(nx)
    ]

    def block_copy(k, count):
        rows_of = pl.ds(pl.multiple_of(column * g_size, g_size), count * g_size)
        return pltpu.make_async_remote_copy(
            src_ref=g_recv.at[rows_of, :], dst_ref=g_recv.at[rows_of, :],
            send_sem=g_sem.at[2], recv_sem=g_sem.at[3],
            device_id=(dp, member(lax.rem(g + k, group)), ch), device_id_type=MESH,
        )

    for here, count in columns:
        if count:
            @pl.when(here)
            def _():
                part = g_recv.at[pl.ds(0, count * g_size), :]
                pltpu.make_async_copy(part, part, g_sem.at[1]).wait()
                for k in range(1, group):
                    block_copy(k, count).start()

    pltpu.make_async_copy(h_recv, h_recv, h_recv_sem).wait()
    gfilt_ref[...] = h_recv[...].astype(F32).T
    outs[2].start()

    for here, count in columns:
        @pl.when(here)
        def _():
            part = g_recv.at[pl.ds(0, (n_own - count) * g_size), :]
            pltpu.make_async_copy(part, part, g_sem.at[3]).wait()
    outs[3].start()

    for sub in range(SUB):
        for qq in range(2):
            for hh in range(2):
                @pl.when(to_other(qq))
                def _():
                    cot_copy(sub, qq, hh).wait_send()
    for qq in range(2):
        for hh in range(2):
            @pl.when((2 * ch + qq == dp) & (ch != hh))
            def _():
                own_copy(qq, hh).wait_send()
    a2a_wait_send(0, sf_send, 8)
    for k, src in ((1, c_send), (2, u_send), (3, ks_send), (4, kf_send)):
        a2a_wait_send(k, src, 1)
    w_copy.wait_send()
    pre0_copy.wait_send()
    wf_copy.wait_send()
    for copy in wy_copies + far_copies + pre_copies + ret_copies + f_copies + h_copies:
        copy.wait_send()

    @pl.when(holds_far)
    def _():
        def sent(d, _):
            pltpu.make_async_copy(m_far.at[0], m_far.at[0], far_sem.at[0]).wait()
            return 0

        lax.fori_loop(1, 2 * group, sent, 0)

    def b_sent(count):
        part = b_send.at[:, pl.ds(0, count * LANES)]
        pltpu.make_async_copy(part, part, b_sem.at[0]).wait()

    @pl.when(is_owner)
    def _():
        b_sent(n_own - 1)
        for step in (1, 3, 2):
            q_copy(step).wait_send()
        for _ in range(1, ny):
            pltpu.make_async_copy(g_send, g_send, g_sem.at[0]).wait()

    @pl.when(jnp.logical_not(is_owner))
    def _():
        b_sent(n_own)

    for here, count in columns:
        if count:
            @pl.when(here)
            def _():
                for k in range(1, group):
                    block_copy(k, count).wait_send()

    for out in outs:
        out.wait()


def received(copy, ref):
    copy.wait_recv()
    return ref[...].astype(F32)


def finish_kernel(
    ny,
    gsig_in, ggat_in, gfilt_in, gbank_in,
    gsig_out, ggat_out, gfilt_out, gskip_out, ga_out, gb_out,
    gsig_ref, ggat_ref, gfilt_ref, gbank_ref, gskip_ref, ga_ref, gb_ref, in_sem, out_sem,
):
    max_rank, half = gb_ref.shape[1:]
    width = ga_ref.shape[2]
    g_size = 2 * max_rank
    up_chunks = half // LANES
    nx = up_chunks // ny
    a_chunks = -(-width // LANES)
    pairs = ((gbank_in, gbank_ref), (gfilt_in, gfilt_ref), (gsig_in, gsig_ref), (ggat_in, ggat_ref))
    loads = [pltpu.make_async_copy(s, d, in_sem.at[i]) for i, (s, d) in enumerate(pairs)]
    for load in loads:
        load.start()
    pairs = (
        (gb_ref, gb_out), (gfilt_ref, gfilt_out), (gsig_ref, gsig_out), (ggat_ref, ggat_out),
        (gskip_ref, gskip_out), (ga_ref, ga_out),
    )
    stores = [pltpu.make_async_copy(s, d, out_sem.at[i]) for i, (s, d) in enumerate(pairs)]
    loads[0].wait()
    for p in range(up_chunks):
        at = ((p % nx) * ny + p // nx) * g_size
        block = gbank_ref[at:at + g_size, :].astype(F32)
        gb_ref[0, :, p * LANES:(p + 1) * LANES] = block[:max_rank]
        gb_ref[1, :, p * LANES:(p + 1) * LANES] = block[max_rank:]
    stores[0].start()
    for k in range(1, 4):
        loads[k].wait()
        stores[k].start()
    size = min(LANES, width)
    for k in range(a_chunks):
        at = (up_chunks + k) * g_size
        block = gbank_ref[at:at + g_size, :].astype(F32)
        ga_ref[0, :, k * size:(k + 1) * size] = block[:max_rank, :size]
        ga_ref[1, :, k * size:(k + 1) * size] = block[max_rank:, :size]
        at = (up_chunks + a_chunks + k) * g_size
        block = gbank_ref[at:at + g_size, :].astype(F32)
        gskip_ref[:, k * size:(k + 1) * size] = (block[0:1] + block[max_rank:max_rank + 1])[:, :size]
    stores[4].start()
    stores[5].start()
    for store in stores:
        store.wait()


def local(
    signal, gating, cotangent, filt, skip, output_projection,
    adapter_down_bank, adapter_up_bank, adapter_index, sequence_rank, real_length,
):
    n = lax.axis_size("seq")
    width = signal.shape[2]
    half = cotangent.shape[2]
    cols = output_projection.shape[1] // 2
    max_rank = adapter_up_bank.shape[1]
    a_chunks = -(-width // LANES)
    n_own = half // LANES + 2 * a_chunks
    piece = LANES // SUB
    group = 2 * min(4, n // 2)
    far_cols = 2 * cols // group
    consts = [jnp.asarray(t) for t in tables(n)]
    rows = consts[4].shape[0]
    vmem = pl.BlockSpec(memory_space=pltpu.VMEM)
    smem = pl.BlockSpec(memory_space=pltpu.SMEM)
    hbm = pl.BlockSpec(memory_space=pltpu.HBM)
    dma = pltpu.SemaphoreType.DMA
    arrays = [
        signal[0], gating[0], cotangent[0], filt, skip[None], output_projection,
        jnp.swapaxes(adapter_down_bank, 1, 2), adapter_up_bank, *consts,
    ]
    block = pltpu.VMEM((n, PER, LANES), F32)
    narrow = pltpu.VMEM((n, PER, LANES), BF)
    eight = pltpu.VMEM((8 * n, LANES), F32)
    wide = pltpu.VMEM((width, LANES), F32)
    spec = pltpu.VMEM((PER * rows, 2 * LANES), F32)
    rank = pltpu.VMEM((max_rank, LANES), F32)
    outs = pl.pallas_call(
        functools.partial(kernel, n),
        out_shape=(
            jax.ShapeDtypeStruct((LANES, width), BF),
            jax.ShapeDtypeStruct((LANES, width), BF),
            jax.ShapeDtypeStruct((LANES, width), F32),
            jax.ShapeDtypeStruct((2 * max_rank * n_own, LANES), BF),
        ),
        in_specs=[smem] * 3 + [hbm] * len(arrays),
        out_specs=(hbm,) * 4,
        scratch_shapes=[
            pltpu.VMEM((LANES, width), BF),
            pltpu.VMEM((LANES, width), BF),
            pltpu.VMEM((LANES, width), F32),
        ] + [pltpu.VMEM(a.shape, a.dtype) for a in arrays] + [
            pltpu.VMEM((LANES, half), BF),
            wide, wide, wide, spec, spec, spec,
            eight, eight, block, block, narrow, narrow, narrow, narrow, narrow, narrow,
            block, block, block, block, block, block,
            pltpu.VMEM((LANES, cols), BF),
            pltpu.VMEM((SUB, 2, piece, cols), BF),
            pltpu.VMEM((group, LANES, far_cols), BF),
            pltpu.VMEM((width, far_cols), BF),
            pltpu.VMEM(((group - 1) * LANES, width), BF),
            pltpu.VMEM((group - 1, LANES, width), BF),
            pltpu.VMEM((width, cols), BF),
            pltpu.VMEM((LANES, width), BF),
            pltpu.VMEM((LANES, width), BF),
            pltpu.VMEM((SUB, 2 * piece, width), BF),
            pltpu.VMEM((SUB, 2 * piece, width), BF),
            pltpu.VMEM((SUB, 2 * piece, width), BF),
            pltpu.VMEM((2, LANES, width), BF),
            rank, rank, rank, rank,
            pltpu.VMEM((max_rank, n_own * LANES), BF),
            pltpu.VMEM((16 * n, LANES), BF),
            pltpu.VMEM((2 * max_rank, LANES), F32),
            pltpu.VMEM((3, 2 * max_rank, LANES), F32),
            pltpu.VMEM((2 * max_rank, LANES), BF),
            pltpu.VMEM((2 * max_rank * n_own, LANES), BF),
            pltpu.VMEM((width, LANES), BF),
            pltpu.VMEM((3, width // 4, LANES), BF),
            wide,
            pltpu.VMEM((width // 4, LANES), BF),
            pltpu.VMEM((width, LANES), BF),
            dma((len(arrays),)), dma((4,)), dma((5,)), dma((5,)), dma((SUB, 4)), dma((SUB,)), dma((2,)), dma((2,)),
            dma((2,)), dma((SUB,)), dma((SUB,)), dma((SUB, 4)), dma, dma((2,)), dma((2,)), dma((2,)),
            dma((4,)), dma, dma((4,)), dma((4,)), dma,
            dma((4,)), dma, dma((2,)), dma((2,)), dma((8,)), dma, dma((group,)), dma,
        ],
        compiler_params=pltpu.CompilerParams(
            collective_id=0, has_side_effects=True, vmem_limit_bytes=VMEM_LIMIT
        ),
    )(adapter_index, sequence_rank, real_length, *arrays)
    grad_signal, grad_gating, grad_filt, grad_skip, grad_a, grad_b = pl.pallas_call(
        functools.partial(finish_kernel, n // group),
        out_shape=(
            jax.ShapeDtypeStruct((LANES, width), BF),
            jax.ShapeDtypeStruct((LANES, width), BF),
            jax.ShapeDtypeStruct((LANES, width), F32),
            jax.ShapeDtypeStruct((1, width), F32),
            jax.ShapeDtypeStruct((2, max_rank, width), F32),
            jax.ShapeDtypeStruct((2, max_rank, half), F32),
        ),
        in_specs=[hbm] * 4,
        out_specs=(hbm,) * 6,
        scratch_shapes=[
            pltpu.VMEM((LANES, width), BF), pltpu.VMEM((LANES, width), BF), pltpu.VMEM((LANES, width), F32),
            pltpu.VMEM((2 * max_rank * n_own, LANES), BF), pltpu.VMEM((1, width), F32),
            pltpu.VMEM((2, max_rank, width), F32), pltpu.VMEM((2, max_rank, half), F32),
            dma((4,)), dma((6,)),
        ],
        compiler_params=pltpu.CompilerParams(vmem_limit_bytes=VMEM_LIMIT),
    )(*outs)
    return (grad_signal[None], grad_gating[None], grad_filt, grad_skip[0], jnp.swapaxes(grad_a, 1, 2), grad_b)


def solution(mesh):
    placed = (
        P("dp", "seq", "chan"), P("dp", "seq", "chan"), P("dp", "seq", "chan"), P("seq", "chan"),
        P("chan"), P("chan", "dp"), P(None, "chan", None), P(None, None, "chan"),
        P("dp"), P("dp"), P("dp"),
    )
    return jax.shard_map(
        local,
        mesh=mesh,
        in_specs=placed,
        out_specs=(
            P("dp", "seq", "chan"), P("dp", "seq", "chan"), P("seq", "chan"), P("chan"),
            P(None, "chan", None), P(None, None, "chan"),
        ),
        check_vma=False,
    )
```

```python
import functools
import math

import jax
import jax.numpy as jnp
import ml_dtypes
import numpy as np
from jax import lax
from jax.experimental import pallas as pl
from jax.experimental.pallas import tpu as pltpu
from jax.sharding import PartitionSpec as P

MESH = pl.DeviceIdType.MESH
BF = jnp.bfloat16
F32 = jnp.float32
LANES = 128
PER = 4
VMEM_LIMIT = 62 * 1024 * 1024
SUB = 2


def split3(table, axis, order):
    high = table.astype(ml_dtypes.bfloat16)
    low = (table - high.astype(np.float64)).astype(ml_dtypes.bfloat16)
    return np.concatenate([high if o else low for o in order], axis=axis)


def tables(n):
    rows = -(-(n + 1) // 8) * 8
    k1 = np.arange(rows)
    used = (k1 <= n).astype(np.float64)
    i = np.arange(n)
    a = np.arange(LANES)
    period = 2 * n * LANES
    th1 = 2 * math.pi * (k1[:, None] * i[None, :] % (2 * n)) / (2 * n)
    first = np.concatenate([np.cos(th1) * used[:, None], -np.sin(th1) * used[:, None]], 0)
    thw = 2 * math.pi * (k1[:, None] * a[None, :] % period) / period
    tw_cos, tw_sin = np.cos(thw), np.sin(thw)
    th2 = 2 * math.pi * (a[:, None] * a[None, :] % LANES) / LANES
    c2, s2 = np.cos(th2), np.sin(th2)
    second = np.block([[c2, -s2], [s2, c2]])
    second_back = np.block([[c2, s2], [-s2, c2]])
    weight = used * np.where((k1 == 0) | (k1 == n), 1.0, 2.0) / period
    last = np.concatenate([np.cos(th1).T * weight, -np.sin(th1).T * weight], 1)
    return (
        split3(first, 1, (1, 1, 0)),
        split3(second, 0, (1, 1, 0)),
        split3(second_back, 0, (1, 1, 0)),
        split3(last, 1, (1, 1, 0)),
        tw_cos.astype(np.float32),
        tw_sin.astype(np.float32),
    )


def split_data(x, axis):
    high = x.astype(BF)
    low = (x - high.astype(F32)).astype(BF)
    return jnp.concatenate([high, low, high], axis=axis)


def dot(a, b):
    return jnp.dot(a, b, preferred_element_type=F32)


def dot_t(a, b):
    return lax.dot_general(a, b, (((1,), (1,)), ((), ())), preferred_element_type=F32)


def dot_0(a, b):
    return lax.dot_general(a, b, (((0,), (0,)), ((), ())), preferred_element_type=F32)


def kernel(
    n,
    index_ref, rank_ref, length_ref,
    signal_hbm, gating_hbm, cot_hbm, filt_hbm, skip_hbm, w_hbm, down_hbm, up_hbm,
    t1_hbm, t2_hbm, t2b_hbm, t1b_hbm, tc_hbm, ts_hbm,
    gsig_hbm, ggat_hbm, gfilt_hbm, gbank_hbm,
    gsig_ref, ggat_ref, gfilt_ref,
    signal_ref, gating_ref, cot_ref, filt_ref, skip_ref, w_ref, down_ref, up_ref,
    t1_ref, t2_ref, t2b_ref, t1b_ref, tc_ref, ts_ref,
    masked, sig_t, gate_t, gradu_t, spec_s, spec_f, spec_g,
    sf_send, sf_recv, c_send, c_recv, u_send, u_recv, ks_send, ks_recv, kf_send, kf_recv,
    u_stage, u_back, ks_stage, ks_back, kf_stage, kf_back,
    m_own, m_recv, m_far, w_far, far_send, far_recv, w_recv, pre0_send, pre0_recv, pre_send, pre_recv, ret_send, ret_recv,
    d_send, d_recv, r_send, r_recv,
    b_send, b_recv, q_send, q_recv, g_send, g_recv, f_send, f_recv, corr_st, h_send, h_recv,
    in_sem, out_sem, a2a_send_sem, a2a_recv_sem, m_send_sem, m_recv_sem, own_sem, w_sem, pre0_sem,
    pre_send_sem, pre_recv_sem, ret_send_sem, ret_recv_sem, d_sem, r_sem, b_sem,
    q_send_sem, q_recv_sem, g_sem, f_send_sem, f_recv_sem,
    h_send_sem, h_recv_sem, far_sem, wf_sem, wy_send_sem, wy_recv_sem, fr_send_sem, fr_recv_sem,
):
    dp = lax.axis_index("dp")
    me = lax.axis_index("seq")
    ch = lax.axis_index("chan")
    other = 1 - ch
    plane = n // 2
    zl, spot = lax.div(me, plane), lax.rem(me, plane)
    nx = m_far.shape[0]
    group = 2 * nx
    ny = plane // nx
    y, x = lax.div(spot, nx), lax.rem(spot, nx)
    g = zl * nx + x
    far_cols = m_far.shape[2]

    def member(k):
        return lax.div(k, nx) * plane + y * nx + lax.rem(k, nx)

    width = w_ref.shape[0]
    cols = w_ref.shape[1] // 2
    half = cot_ref.shape[1]
    piece = LANES // SUB
    n_own = b_send.shape[1] // LANES
    extras = n_own - n // 2
    rows = t1_ref.shape[0] // 2
    a_chunks = -(-width // LANES)

    pairs = (
        (signal_hbm, signal_ref), (filt_hbm, filt_ref), (cot_hbm, cot_ref), (up_hbm, up_ref),
        (w_hbm, w_ref), (t1_hbm, t1_ref), (t2_hbm, t2_ref), (t2b_hbm, t2b_ref), (t1b_hbm, t1b_ref),
        (tc_hbm, tc_ref), (ts_hbm, ts_ref), (gating_hbm, gating_ref), (down_hbm, down_ref),
        (skip_hbm, skip_ref),
    )
    loads = [pltpu.make_async_copy(s, d, in_sem.at[i]) for i, (s, d) in enumerate(pairs)]
    for load in loads:
        load.start()

    barrier = pltpu.get_barrier_semaphore()
    for d in range(4):
        for z in range(2):
            for c in range(2):
                if d or c:
                    pl.semaphore_signal(
                        barrier, inc=1,
                        device_id=(lax.rem(dp + d, 4), lax.rem(zl + z, 2) * plane + spot, lax.rem(ch + c, 2)),
                        device_id_type=MESH,
                    )

    def greet(d, _):
        pl.semaphore_signal(
            barrier, inc=1, device_id=(dp, lax.rem(me + d, n), ch), device_id_type=MESH
        )
        return 0

    lax.fori_loop(1, n, greet, 0, unroll=9 if n == 64 else 1)
    for z in range(2):
        for k in range(1, nx):
            pl.semaphore_signal(
                barrier, inc=1, device_id=(dp, member(z * nx + lax.rem(x + k, nx)), other),
                device_id_type=MESH,
            )

    loads[0].wait()
    loads[1].wait()
    sig_t[...] = signal_ref[...].astype(F32).T
    filt_t = filt_ref[...].T
    for cc in range(PER):
        sf_send[pl.ds(cc, n, stride=8), :] = sig_t[cc * n:(cc + 1) * n, :]
        sf_send[pl.ds(PER + cc, n, stride=8), :] = filt_t[cc * n:(cc + 1) * n, :]
    real_length = length_ref[0]
    live_col = (me * LANES + lax.broadcasted_iota(jnp.int32, (LANES, 1), 0) < real_length).astype(F32)
    live_row = (me * LANES + lax.broadcasted_iota(jnp.int32, (1, LANES), 1) < real_length).astype(F32)
    pick1 = index_ref[0].astype(F32)
    pick0 = 1.0 - pick1

    pl.semaphore_wait(barrier, n - 1 + 14 + 2 * (nx - 1))

    def a2a_start(k, src, dst, at):
        def body(d, _):
            j = lax.rem(me + d, n)
            pltpu.make_async_remote_copy(
                src_ref=src.at[at(j)],
                dst_ref=dst.at[at(me)],
                send_sem=a2a_send_sem.at[k],
                recv_sem=a2a_recv_sem.at[k],
                device_id=(dp, j, ch),
                device_id_type=MESH,
            ).start()
            return 0

        lax.fori_loop(1, n, body, 0, unroll=9 if n == 64 else 1)
        pltpu.make_async_copy(src.at[at(me)], dst.at[at(me)], a2a_recv_sem.at[k]).start()

    def a2a_wait(k, dst):
        pltpu.make_async_copy(dst, dst, a2a_recv_sem.at[k]).wait()

    def a2a_wait_send(k, src, size):
        part = src.at[pl.ds(0, (n - 1) * size)]
        pltpu.make_async_copy(part, part, a2a_send_sem.at[k]).wait()

    def eight(j):
        return pl.ds(pl.multiple_of(j * 8, 8), 8)

    def block(j):
        return j

    a2a_start(0, sf_send, sf_recv, eight)

    def cot_copy(sub, qq, hh):
        q = 2 * ch + qq
        return pltpu.make_async_remote_copy(
            src_ref=cot_hbm.at[pl.ds(sub * piece, piece), pl.ds((2 * qq + hh) * cols, cols)],
            dst_ref=m_recv.at[sub, zl],
            send_sem=m_send_sem.at[sub, 2 * qq + hh],
            recv_sem=m_recv_sem.at[sub],
            device_id=(q, lax.div(lax.rem(q - dp + 4, 4), 3) * plane + spot, hh),
            device_id_type=MESH,
        )

    def own_copy(qq, hh):
        return pltpu.make_async_remote_copy(
            src_ref=cot_hbm.at[:, pl.ds((2 * qq + hh) * cols, cols)],
            dst_ref=m_own,
            send_sem=own_sem.at[0],
            recv_sem=own_sem.at[1],
            device_id=(dp, me, hh),
            device_id_type=MESH,
        )

    def to_other(qq):
        return lax.rem(2 * ch + qq - dp + 4, 2) == 1

    for sub in range(SUB):
        for qq in range(2):
            for hh in range(2):
                @pl.when(to_other(qq))
                def _():
                    cot_copy(sub, qq, hh).start()
    for qq in range(2):
        for hh in range(2):
            @pl.when((2 * ch + qq == dp) & (ch != hh))
            def _():
                own_copy(qq, hh).start()

            @pl.when((2 * ch + qq == dp) & (ch == hh))
            def _():
                pltpu.make_async_copy(
                    cot_hbm.at[:, pl.ds((2 * qq + hh) * cols, cols)], m_own, own_sem.at[1]
                ).start()

    far = lax.rem(dp + 2, 4)
    slice_rows = width // ny
    my_slice = pl.ds(pl.multiple_of(y * slice_rows, slice_rows), slice_rows)

    wf_copy = pltpu.make_async_remote_copy(
        src_ref=w_hbm.at[my_slice, pl.ds(pl.multiple_of(x * far_cols, far_cols), far_cols)],
        dst_ref=w_far.at[my_slice, :],
        send_sem=wf_sem.at[0], recv_sem=wf_sem.at[1], device_id=(far, me, ch), device_id_type=MESH,
    )
    wf_copy.start()

    def far_copy(d, c):
        k = lax.rem(x + d, nx)
        at = lax.rem(far, 2) * 2 * cols + k * far_cols
        src = cot_hbm.at[:, pl.ds(pl.multiple_of(at, far_cols), far_cols)]
        if d == 0 and c == 0:
            return pltpu.make_async_copy(src, m_far.at[d], far_sem.at[1])
        return pltpu.make_async_remote_copy(
            src_ref=src, dst_ref=m_far.at[d], send_sem=far_sem.at[0], recv_sem=far_sem.at[1],
            device_id=(dp, member(zl * nx + k), lax.rem(ch + c, 2)), device_id_type=MESH,
        )

    holds_far = ch == lax.div(far, 2)

    @pl.when(holds_far)
    def _():
        for d in range(nx):
            for c in range(2):
                far_copy(d, c).start()

    def to_chan(src, dst, send_sem, recv_sem):
        return pltpu.make_async_remote_copy(
            src_ref=src, dst_ref=dst, send_sem=send_sem, recv_sem=recv_sem,
            device_id=(dp, me, other), device_id_type=MESH,
        )

    w_copy = to_chan(
        w_hbm.at[:, pl.ds(pl.multiple_of(other * cols, LANES), cols)], w_recv, w_sem.at[0], w_sem.at[1]
    )
    w_copy.start()

    wf_copy.wait_recv()
    wy_copies = []
    for k in range(1, ny):
        copy = pltpu.make_async_remote_copy(
            src_ref=w_far.at[my_slice, :], dst_ref=w_far.at[my_slice, :],
            send_sem=wy_send_sem.at[k], recv_sem=wy_recv_sem,
            device_id=(dp, zl * plane + lax.rem(y + k, ny) * nx + x, ch), device_id_type=MESH,
        )
        copy.start()
        wy_copies.append(copy)

    for load in loads[2:]:
        load.wait()
    masked[...] = (cot_ref[...].astype(F32) * live_col).astype(BF)
    up_sel = (up_ref[0].astype(F32) * pick0 + up_ref[1].astype(F32) * pick1).astype(BF)
    down_sel = (down_ref[0].astype(F32) * pick0 + down_ref[1].astype(F32) * pick1).astype(BF)
    max_rank = up_sel.shape[0]
    keep = (lax.broadcasted_iota(jnp.int32, (max_rank, LANES), 0) < rank_ref[0]).astype(F32)
    d_send[...] = dot_t(up_sel, masked[...])
    d_copy = to_chan(d_send, d_recv, d_sem.at[0], d_sem.at[1])
    d_copy.start()
    gate_t[...] = gating_ref[...].astype(F32).T
    skip_t = jnp.broadcast_to(skip_ref[...], (LANES, width)).T

    own_cols = pl.ds(pl.multiple_of(ch * cols, LANES), cols)
    pltpu.make_async_copy(m_own, m_own, own_sem.at[1]).wait()
    w_copy.wait_recv()
    pre0_send[...] = dot_t(m_own[...], w_recv[...]).astype(BF)
    pre0_copy = to_chan(pre0_send, pre0_recv, pre0_sem.at[0], pre0_sem.at[1])
    pre0_copy.start()
    own_part = dot_t(m_own[...], w_ref[:, own_cols])

    pre_copies, ret_copies = [], []

    def project(sub):
        pltpu.make_async_copy(m_recv.at[sub], m_recv.at[sub], m_recv_sem.at[sub]).wait()
        part = m_recv[sub].reshape(2 * piece, cols)
        pre_send[sub] = dot_t(part, w_recv[...]).astype(BF)
        copy = to_chan(pre_send.at[sub], pre_recv.at[sub], pre_send_sem.at[sub], pre_recv_sem.at[sub])
        copy.start()
        pre_copies.append(copy)
        return dot_t(part, w_ref[:, own_cols])

    def give_back(sub, mine):
        pre_copies[sub].wait_recv()
        ret_send[sub] = (mine + pre_recv[sub].astype(F32)).astype(BF)
        for slot in range(2):
            copy = pltpu.make_async_remote_copy(
                src_ref=ret_send.at[sub, pl.ds(slot * piece, piece)],
                dst_ref=ret_recv.at[zl, pl.ds(sub * piece, piece)],
                send_sem=ret_send_sem.at[sub, slot], recv_sem=ret_recv_sem,
                device_id=(lax.rem(dp + 3 - 2 * zl, 4), slot * plane + spot, ch), device_id_type=MESH,
            )
            copy.start()
            ret_copies.append(copy)

    tc, ts = tc_ref[...], ts_ref[...]

    def forward(load, store):
        x = jnp.concatenate([load(cc) for cc in range(PER)], axis=1)
        y = dot(t1_ref[...], split_data(x, 0))
        parts = []
        for cc in range(PER):
            re = y[:rows, cc * LANES:(cc + 1) * LANES]
            im = y[rows:, cc * LANES:(cc + 1) * LANES]
            parts.append(jnp.concatenate([re * tc + im * ts, im * tc - re * ts], axis=1))
        store[...] = dot(split_data(jnp.concatenate(parts, axis=0), 1), t2_ref[...])

    def inverse(re, im):
        q = dot(split_data(jnp.concatenate([re, im], axis=1), 1), t2b_ref[...])
        parts = []
        for cc in range(PER):
            qr = q[cc * rows:(cc + 1) * rows, :LANES]
            qi = q[cc * rows:(cc + 1) * rows, LANES:]
            parts.append(jnp.concatenate([qr * tc - qi * ts, qi * tc + qr * ts], axis=0))
        return dot(t1b_ref[...], split_data(jnp.concatenate(parts, axis=1), 0))

    def spread_channels(dst, values):
        for cc in range(PER):
            dst[:, cc, :] = values[:, cc * LANES:(cc + 1) * LANES]

    def gather_channels(src):
        return jnp.concatenate([src[:, cc, :] for cc in range(PER)], axis=0)

    a2a_wait(0, sf_recv)
    forward(lambda cc: sf_recv[pl.ds(cc, n, stride=8), :], spec_s)
    forward(lambda cc: sf_recv[pl.ds(PER + cc, n, stride=8), :], spec_f)
    s_re, s_im = spec_s[:, :LANES], spec_s[:, LANES:]
    f_re, f_im = spec_f[:, :LANES], spec_f[:, LANES:]
    spread_channels(c_send, inverse(s_re * f_re - s_im * f_im, s_re * f_im + s_im * f_re))
    a2a_start(1, c_send, c_recv, block)

    d_copy.wait()
    back_rank = (2.0 * (d_send[...] + d_recv[...]) * keep).astype(BF)

    pltpu.make_async_copy(m_far, m_far, far_sem.at[1]).wait()
    if ny > 1:
        rest = w_far.at[pl.ds(0, (ny - 1) * slice_rows), :]
        pltpu.make_async_copy(rest, rest, wy_recv_sem).wait()
    far_part = dot_t(m_far[...].reshape(nx * LANES, far_cols), w_far[...])
    far_send[...] = far_part[LANES:].astype(BF)
    own_part = own_part + far_part[:LANES]
    far_copies = []
    for d in range(1, nx):
        copy = pltpu.make_async_remote_copy(
            src_ref=far_send.at[pl.ds((d - 1) * LANES, LANES), :], dst_ref=far_recv.at[d - 1],
            send_sem=fr_send_sem.at[d], recv_sem=fr_recv_sem,
            device_id=(dp, member(zl * nx + lax.rem(x + nx - d, nx)), ch), device_id_type=MESH,
        )
        copy.start()
        far_copies.append(copy)

    mine = project(0)
    for sub in range(1, SUB):
        after = project(sub)
        give_back(sub - 1, mine)
        mine = after
    give_back(SUB - 1, mine)

    a2a_wait(1, c_recv)
    inner_t = gather_channels(c_recv) + skip_t * sig_t[...]
    gated_t = (gate_t[...] * inner_t).astype(BF)
    r_send[...] = dot(down_sel, gated_t)
    r_copy = to_chan(r_send, r_recv, r_sem.at[0], r_sem.at[1])
    r_copy.start()
    b_send[:, half:half + width] = dot_t(back_rank, gated_t).astype(BF)

    grad_y = own_part + received(pre0_copy, pre0_recv)
    pltpu.make_async_copy(ret_recv, ret_recv, ret_recv_sem).wait()
    pltpu.make_async_copy(far_recv, far_recv, fr_recv_sem).wait()
    for k in range(2):
        grad_y = grad_y + ret_recv[k].astype(F32)
    for k in range(nx - 1):
        grad_y = grad_y + far_recv[k].astype(F32)
    grad_y = grad_y.T * live_row + dot_0(down_sel, back_rank)
    grad_u = grad_y * gate_t[...]
    gradu_t[...] = grad_u
    for cc in range(PER):
        u_stage[:, cc, :] = gradu_t[cc * n:(cc + 1) * n, :]
    u_send[...] = u_stage[...].astype(BF)
    a2a_start(2, u_send, u_recv, block)
    r_copy.wait()
    fwd_rank = (2.0 * (r_send[...] + r_recv[...]) * keep).astype(BF)
    b_send[:, :half] = dot(fwd_rank, masked[...]).astype(BF)

    product = grad_u * sig_t[...]
    high = product.astype(BF)
    low = (product - high.astype(F32)).astype(BF)
    ones = jnp.ones((max_rank, LANES), BF)
    at = half + a_chunks * LANES
    b_send[:, at:at + width] = (dot_t(ones, high) + dot_t(ones, low)).astype(BF)

    def share(p, owner):
        src = b_send.at[:, pl.ds(pl.multiple_of(p * LANES, LANES), LANES)]
        dst = b_recv.at[pl.ds(pl.multiple_of(me * 16, 16), 16), :]

        @pl.when(owner != me)
        def _():
            pltpu.make_async_remote_copy(
                src_ref=src, dst_ref=dst, send_sem=b_sem.at[0], recv_sem=b_sem.at[1],
                device_id=(dp, owner, ch), device_id_type=MESH,
            ).start()

        @pl.when(owner == me)
        def _():
            pltpu.make_async_copy(src, dst, b_sem.at[1]).start()

    def share_main(d, _):
        p = lax.rem(me + d, plane)
        share(p, p)
        return 0

    for k in range(extras):
        share(plane + k, plane + (k % ny) * nx + k // ny)
    lax.fori_loop(0, plane, share_main, 0, unroll=4 if n == 64 else 1)

    ggat_ref[...] = (grad_y * inner_t).T.astype(BF)
    outs = [
        pltpu.make_async_copy(s, d, out_sem.at[i])
        for i, (s, d) in enumerate((
            (ggat_ref, ggat_hbm), (gsig_ref, gsig_hbm), (gfilt_ref, gfilt_hbm), (g_recv, gbank_hbm),
        ))
    ]
    outs[0].start()

    a2a_wait(2, u_recv)
    u_back[...] = u_recv[...].astype(F32)
    forward(lambda cc: u_back[:, cc, :], spec_g)
    g_re, g_im = spec_g[:, :LANES], spec_g[:, LANES:]
    s_re, s_im = spec_s[:, :LANES], spec_s[:, LANES:]
    spread_channels(ks_stage, inverse(g_re * s_re + g_im * s_im, g_im * s_re - g_re * s_im))
    ks_send[...] = ks_stage[...].astype(BF)
    a2a_start(3, ks_send, ks_recv, block)

    column = zl * plane + x * ny
    is_owner = column + y < n_own

    def q_copy(step):
        return pltpu.make_async_remote_copy(
            src_ref=q_send, dst_ref=q_recv.at[step - 1], send_sem=q_send_sem.at[step],
            recv_sem=q_recv_sem, device_id=(lax.rem(dp + step, 4), me, ch), device_id_type=MESH,
        )

    @pl.when(is_owner)
    def _():
        pltpu.make_async_copy(b_recv, b_recv, b_sem.at[1]).wait()
        acc = b_recv[0:16, :].astype(F32)
        for i in range(1, n):
            acc = acc + b_recv[16 * i:16 * (i + 1), :].astype(F32)
        q_send[...] = jnp.concatenate([acc * pick0, acc * pick1], axis=0)
        for step in (1, 3, 2):
            q_copy(step).start()

    f_re, f_im = spec_f[:, :LANES], spec_f[:, LANES:]
    spread_channels(kf_stage, inverse(g_re * f_re + g_im * f_im, g_im * f_re - g_re * f_im))
    kf_send[...] = kf_stage[...].astype(BF)
    a2a_start(4, kf_send, kf_recv, block)

    g_size = 2 * max_rank
    bank_rows = pl.ds(pl.multiple_of((column + y) * g_size, g_size), g_size)

    @pl.when(is_owner)
    def _():
        pltpu.make_async_copy(q_recv, q_recv, q_recv_sem).wait()
        g_send[...] = (q_send[...] + q_recv[0] + q_recv[1] + q_recv[2]).astype(BF)
        for k in range(1, ny):
            pltpu.make_async_remote_copy(
                src_ref=g_send, dst_ref=g_recv.at[bank_rows, :], send_sem=g_sem.at[0], recv_sem=g_sem.at[1],
                device_id=(dp, zl * plane + lax.rem(y + k, ny) * nx + x, ch), device_id_type=MESH,
            ).start()
        pltpu.make_async_copy(g_send, g_recv.at[bank_rows, :], g_sem.at[1]).start()

    a2a_wait(3, ks_recv)
    quarter = width // 4
    ks_back[...] = ks_recv[...].astype(F32)
    corr_st[...] = gather_channels(ks_back)
    f_send[...] = corr_st[...].astype(BF)
    f_copies = []
    for step in (1, 3, 2):
        q = lax.rem(dp + step, 4)
        copy = pltpu.make_async_remote_copy(
            src_ref=f_send.at[pl.ds(pl.multiple_of(q * quarter, quarter), quarter), :],
            dst_ref=f_recv.at[step - 1], send_sem=f_send_sem.at[step], recv_sem=f_recv_sem,
            device_id=(q, me, ch), device_id_type=MESH,
        )
        copy.start()
        f_copies.append(copy)

    columns = [(zl == 0, ny)] + [
        ((zl == 1) & (x == k), max(0, min(ny, extras - k * ny))) for k in range(nx)
    ]

    def block_copy(k, count):
        rows_of = pl.ds(pl.multiple_of(column * g_size, g_size), count * g_size)
        return pltpu.make_async_remote_copy(
            src_ref=g_recv.at[rows_of, :], dst_ref=g_recv.at[rows_of, :],
            send_sem=g_sem.at[2], recv_sem=g_sem.at[3],
            device_id=(dp, member(lax.rem(g + k, group)), ch), device_id_type=MESH,
        )

    for here, count in columns:
        if count:
            @pl.when(here)
            def _():
                part = g_recv.at[pl.ds(0, count * g_size), :]
                pltpu.make_async_copy(part, part, g_sem.at[1]).wait()
                for k in range(1, group):
                    block_copy(k, count).start()

    a2a_wait(4, kf_recv)
    kf_back[...] = kf_recv[...].astype(F32)
    gsig_ref[...] = (gather_channels(kf_back) + skip_t * gradu_t[...]).T.astype(BF)
    outs[1].start()

    pltpu.make_async_copy(f_recv, f_recv, f_recv_sem).wait()
    my_quarter = pl.ds(pl.multiple_of(dp * quarter, quarter), quarter)
    sums = corr_st[my_quarter, :]
    for k in range(3):
        sums = sums + f_recv[k].astype(F32)
    h_send[...] = sums.astype(BF)
    h_copies = []
    for step in (1, 3, 2):
        copy = pltpu.make_async_remote_copy(
            src_ref=h_send, dst_ref=h_recv.at[my_quarter, :], send_sem=h_send_sem.at[step],
            recv_sem=h_recv_sem, device_id=(lax.rem(dp + step, 4), me, ch), device_id_type=MESH,
        )
        copy.start()
        h_copies.append(copy)
    pltpu.make_async_copy(h_send, h_recv.at[my_quarter, :], h_recv_sem).start()

    pltpu.make_async_copy(h_recv, h_recv, h_recv_sem).wait()
    gfilt_ref[...] = h_recv[...].astype(F32).T
    outs[2].start()

    for here, count in columns:
        @pl.when(here)
        def _():
            part = g_recv.at[pl.ds(0, (n_own - count) * g_size), :]
            pltpu.make_async_copy(part, part, g_sem.at[3]).wait()
    outs[3].start()

    for sub in range(SUB):
        for qq in range(2):
            for hh in range(2):
                @pl.when(to_other(qq))
                def _():
                    cot_copy(sub, qq, hh).wait_send()
    for qq in range(2):
        for hh in range(2):
            @pl.when((2 * ch + qq == dp) & (ch != hh))
            def _():
                own_copy(qq, hh).wait_send()
    a2a_wait_send(0, sf_send, 8)
    for k, src in ((1, c_send), (2, u_send), (3, ks_send), (4, kf_send)):
        a2a_wait_send(k, src, 1)
    w_copy.wait_send()
    pre0_copy.wait_send()
    wf_copy.wait_send()
    for copy in wy_copies + far_copies + pre_copies + ret_copies + f_copies + h_copies:
        copy.wait_send()

    @pl.when(holds_far)
    def _():
        def sent(d, _):
            pltpu.make_async_copy(m_far.at[0], m_far.at[0], far_sem.at[0]).wait()
            return 0

        lax.fori_loop(1, 2 * nx, sent, 0)

    def b_sent(count):
        part = b_send.at[:, pl.ds(0, count * LANES)]
        pltpu.make_async_copy(part, part, b_sem.at[0]).wait()

    @pl.when(is_owner)
    def _():
        b_sent(n_own - 1)
        for step in (1, 3, 2):
            q_copy(step).wait_send()
        for _ in range(1, ny):
            pltpu.make_async_copy(g_send, g_send, g_sem.at[0]).wait()

    @pl.when(jnp.logical_not(is_owner))
    def _():
        b_sent(n_own)

    for here, count in columns:
        if count:
            @pl.when(here)
            def _():
                for k in range(1, group):
                    block_copy(k, count).wait_send()

    for out in outs:
        out.wait()


def received(copy, ref):
    copy.wait_recv()
    return ref[...].astype(F32)


def finish_kernel(
    ny,
    gsig_in, ggat_in, gfilt_in, gbank_in,
    gsig_out, ggat_out, gfilt_out, gskip_out, ga_out, gb_out,
    gsig_ref, ggat_ref, gfilt_ref, gbank_ref, gskip_ref, ga_ref, gb_ref, in_sem, out_sem,
):
    max_rank, half = gb_ref.shape[1:]
    width = ga_ref.shape[2]
    g_size = 2 * max_rank
    up_chunks = half // LANES
    nx = up_chunks // ny
    a_chunks = -(-width // LANES)
    pairs = ((gbank_in, gbank_ref), (gfilt_in, gfilt_ref), (gsig_in, gsig_ref), (ggat_in, ggat_ref))
    loads = [pltpu.make_async_copy(s, d, in_sem.at[i]) for i, (s, d) in enumerate(pairs)]
    for load in loads:
        load.start()
    pairs = (
        (gb_ref, gb_out), (gfilt_ref, gfilt_out), (gsig_ref, gsig_out), (ggat_ref, ggat_out),
        (gskip_ref, gskip_out), (ga_ref, ga_out),
    )
    stores = [pltpu.make_async_copy(s, d, out_sem.at[i]) for i, (s, d) in enumerate(pairs)]
    loads[0].wait()
    for p in range(up_chunks):
        at = ((p % nx) * ny + p // nx) * g_size
        block = gbank_ref[at:at + g_size, :].astype(F32)
        gb_ref[0, :, p * LANES:(p + 1) * LANES] = block[:max_rank]
        gb_ref[1, :, p * LANES:(p + 1) * LANES] = block[max_rank:]
    stores[0].start()
    for k in range(1, 4):
        loads[k].wait()
        stores[k].start()
    size = min(LANES, width)
    for k in range(a_chunks):
        at = (up_chunks + k) * g_size
        block = gbank_ref[at:at + g_size, :].astype(F32)
        ga_ref[0, :, k * size:(k + 1) * size] = block[:max_rank, :size]
        ga_ref[1, :, k * size:(k + 1) * size] = block[max_rank:, :size]
        at = (up_chunks + a_chunks + k) * g_size
        block = gbank_ref[at:at + g_size, :].astype(F32)
        gskip_ref[:, k * size:(k + 1) * size] = (block[0:1] + block[max_rank:max_rank + 1])[:, :size]
    stores[4].start()
    stores[5].start()
    for store in stores:
        store.wait()


def local(
    signal, gating, cotangent, filt, skip, output_projection,
    adapter_down_bank, adapter_up_bank, adapter_index, sequence_rank, real_length,
):
    n = lax.axis_size("seq")
    width = signal.shape[2]
    half = cotangent.shape[2]
    cols = output_projection.shape[1] // 2
    max_rank = adapter_up_bank.shape[1]
    a_chunks = -(-width // LANES)
    n_own = half // LANES + 2 * a_chunks
    piece = LANES // SUB
    nx = min(4, n // 2)
    far_cols = 2 * cols // nx
    consts = [jnp.asarray(t) for t in tables(n)]
    rows = consts[4].shape[0]
    vmem = pl.BlockSpec(memory_space=pltpu.VMEM)
    smem = pl.BlockSpec(memory_space=pltpu.SMEM)
    hbm = pl.BlockSpec(memory_space=pltpu.HBM)
    dma = pltpu.SemaphoreType.DMA
    arrays = [
        signal[0], gating[0], cotangent[0], filt, skip[None], output_projection,
        jnp.swapaxes(adapter_down_bank, 1, 2), adapter_up_bank, *consts,
    ]
    block = pltpu.VMEM((n, PER, LANES), F32)
    narrow = pltpu.VMEM((n, PER, LANES), BF)
    eight = pltpu.VMEM((8 * n, LANES), F32)
    wide = pltpu.VMEM((width, LANES), F32)
    spec = pltpu.VMEM((PER * rows, 2 * LANES), F32)
    rank = pltpu.VMEM((max_rank, LANES), F32)
    outs = pl.pallas_call(
        functools.partial(kernel, n),
        out_shape=(
            jax.ShapeDtypeStruct((LANES, width), BF),
            jax.ShapeDtypeStruct((LANES, width), BF),
            jax.ShapeDtypeStruct((LANES, width), F32),
            jax.ShapeDtypeStruct((2 * max_rank * n_own, LANES), BF),
        ),
        in_specs=[smem] * 3 + [hbm] * len(arrays),
        out_specs=(hbm,) * 4,
        scratch_shapes=[
            pltpu.VMEM((LANES, width), BF),
            pltpu.VMEM((LANES, width), BF),
            pltpu.VMEM((LANES, width), F32),
        ] + [pltpu.VMEM(a.shape, a.dtype) for a in arrays] + [
            pltpu.VMEM((LANES, half), BF),
            wide, wide, wide, spec, spec, spec,
            eight, eight, block, block, narrow, narrow, narrow, narrow, narrow, narrow,
            block, block, block, block, block, block,
            pltpu.VMEM((LANES, cols), BF),
            pltpu.VMEM((SUB, 2, piece, cols), BF),
            pltpu.VMEM((nx, LANES, far_cols), BF),
            pltpu.VMEM((width, far_cols), BF),
            pltpu.VMEM(((nx - 1) * LANES, width), BF),
            pltpu.VMEM((nx - 1, LANES, width), BF),
            pltpu.VMEM((width, cols), BF),
            pltpu.VMEM((LANES, width), BF),
            pltpu.VMEM((LANES, width), BF),
            pltpu.VMEM((SUB, 2 * piece, width), BF),
            pltpu.VMEM((SUB, 2 * piece, width), BF),
            pltpu.VMEM((SUB, 2 * piece, width), BF),
            pltpu.VMEM((2, LANES, width), BF),
            rank, rank, rank, rank,
            pltpu.VMEM((max_rank, n_own * LANES), BF),
            pltpu.VMEM((16 * n, LANES), BF),
            pltpu.VMEM((2 * max_rank, LANES), F32),
            pltpu.VMEM((3, 2 * max_rank, LANES), F32),
            pltpu.VMEM((2 * max_rank, LANES), BF),
            pltpu.VMEM((2 * max_rank * n_own, LANES), BF),
            pltpu.VMEM((width, LANES), BF),
            pltpu.VMEM((3, width // 4, LANES), BF),
            wide,
            pltpu.VMEM((width // 4, LANES), BF),
            pltpu.VMEM((width, LANES), BF),
            dma((len(arrays),)), dma((4,)), dma((5,)), dma((5,)), dma((SUB, 4)), dma((SUB,)), dma((2,)), dma((2,)),
            dma((2,)), dma((SUB,)), dma((SUB,)), dma((SUB, 4)), dma, dma((2,)), dma((2,)), dma((2,)),
            dma((4,)), dma, dma((4,)), dma((4,)), dma,
            dma((4,)), dma, dma((2,)), dma((2,)), dma((8,)), dma, dma((nx,)), dma,
        ],
        compiler_params=pltpu.CompilerParams(
            collective_id=0, has_side_effects=True, vmem_limit_bytes=VMEM_LIMIT
        ),
    )(adapter_index, sequence_rank, real_length, *arrays)
    grad_signal, grad_gating, grad_filt, grad_skip, grad_a, grad_b = pl.pallas_call(
        functools.partial(finish_kernel, n // (2 * nx)),
        out_shape=(
            jax.ShapeDtypeStruct((LANES, width), BF),
            jax.ShapeDtypeStruct((LANES, width), BF),
            jax.ShapeDtypeStruct((LANES, width), F32),
            jax.ShapeDtypeStruct((1, width), F32),
            jax.ShapeDtypeStruct((2, max_rank, width), F32),
            jax.ShapeDtypeStruct((2, max_rank, half), F32),
        ),
        in_specs=[hbm] * 4,
        out_specs=(hbm,) * 6,
        scratch_shapes=[
            pltpu.VMEM((LANES, width), BF), pltpu.VMEM((LANES, width), BF), pltpu.VMEM((LANES, width), F32),
            pltpu.VMEM((2 * max_rank * n_own, LANES), BF), pltpu.VMEM((1, width), F32),
            pltpu.VMEM((2, max_rank, width), F32), pltpu.VMEM((2, max_rank, half), F32),
            dma((4,)), dma((6,)),
        ],
        compiler_params=pltpu.CompilerParams(vmem_limit_bytes=VMEM_LIMIT),
    )(*outs)
    return (grad_signal[None], grad_gating[None], grad_filt, grad_skip[0], jnp.swapaxes(grad_a, 1, 2), grad_b)


def solution(mesh):
    placed = (
        P("dp", "seq", "chan"), P("dp", "seq", "chan"), P("dp", "seq", "chan"), P("seq", "chan"),
        P("chan"), P("chan", "dp"), P(None, "chan", None), P(None, None, "chan"),
        P("dp"), P("dp"), P("dp"),
    )
    return jax.shard_map(
        local,
        mesh=mesh,
        in_specs=placed,
        out_specs=(
            P("dp", "seq", "chan"), P("dp", "seq", "chan"), P("seq", "chan"), P("chan"),
            P(None, "chan", None), P(None, None, "chan"),
        ),
        check_vma=False,
    )
```

```python
import functools
import math

import jax
import jax.numpy as jnp
import ml_dtypes
import numpy as np
from jax import lax
from jax.experimental import pallas as pl
from jax.experimental.pallas import tpu as pltpu
from jax.sharding import PartitionSpec as P

MESH = pl.DeviceIdType.MESH
BF = jnp.bfloat16
F32 = jnp.float32
LANES = 128
PER = 4
VMEM_LIMIT = 62 * 1024 * 1024
SUB = 2


def split3(table, axis, order):
    high = table.astype(ml_dtypes.bfloat16)
    low = (table - high.astype(np.float64)).astype(ml_dtypes.bfloat16)
    return np.concatenate([high if o else low for o in order], axis=axis)


def tables(n):
    rows = -(-(n + 1) // 8) * 8
    k1 = np.arange(rows)
    used = (k1 <= n).astype(np.float64)
    i = np.arange(n)
    a = np.arange(LANES)
    period = 2 * n * LANES
    th1 = 2 * math.pi * (k1[:, None] * i[None, :] % (2 * n)) / (2 * n)
    first = np.concatenate([np.cos(th1) * used[:, None], -np.sin(th1) * used[:, None]], 0)
    thw = 2 * math.pi * (k1[:, None] * a[None, :] % period) / period
    tw_cos, tw_sin = np.cos(thw), np.sin(thw)
    th2 = 2 * math.pi * (a[:, None] * a[None, :] % LANES) / LANES
    c2, s2 = np.cos(th2), np.sin(th2)
    second = np.block([[c2, -s2], [s2, c2]])
    second_back = np.block([[c2, s2], [-s2, c2]])
    weight = used * np.where((k1 == 0) | (k1 == n), 1.0, 2.0) / period
    last = np.concatenate([np.cos(th1).T * weight, -np.sin(th1).T * weight], 1)
    return (
        split3(first, 1, (1, 1, 0)),
        split3(second, 0, (1, 1, 0)),
        split3(second_back, 0, (1, 1, 0)),
        split3(last, 1, (1, 1, 0)),
        tw_cos.astype(np.float32),
        tw_sin.astype(np.float32),
    )


def split_data(x, axis):
    high = x.astype(BF)
    low = (x - high.astype(F32)).astype(BF)
    return jnp.concatenate([high, low, high], axis=axis)


def dot(a, b):
    return jnp.dot(a, b, preferred_element_type=F32)


def dot_t(a, b):
    return lax.dot_general(a, b, (((1,), (1,)), ((), ())), preferred_element_type=F32)


def dot_0(a, b):
    return lax.dot_general(a, b, (((0,), (0,)), ((), ())), preferred_element_type=F32)


def kernel(
    n,
    index_ref, rank_ref, length_ref,
    signal_hbm, gating_hbm, cot_hbm, filt_hbm, skip_hbm, w_hbm, down_hbm, up_hbm,
    t1_hbm, t2_hbm, t2b_hbm, t1b_hbm, tc_hbm, ts_hbm,
    gsig_hbm, ggat_hbm, gfilt_hbm, gbank_hbm,
    gsig_ref, ggat_ref, gfilt_ref,
    signal_ref, gating_ref, cot_ref, filt_ref, skip_ref, w_ref, down_ref, up_ref,
    t1_ref, t2_ref, t2b_ref, t1b_ref, tc_ref, ts_ref,
    masked, sig_t, gate_t, gradu_t, spec_s, spec_f, spec_g,
    sf_send, sf_recv, c_send, c_recv, u_send, u_recv, ks_send, ks_recv, kf_send, kf_recv,
    u_stage, u_back, ks_stage, ks_back, kf_stage, kf_back,
    m_own, m_recv, m_far, w_far, far_send, far_recv, w_recv, pre0_send, pre0_recv, pre_send, pre_recv, ret_send, ret_recv,
    d_send, d_recv, r_send, r_recv,
    b_send, b_recv, q_send, q_recv, g_send, g_recv, f_send, f_recv, corr_st, h_send, h_recv,
    in_sem, out_sem, a2a_send_sem, a2a_recv_sem, m_send_sem, m_recv_sem, own_sem, w_sem, pre0_sem,
    pre_send_sem, pre_recv_sem, ret_send_sem, ret_recv_sem, d_sem, r_sem, b_sem,
    q_send_sem, q_recv_sem, g_sem, f_send_sem, f_recv_sem,
    h_send_sem, h_recv_sem, far_sem, wf_sem, wy_send_sem, wy_recv_sem, fr_send_sem, fr_recv_sem,
):
    dp = lax.axis_index("dp")
    me = lax.axis_index("seq")
    ch = lax.axis_index("chan")
    other = 1 - ch
    width = w_ref.shape[0]
    cols = w_ref.shape[1] // 2
    plane = n // 2
    zl, spot = lax.div(me, plane), lax.rem(me, plane)
    nx = m_far.shape[0]
    group = 2 * nx
    ny = plane // nx
    y, x = lax.div(spot, nx), lax.rem(spot, nx)
    g = zl * nx + x
    far_cols = 2 * cols // nx
    near_cols = m_recv.shape[3]
    shared_cols = (2 * cols - 2 * near_cols) // nx

    def member(k):
        return lax.div(k, nx) * plane + y * nx + lax.rem(k, nx)

    half = cot_ref.shape[1]
    piece = LANES // SUB
    n_own = b_send.shape[1] // LANES
    extras = n_own - n // 2
    rows = t1_ref.shape[0] // 2
    a_chunks = -(-width // LANES)

    pairs = (
        (signal_hbm, signal_ref), (filt_hbm, filt_ref), (cot_hbm, cot_ref), (up_hbm, up_ref),
        (w_hbm, w_ref), (t1_hbm, t1_ref), (t2_hbm, t2_ref), (t2b_hbm, t2b_ref), (t1b_hbm, t1b_ref),
        (tc_hbm, tc_ref), (ts_hbm, ts_ref), (gating_hbm, gating_ref), (down_hbm, down_ref),
        (skip_hbm, skip_ref),
    )
    loads = [pltpu.make_async_copy(s, d, in_sem.at[i]) for i, (s, d) in enumerate(pairs)]
    for load in loads:
        load.start()

    barrier = pltpu.get_barrier_semaphore()
    for d in range(4):
        for z in range(2):
            for c in range(2):
                if d or c:
                    pl.semaphore_signal(
                        barrier, inc=1,
                        device_id=(lax.rem(dp + d, 4), lax.rem(zl + z, 2) * plane + spot, lax.rem(ch + c, 2)),
                        device_id_type=MESH,
                    )

    def greet(d, _):
        pl.semaphore_signal(
            barrier, inc=1, device_id=(dp, lax.rem(me + d, n), ch), device_id_type=MESH
        )
        return 0

    lax.fori_loop(1, n, greet, 0, unroll=9 if n == 64 else 1)
    for z in range(2):
        for k in range(1, nx):
            pl.semaphore_signal(
                barrier, inc=1, device_id=(dp, member(z * nx + lax.rem(x + k, nx)), other),
                device_id_type=MESH,
            )

    loads[0].wait()
    loads[1].wait()
    sig_t[...] = signal_ref[...].astype(F32).T
    filt_t = filt_ref[...].T
    for cc in range(PER):
        sf_send[pl.ds(cc, n, stride=8), :] = sig_t[cc * n:(cc + 1) * n, :]
        sf_send[pl.ds(PER + cc, n, stride=8), :] = filt_t[cc * n:(cc + 1) * n, :]
    real_length = length_ref[0]
    live_col = (me * LANES + lax.broadcasted_iota(jnp.int32, (LANES, 1), 0) < real_length).astype(F32)
    live_row = (me * LANES + lax.broadcasted_iota(jnp.int32, (1, LANES), 1) < real_length).astype(F32)
    pick1 = index_ref[0].astype(F32)
    pick0 = 1.0 - pick1

    pl.semaphore_wait(barrier, n - 1 + 14 + 2 * (nx - 1))

    def a2a_start(k, src, dst, at):
        def body(d, _):
            j = lax.rem(me + d, n)
            pltpu.make_async_remote_copy(
                src_ref=src.at[at(j)],
                dst_ref=dst.at[at(me)],
                send_sem=a2a_send_sem.at[k],
                recv_sem=a2a_recv_sem.at[k],
                device_id=(dp, j, ch),
                device_id_type=MESH,
            ).start()
            return 0

        lax.fori_loop(1, n, body, 0, unroll=9 if n == 64 else 1)
        pltpu.make_async_copy(src.at[at(me)], dst.at[at(me)], a2a_recv_sem.at[k]).start()

    def a2a_wait(k, dst):
        pltpu.make_async_copy(dst, dst, a2a_recv_sem.at[k]).wait()

    def a2a_wait_send(k, src, size):
        part = src.at[pl.ds(0, (n - 1) * size)]
        pltpu.make_async_copy(part, part, a2a_send_sem.at[k]).wait()

    def eight(j):
        return pl.ds(pl.multiple_of(j * 8, 8), 8)

    def block(j):
        return j

    a2a_start(0, sf_send, sf_recv, eight)

    def cot_copy(sub, qq, hh):
        q = 2 * ch + qq
        return pltpu.make_async_remote_copy(
            src_ref=cot_hbm.at[pl.ds(sub * piece, piece), pl.ds(2 * qq * cols + hh * near_cols, near_cols)],
            dst_ref=m_recv.at[sub, zl],
            send_sem=m_send_sem.at[sub, 2 * qq + hh],
            recv_sem=m_recv_sem.at[sub],
            device_id=(q, lax.div(lax.rem(q - dp + 4, 4), 3) * plane + spot, hh),
            device_id_type=MESH,
        )

    def own_copy(qq, hh):
        return pltpu.make_async_remote_copy(
            src_ref=cot_hbm.at[:, pl.ds((2 * qq + hh) * cols, cols)],
            dst_ref=m_own,
            send_sem=own_sem.at[0],
            recv_sem=own_sem.at[1],
            device_id=(dp, me, hh),
            device_id_type=MESH,
        )

    def to_other(qq):
        return lax.rem(2 * ch + qq - dp + 4, 2) == 1

    for sub in range(SUB):
        for qq in range(2):
            for hh in range(2):
                @pl.when(to_other(qq))
                def _():
                    cot_copy(sub, qq, hh).start()
    for qq in range(2):
        for hh in range(2):
            @pl.when((2 * ch + qq == dp) & (ch != hh))
            def _():
                own_copy(qq, hh).start()

            @pl.when((2 * ch + qq == dp) & (ch == hh))
            def _():
                pltpu.make_async_copy(
                    cot_hbm.at[:, pl.ds((2 * qq + hh) * cols, cols)], m_own, own_sem.at[1]
                ).start()

    far = lax.rem(dp + 2, 4)
    slice_rows = width // ny
    my_slice = pl.ds(pl.multiple_of(y * slice_rows, slice_rows), slice_rows)

    wf_copies = []
    for i, (b, first, size, at) in enumerate((
        (2, 0, far_cols, 0),
        (3, 2 * near_cols, shared_cols, far_cols),
        (1, 2 * near_cols, shared_cols, far_cols + shared_cols),
    )):
        wf_copies.append(pltpu.make_async_remote_copy(
            src_ref=w_hbm.at[my_slice, pl.ds(pl.multiple_of(first + x * size, size), size)],
            dst_ref=w_far.at[my_slice, pl.ds(at, size)],
            send_sem=wf_sem.at[2 * i], recv_sem=wf_sem.at[2 * i + 1],
            device_id=(lax.rem(dp + b, 4), me, ch), device_id_type=MESH,
        ))
        wf_copies[-1].start()

    def row_copy(src, at, size, d, c, send_sem):
        dst = m_far.at[d, :, pl.ds(at, size)]
        if d == 0 and c == 0:
            return pltpu.make_async_copy(src, dst, far_sem.at[1])
        return pltpu.make_async_remote_copy(
            src_ref=src, dst_ref=dst, send_sem=send_sem, recv_sem=far_sem.at[1],
            device_id=(dp, member(zl * nx + lax.rem(x + d, nx)), lax.rem(ch + c, 2)), device_id_type=MESH,
        )

    def far_copy(d, c):
        at = lax.rem(far, 2) * 2 * cols + lax.rem(x + d, nx) * far_cols
        src = cot_hbm.at[:, pl.ds(pl.multiple_of(at, far_cols), far_cols)]
        return row_copy(src, 0, far_cols, d, c, far_sem.at[0])

    def shared_copy(qq, step, d, c):
        at = 2 * qq * cols + 2 * near_cols + lax.rem(x + d, nx) * shared_cols
        src = cot_hbm.at[:, pl.ds(pl.multiple_of(at, shared_cols), shared_cols)]
        return row_copy(src, far_cols + (step // 3) * shared_cols, shared_cols, d, c, far_sem.at[2])

    for qq in range(2):
        for step in (1, 3):
            @pl.when(lax.rem(2 * ch + qq - dp + 4, 4) == step)
            def _():
                for d in range(nx):
                    for c in range(2):
                        shared_copy(qq, step, d, c).start()

    holds_far = ch == lax.div(far, 2)

    @pl.when(holds_far)
    def _():
        for d in range(nx):
            for c in range(2):
                far_copy(d, c).start()

    def to_chan(src, dst, send_sem, recv_sem):
        return pltpu.make_async_remote_copy(
            src_ref=src, dst_ref=dst, send_sem=send_sem, recv_sem=recv_sem,
            device_id=(dp, me, other), device_id_type=MESH,
        )

    w_copy = to_chan(
        w_hbm.at[:, pl.ds(pl.multiple_of(other * near_cols, LANES), w_recv.shape[1])], w_recv, w_sem.at[0], w_sem.at[1]
    )
    w_copy.start()

    for copy in wf_copies:
        copy.wait_recv()
    wy_copies = []
    for k in range(1, ny):
        copy = pltpu.make_async_remote_copy(
            src_ref=w_far.at[my_slice, :], dst_ref=w_far.at[my_slice, :],
            send_sem=wy_send_sem.at[k], recv_sem=wy_recv_sem,
            device_id=(dp, zl * plane + lax.rem(y + k, ny) * nx + x, ch), device_id_type=MESH,
        )
        copy.start()
        wy_copies.append(copy)

    for load in loads[2:]:
        load.wait()
    masked[...] = (cot_ref[...].astype(F32) * live_col).astype(BF)
    up_sel = (up_ref[0].astype(F32) * pick0 + up_ref[1].astype(F32) * pick1).astype(BF)
    down_sel = (down_ref[0].astype(F32) * pick0 + down_ref[1].astype(F32) * pick1).astype(BF)
    max_rank = up_sel.shape[0]
    keep = (lax.broadcasted_iota(jnp.int32, (max_rank, LANES), 0) < rank_ref[0]).astype(F32)
    d_send[...] = dot_t(up_sel, masked[...])
    d_copy = to_chan(d_send, d_recv, d_sem.at[0], d_sem.at[1])
    d_copy.start()
    gate_t[...] = gating_ref[...].astype(F32).T
    skip_t = jnp.broadcast_to(skip_ref[...], (LANES, width)).T

    own_cols = pl.ds(pl.multiple_of(ch * cols, LANES), cols)
    pltpu.make_async_copy(m_own, m_own, own_sem.at[1]).wait()
    w_copy.wait_recv()
    skipped = pl.ds(pl.multiple_of(ch * (cols - near_cols), LANES), cols)
    pre0_send[...] = dot_t(m_own[...], w_recv[:, skipped]).astype(BF)
    pre0_copy = to_chan(pre0_send, pre0_recv, pre0_sem.at[0], pre0_sem.at[1])
    pre0_copy.start()
    own_part = dot_t(m_own[...], w_ref[:, own_cols])

    pre_copies, ret_copies = [], []

    def project(sub):
        pltpu.make_async_copy(m_recv.at[sub], m_recv.at[sub], m_recv_sem.at[sub]).wait()
        part = m_recv[sub].reshape(2 * piece, near_cols)
        pre_send[sub] = dot_t(part, w_recv[:, :near_cols]).astype(BF)
        copy = to_chan(pre_send.at[sub], pre_recv.at[sub], pre_send_sem.at[sub], pre_recv_sem.at[sub])
        copy.start()
        pre_copies.append(copy)
        return dot_t(part, w_ref[:, pl.ds(pl.multiple_of(ch * near_cols, LANES), near_cols)])

    def give_back(sub, mine):
        pre_copies[sub].wait_recv()
        ret_send[sub] = (mine + pre_recv[sub].astype(F32)).astype(BF)
        for slot in range(2):
            copy = pltpu.make_async_remote_copy(
                src_ref=ret_send.at[sub, pl.ds(slot * piece, piece)],
                dst_ref=ret_recv.at[zl, pl.ds(sub * piece, piece)],
                send_sem=ret_send_sem.at[sub, slot], recv_sem=ret_recv_sem,
                device_id=(lax.rem(dp + 3 - 2 * zl, 4), slot * plane + spot, ch), device_id_type=MESH,
            )
            copy.start()
            ret_copies.append(copy)

    tc, ts = tc_ref[...], ts_ref[...]

    def forward(load, store):
        x = jnp.concatenate([load(cc) for cc in range(PER)], axis=1)
        y = dot(t1_ref[...], split_data(x, 0))
        parts = []
        for cc in range(PER):
            re = y[:rows, cc * LANES:(cc + 1) * LANES]
            im = y[rows:, cc * LANES:(cc + 1) * LANES]
            parts.append(jnp.concatenate([re * tc + im * ts, im * tc - re * ts], axis=1))
        store[...] = dot(split_data(jnp.concatenate(parts, axis=0), 1), t2_ref[...])

    def inverse(re, im):
        q = dot(split_data(jnp.concatenate([re, im], axis=1), 1), t2b_ref[...])
        parts = []
        for cc in range(PER):
            qr = q[cc * rows:(cc + 1) * rows, :LANES]
            qi = q[cc * rows:(cc + 1) * rows, LANES:]
            parts.append(jnp.concatenate([qr * tc - qi * ts, qi * tc + qr * ts], axis=0))
        return dot(t1b_ref[...], split_data(jnp.concatenate(parts, axis=1), 0))

    def spread_channels(dst, values):
        for cc in range(PER):
            dst[:, cc, :] = values[:, cc * LANES:(cc + 1) * LANES]

    def gather_channels(src):
        return jnp.concatenate([src[:, cc, :] for cc in range(PER)], axis=0)

    a2a_wait(0, sf_recv)
    forward(lambda cc: sf_recv[pl.ds(cc, n, stride=8), :], spec_s)
    forward(lambda cc: sf_recv[pl.ds(PER + cc, n, stride=8), :], spec_f)
    s_re, s_im = spec_s[:, :LANES], spec_s[:, LANES:]
    f_re, f_im = spec_f[:, :LANES], spec_f[:, LANES:]
    spread_channels(c_send, inverse(s_re * f_re - s_im * f_im, s_re * f_im + s_im * f_re))
    a2a_start(1, c_send, c_recv, block)

    d_copy.wait()
    back_rank = (2.0 * (d_send[...] + d_recv[...]) * keep).astype(BF)

    pltpu.make_async_copy(m_far, m_far, far_sem.at[1]).wait()
    if ny > 1:
        rest = w_far.at[pl.ds(0, (ny - 1) * slice_rows), :]
        pltpu.make_async_copy(rest, rest, wy_recv_sem).wait()
    far_part = dot_t(m_far[...].reshape(nx * LANES, far_cols + 2 * shared_cols), w_far[...])
    far_send[...] = far_part[LANES:].astype(BF)
    own_part = own_part + far_part[:LANES]
    far_copies = []
    for d in range(1, nx):
        copy = pltpu.make_async_remote_copy(
            src_ref=far_send.at[pl.ds((d - 1) * LANES, LANES), :], dst_ref=far_recv.at[d - 1],
            send_sem=fr_send_sem.at[d], recv_sem=fr_recv_sem,
            device_id=(dp, member(zl * nx + lax.rem(x + nx - d, nx)), ch), device_id_type=MESH,
        )
        copy.start()
        far_copies.append(copy)

    mine = project(0)
    for sub in range(1, SUB):
        after = project(sub)
        give_back(sub - 1, mine)
        mine = after
    give_back(SUB - 1, mine)

    a2a_wait(1, c_recv)
    inner_t = gather_channels(c_recv) + skip_t * sig_t[...]
    gated_t = (gate_t[...] * inner_t).astype(BF)
    r_send[...] = dot(down_sel, gated_t)
    r_copy = to_chan(r_send, r_recv, r_sem.at[0], r_sem.at[1])
    r_copy.start()
    b_send[:, half:half + width] = dot_t(back_rank, gated_t).astype(BF)

    grad_y = own_part + received(pre0_copy, pre0_recv)
    pltpu.make_async_copy(ret_recv, ret_recv, ret_recv_sem).wait()
    pltpu.make_async_copy(far_recv, far_recv, fr_recv_sem).wait()
    for k in range(2):
        grad_y = grad_y + ret_recv[k].astype(F32)
    for k in range(nx - 1):
        grad_y = grad_y + far_recv[k].astype(F32)
    grad_y = grad_y.T * live_row + dot_0(down_sel, back_rank)
    grad_u = grad_y * gate_t[...]
    gradu_t[...] = grad_u
    for cc in range(PER):
        u_stage[:, cc, :] = gradu_t[cc * n:(cc + 1) * n, :]
    u_send[...] = u_stage[...].astype(BF)
    a2a_start(2, u_send, u_recv, block)
    r_copy.wait()
    fwd_rank = (2.0 * (r_send[...] + r_recv[...]) * keep).astype(BF)
    b_send[:, :half] = dot(fwd_rank, masked[...]).astype(BF)

    product = grad_u * sig_t[...]
    high = product.astype(BF)
    low = (product - high.astype(F32)).astype(BF)
    ones = jnp.ones((max_rank, LANES), BF)
    at = half + a_chunks * LANES
    b_send[:, at:at + width] = (dot_t(ones, high) + dot_t(ones, low)).astype(BF)

    def share(p, owner):
        src = b_send.at[:, pl.ds(pl.multiple_of(p * LANES, LANES), LANES)]
        dst = b_recv.at[pl.ds(pl.multiple_of(me * 16, 16), 16), :]

        @pl.when(owner != me)
        def _():
            pltpu.make_async_remote_copy(
                src_ref=src, dst_ref=dst, send_sem=b_sem.at[0], recv_sem=b_sem.at[1],
                device_id=(dp, owner, ch), device_id_type=MESH,
            ).start()

        @pl.when(owner == me)
        def _():
            pltpu.make_async_copy(src, dst, b_sem.at[1]).start()

    def share_main(d, _):
        p = lax.rem(me + d, plane)
        share(p, p)
        return 0

    for k in range(extras):
        share(plane + k, plane + (k % ny) * nx + k // ny)
    lax.fori_loop(0, plane, share_main, 0, unroll=4 if n == 64 else 1)

    ggat_ref[...] = (grad_y * inner_t).T.astype(BF)
    outs = [
        pltpu.make_async_copy(s, d, out_sem.at[i])
        for i, (s, d) in enumerate((
            (ggat_ref, ggat_hbm), (gsig_ref, gsig_hbm), (gfilt_ref, gfilt_hbm), (g_recv, gbank_hbm),
        ))
    ]
    outs[0].start()

    a2a_wait(2, u_recv)
    u_back[...] = u_recv[...].astype(F32)
    forward(lambda cc: u_back[:, cc, :], spec_g)
    g_re, g_im = spec_g[:, :LANES], spec_g[:, LANES:]
    s_re, s_im = spec_s[:, :LANES], spec_s[:, LANES:]
    spread_channels(ks_stage, inverse(g_re * s_re + g_im * s_im, g_im * s_re - g_re * s_im))
    ks_send[...] = ks_stage[...].astype(BF)
    a2a_start(3, ks_send, ks_recv, block)

    column = zl * plane + x * ny
    is_owner = column + y < n_own

    def q_copy(step):
        return pltpu.make_async_remote_copy(
            src_ref=q_send, dst_ref=q_recv.at[step - 1], send_sem=q_send_sem.at[step],
            recv_sem=q_recv_sem, device_id=(lax.rem(dp + step, 4), me, ch), device_id_type=MESH,
        )

    @pl.when(is_owner)
    def _():
        pltpu.make_async_copy(b_recv, b_recv, b_sem.at[1]).wait()
        acc = b_recv[0:16, :].astype(F32)
        for i in range(1, n):
            acc = acc + b_recv[16 * i:16 * (i + 1), :].astype(F32)
        q_send[...] = jnp.concatenate([acc * pick0, acc * pick1], axis=0)
        for step in (1, 3, 2):
            q_copy(step).start()

    f_re, f_im = spec_f[:, :LANES], spec_f[:, LANES:]
    spread_channels(kf_stage, inverse(g_re * f_re + g_im * f_im, g_im * f_re - g_re * f_im))
    kf_send[...] = kf_stage[...].astype(BF)
    a2a_start(4, kf_send, kf_recv, block)

    g_size = 2 * max_rank
    bank_rows = pl.ds(pl.multiple_of((column + y) * g_size, g_size), g_size)

    @pl.when(is_owner)
    def _():
        pltpu.make_async_copy(q_recv, q_recv, q_recv_sem).wait()
        g_send[...] = (q_send[...] + q_recv[0] + q_recv[1] + q_recv[2]).astype(BF)
        for k in range(1, ny):
            pltpu.make_async_remote_copy(
                src_ref=g_send, dst_ref=g_recv.at[bank_rows, :], send_sem=g_sem.at[0], recv_sem=g_sem.at[1],
                device_id=(dp, zl * plane + lax.rem(y + k, ny) * nx + x, ch), device_id_type=MESH,
            ).start()
        pltpu.make_async_copy(g_send, g_recv.at[bank_rows, :], g_sem.at[1]).start()

    a2a_wait(3, ks_recv)
    quarter = width // 4
    ks_back[...] = ks_recv[...].astype(F32)
    corr_st[...] = gather_channels(ks_back)
    f_send[...] = corr_st[...].astype(BF)
    f_copies = []
    for step in (1, 3, 2):
        q = lax.rem(dp + step, 4)
        copy = pltpu.make_async_remote_copy(
            src_ref=f_send.at[pl.ds(pl.multiple_of(q * quarter, quarter), quarter), :],
            dst_ref=f_recv.at[step - 1], send_sem=f_send_sem.at[step], recv_sem=f_recv_sem,
            device_id=(q, me, ch), device_id_type=MESH,
        )
        copy.start()
        f_copies.append(copy)

    columns = [(zl == 0, ny)] + [
        ((zl == 1) & (x == k), max(0, min(ny, extras - k * ny))) for k in range(nx)
    ]

    def block_copy(k, count):
        rows_of = pl.ds(pl.multiple_of(column * g_size, g_size), count * g_size)
        return pltpu.make_async_remote_copy(
            src_ref=g_recv.at[rows_of, :], dst_ref=g_recv.at[rows_of, :],
            send_sem=g_sem.at[2], recv_sem=g_sem.at[3],
            device_id=(dp, member(lax.rem(g + k, group)), ch), device_id_type=MESH,
        )

    for here, count in columns:
        if count:
            @pl.when(here)
            def _():
                part = g_recv.at[pl.ds(0, count * g_size), :]
                pltpu.make_async_copy(part, part, g_sem.at[1]).wait()
                for k in range(1, group):
                    block_copy(k, count).start()

    a2a_wait(4, kf_recv)
    kf_back[...] = kf_recv[...].astype(F32)
    gsig_ref[...] = (gather_channels(kf_back) + skip_t * gradu_t[...]).T.astype(BF)
    outs[1].start()

    pltpu.make_async_copy(f_recv, f_recv, f_recv_sem).wait()
    my_quarter = pl.ds(pl.multiple_of(dp * quarter, quarter), quarter)
    sums = corr_st[my_quarter, :]
    for k in range(3):
        sums = sums + f_recv[k].astype(F32)
    h_send[...] = sums.astype(BF)
    h_copies = []
    for step in (1, 3, 2):
        copy = pltpu.make_async_remote_copy(
            src_ref=h_send, dst_ref=h_recv.at[my_quarter, :], send_sem=h_send_sem.at[step],
            recv_sem=h_recv_sem, device_id=(lax.rem(dp + step, 4), me, ch), device_id_type=MESH,
        )
        copy.start()
        h_copies.append(copy)
    pltpu.make_async_copy(h_send, h_recv.at[my_quarter, :], h_recv_sem).start()

    pltpu.make_async_copy(h_recv, h_recv, h_recv_sem).wait()
    gfilt_ref[...] = h_recv[...].astype(F32).T
    outs[2].start()

    for here, count in columns:
        @pl.when(here)
        def _():
            part = g_recv.at[pl.ds(0, (n_own - count) * g_size), :]
            pltpu.make_async_copy(part, part, g_sem.at[3]).wait()
    outs[3].start()

    for sub in range(SUB):
        for qq in range(2):
            for hh in range(2):
                @pl.when(to_other(qq))
                def _():
                    cot_copy(sub, qq, hh).wait_send()
    for qq in range(2):
        for hh in range(2):
            @pl.when((2 * ch + qq == dp) & (ch != hh))
            def _():
                own_copy(qq, hh).wait_send()
    a2a_wait_send(0, sf_send, 8)
    for k, src in ((1, c_send), (2, u_send), (3, ks_send), (4, kf_send)):
        a2a_wait_send(k, src, 1)
    w_copy.wait_send()
    pre0_copy.wait_send()
    for copy in wf_copies + wy_copies + far_copies + pre_copies + ret_copies + f_copies + h_copies:
        copy.wait_send()

    def shared_sent(d, _):
        part = m_far.at[0, :, pl.ds(far_cols, shared_cols)]
        pltpu.make_async_copy(part, part, far_sem.at[2]).wait()
        return 0

    lax.fori_loop(1, 2 * nx, shared_sent, 0)

    @pl.when(holds_far)
    def _():
        def sent(d, _):
            part = m_far.at[0, :, pl.ds(0, far_cols)]
            pltpu.make_async_copy(part, part, far_sem.at[0]).wait()
            return 0

        lax.fori_loop(1, 2 * nx, sent, 0)

    def b_sent(count):
        part = b_send.at[:, pl.ds(0, count * LANES)]
        pltpu.make_async_copy(part, part, b_sem.at[0]).wait()

    @pl.when(is_owner)
    def _():
        b_sent(n_own - 1)
        for step in (1, 3, 2):
            q_copy(step).wait_send()
        for _ in range(1, ny):
            pltpu.make_async_copy(g_send, g_send, g_sem.at[0]).wait()

    @pl.when(jnp.logical_not(is_owner))
    def _():
        b_sent(n_own)

    for here, count in columns:
        if count:
            @pl.when(here)
            def _():
                for k in range(1, group):
                    block_copy(k, count).wait_send()

    for out in outs:
        out.wait()


def received(copy, ref):
    copy.wait_recv()
    return ref[...].astype(F32)


def finish_kernel(
    ny,
    gsig_in, ggat_in, gfilt_in, gbank_in,
    gsig_out, ggat_out, gfilt_out, gskip_out, ga_out, gb_out,
    gsig_ref, ggat_ref, gfilt_ref, gbank_ref, gskip_ref, ga_ref, gb_ref, in_sem, out_sem,
):
    max_rank, half = gb_ref.shape[1:]
    width = ga_ref.shape[2]
    g_size = 2 * max_rank
    up_chunks = half // LANES
    nx = up_chunks // ny
    a_chunks = -(-width // LANES)
    pairs = ((gbank_in, gbank_ref), (gfilt_in, gfilt_ref), (gsig_in, gsig_ref), (ggat_in, ggat_ref))
    loads = [pltpu.make_async_copy(s, d, in_sem.at[i]) for i, (s, d) in enumerate(pairs)]
    for load in loads:
        load.start()
    pairs = (
        (gb_ref, gb_out), (gfilt_ref, gfilt_out), (gsig_ref, gsig_out), (ggat_ref, ggat_out),
        (gskip_ref, gskip_out), (ga_ref, ga_out),
    )
    stores = [pltpu.make_async_copy(s, d, out_sem.at[i]) for i, (s, d) in enumerate(pairs)]
    loads[0].wait()
    for p in range(up_chunks):
        at = ((p % nx) * ny + p // nx) * g_size
        block = gbank_ref[at:at + g_size, :].astype(F32)
        gb_ref[0, :, p * LANES:(p + 1) * LANES] = block[:max_rank]
        gb_ref[1, :, p * LANES:(p + 1) * LANES] = block[max_rank:]
    stores[0].start()
    for k in range(1, 4):
        loads[k].wait()
        stores[k].start()
    size = min(LANES, width)
    for k in range(a_chunks):
        at = (up_chunks + k) * g_size
        block = gbank_ref[at:at + g_size, :].astype(F32)
        ga_ref[0, :, k * size:(k + 1) * size] = block[:max_rank, :size]
        ga_ref[1, :, k * size:(k + 1) * size] = block[max_rank:, :size]
        at = (up_chunks + a_chunks + k) * g_size
        block = gbank_ref[at:at + g_size, :].astype(F32)
        gskip_ref[:, k * size:(k + 1) * size] = (block[0:1] + block[max_rank:max_rank + 1])[:, :size]
    stores[4].start()
    stores[5].start()
    for store in stores:
        store.wait()


def local(
    signal, gating, cotangent, filt, skip, output_projection,
    adapter_down_bank, adapter_up_bank, adapter_index, sequence_rank, real_length,
):
    n = lax.axis_size("seq")
    width = signal.shape[2]
    half = cotangent.shape[2]
    cols = output_projection.shape[1] // 2
    max_rank = adapter_up_bank.shape[1]
    a_chunks = -(-width // LANES)
    n_own = half // LANES + 2 * a_chunks
    piece = LANES // SUB
    nx = min(4, n // 2)
    shared = cols // 2
    near_cols = cols - shared // 2
    row_cols = 2 * (cols + shared) // nx
    consts = [jnp.asarray(t) for t in tables(n)]
    rows = consts[4].shape[0]
    vmem = pl.BlockSpec(memory_space=pltpu.VMEM)
    smem = pl.BlockSpec(memory_space=pltpu.SMEM)
    hbm = pl.BlockSpec(memory_space=pltpu.HBM)
    dma = pltpu.SemaphoreType.DMA
    arrays = [
        signal[0], gating[0], cotangent[0], filt, skip[None], output_projection,
        jnp.swapaxes(adapter_down_bank, 1, 2), adapter_up_bank, *consts,
    ]
    block = pltpu.VMEM((n, PER, LANES), F32)
    narrow = pltpu.VMEM((n, PER, LANES), BF)
    eight = pltpu.VMEM((8 * n, LANES), F32)
    wide = pltpu.VMEM((width, LANES), F32)
    spec = pltpu.VMEM((PER * rows, 2 * LANES), F32)
    rank = pltpu.VMEM((max_rank, LANES), F32)
    outs = pl.pallas_call(
        functools.partial(kernel, n),
        out_shape=(
            jax.ShapeDtypeStruct((LANES, width), BF),
            jax.ShapeDtypeStruct((LANES, width), BF),
            jax.ShapeDtypeStruct((LANES, width), F32),
            jax.ShapeDtypeStruct((2 * max_rank * n_own, LANES), BF),
        ),
        in_specs=[smem] * 3 + [hbm] * len(arrays),
        out_specs=(hbm,) * 4,
        scratch_shapes=[
            pltpu.VMEM((LANES, width), BF),
            pltpu.VMEM((LANES, width), BF),
            pltpu.VMEM((LANES, width), F32),
        ] + [pltpu.VMEM(a.shape, a.dtype) for a in arrays] + [
            pltpu.VMEM((LANES, half), BF),
            wide, wide, wide, spec, spec, spec,
            eight, eight, block, block, narrow, narrow, narrow, narrow, narrow, narrow,
            block, block, block, block, block, block,
            pltpu.VMEM((LANES, cols), BF),
            pltpu.VMEM((SUB, 2, piece, near_cols), BF),
            pltpu.VMEM((nx, LANES, row_cols), BF),
            pltpu.VMEM((width, row_cols), BF),
            pltpu.VMEM(((nx - 1) * LANES, width), BF),
            pltpu.VMEM((nx - 1, LANES, width), BF),
            pltpu.VMEM((width, 2 * cols - near_cols), BF),
            pltpu.VMEM((LANES, width), BF),
            pltpu.VMEM((LANES, width), BF),
            pltpu.VMEM((SUB, 2 * piece, width), BF),
            pltpu.VMEM((SUB, 2 * piece, width), BF),
            pltpu.VMEM((SUB, 2 * piece, width), BF),
            pltpu.VMEM((2, LANES, width), BF),
            rank, rank, rank, rank,
            pltpu.VMEM((max_rank, n_own * LANES), BF),
            pltpu.VMEM((16 * n, LANES), BF),
            pltpu.VMEM((2 * max_rank, LANES), F32),
            pltpu.VMEM((3, 2 * max_rank, LANES), F32),
            pltpu.VMEM((2 * max_rank, LANES), BF),
            pltpu.VMEM((2 * max_rank * n_own, LANES), BF),
            pltpu.VMEM((width, LANES), BF),
            pltpu.VMEM((3, width // 4, LANES), BF),
            wide,
            pltpu.VMEM((width // 4, LANES), BF),
            pltpu.VMEM((width, LANES), BF),
            dma((len(arrays),)), dma((4,)), dma((5,)), dma((5,)), dma((SUB, 4)), dma((SUB,)), dma((2,)), dma((2,)),
            dma((2,)), dma((SUB,)), dma((SUB,)), dma((SUB, 4)), dma, dma((2,)), dma((2,)), dma((2,)),
            dma((4,)), dma, dma((4,)), dma((4,)), dma,
            dma((4,)), dma, dma((3,)), dma((6,)), dma((8,)), dma, dma((nx,)), dma,
        ],
        compiler_params=pltpu.CompilerParams(
            collective_id=0, has_side_effects=True, vmem_limit_bytes=VMEM_LIMIT
        ),
    )(adapter_index, sequence_rank, real_length, *arrays)
    grad_signal, grad_gating, grad_filt, grad_skip, grad_a, grad_b = pl.pallas_call(
        functools.partial(finish_kernel, n // (2 * nx)),
        out_shape=(
            jax.ShapeDtypeStruct((LANES, width), BF),
            jax.ShapeDtypeStruct((LANES, width), BF),
            jax.ShapeDtypeStruct((LANES, width), F32),
            jax.ShapeDtypeStruct((1, width), F32),
            jax.ShapeDtypeStruct((2, max_rank, width), F32),
            jax.ShapeDtypeStruct((2, max_rank, half), F32),
        ),
        in_specs=[hbm] * 4,
        out_specs=(hbm,) * 6,
        scratch_shapes=[
            pltpu.VMEM((LANES, width), BF), pltpu.VMEM((LANES, width), BF), pltpu.VMEM((LANES, width), F32),
            pltpu.VMEM((2 * max_rank * n_own, LANES), BF), pltpu.VMEM((1, width), F32),
            pltpu.VMEM((2, max_rank, width), F32), pltpu.VMEM((2, max_rank, half), F32),
            dma((4,)), dma((6,)),
        ],
        compiler_params=pltpu.CompilerParams(vmem_limit_bytes=VMEM_LIMIT),
    )(*outs)
    return (grad_signal[None], grad_gating[None], grad_filt, grad_skip[0], jnp.swapaxes(grad_a, 1, 2), grad_b)


def solution(mesh):
    placed = (
        P("dp", "seq", "chan"), P("dp", "seq", "chan"), P("dp", "seq", "chan"), P("seq", "chan"),
        P("chan"), P("chan", "dp"), P(None, "chan", None), P(None, None, "chan"),
        P("dp"), P("dp"), P("dp"),
    )
    return jax.shard_map(
        local,
        mesh=mesh,
        in_specs=placed,
        out_specs=(
            P("dp", "seq", "chan"), P("dp", "seq", "chan"), P("seq", "chan"), P("chan"),
            P(None, "chan", None), P(None, None, "chan"),
        ),
        check_vma=False,
    )
```

```python
import functools
import math

import jax
import jax.numpy as jnp
import ml_dtypes
import numpy as np
from jax import lax
from jax.experimental import pallas as pl
from jax.experimental.pallas import tpu as pltpu
from jax.sharding import PartitionSpec as P

MESH = pl.DeviceIdType.MESH
BF = jnp.bfloat16
F32 = jnp.float32
LANES = 128
PER = 4
VMEM_LIMIT = 62 * 1024 * 1024
SUB = 2


def split3(table, axis, order):
    high = table.astype(ml_dtypes.bfloat16)
    low = (table - high.astype(np.float64)).astype(ml_dtypes.bfloat16)
    return np.concatenate([high if o else low for o in order], axis=axis)


def tables(n):
    rows = -(-(n + 1) // 8) * 8
    k1 = np.arange(rows)
    used = (k1 <= n).astype(np.float64)
    i = np.arange(n)
    a = np.arange(LANES)
    period = 2 * n * LANES
    th1 = 2 * math.pi * (k1[:, None] * i[None, :] % (2 * n)) / (2 * n)
    first = np.concatenate([np.cos(th1) * used[:, None], -np.sin(th1) * used[:, None]], 0)
    thw = 2 * math.pi * (k1[:, None] * a[None, :] % period) / period
    tw_cos, tw_sin = np.cos(thw), np.sin(thw)
    th2 = 2 * math.pi * (a[:, None] * a[None, :] % LANES) / LANES
    c2, s2 = np.cos(th2), np.sin(th2)
    second = np.block([[c2, -s2], [s2, c2]])
    second_back = np.block([[c2, s2], [-s2, c2]])
    weight = used * np.where((k1 == 0) | (k1 == n), 1.0, 2.0) / period
    last = np.concatenate([np.cos(th1).T * weight, -np.sin(th1).T * weight], 1)
    return (
        split3(first, 1, (1, 1, 0)),
        split3(second, 0, (1, 1, 0)),
        split3(second_back, 0, (1, 1, 0)),
        split3(last, 1, (1, 1, 0)),
        tw_cos.astype(np.float32),
        tw_sin.astype(np.float32),
    )


def split_data(x, axis):
    high = x.astype(BF)
    low = (x - high.astype(F32)).astype(BF)
    return jnp.concatenate([high, low, high], axis=axis)


def dot(a, b):
    return jnp.dot(a, b, preferred_element_type=F32)


def dot_t(a, b):
    return lax.dot_general(a, b, (((1,), (1,)), ((), ())), preferred_element_type=F32)


def dot_0(a, b):
    return lax.dot_general(a, b, (((0,), (0,)), ((), ())), preferred_element_type=F32)


def kernel(
    n,
    index_ref, rank_ref, length_ref,
    signal_hbm, gating_hbm, cot_hbm, filt_hbm, skip_hbm, w_hbm, down_hbm, up_hbm,
    t1_hbm, t2_hbm, t2b_hbm, t1b_hbm, tc_hbm, ts_hbm,
    gsig_hbm, ggat_hbm, gfilt_hbm, gbank_hbm,
    gsig_ref, ggat_ref, gfilt_ref,
    signal_ref, gating_ref, cot_ref, filt_ref, skip_ref, w_ref, down_ref, up_ref,
    t1_ref, t2_ref, t2b_ref, t1b_ref, tc_ref, ts_ref,
    masked, sig_t, gate_t, gradu_t, spec_s, spec_f, spec_g,
    sf_send, sf_recv, c_send, c_recv, u_send, u_recv, ks_send, ks_recv, kf_send, kf_recv,
    u_stage, u_back, ks_stage, ks_back, kf_stage, kf_back,
    m_own, m_recv, m_far, w_far, far_send, far_recv, w_recv, pre0_send, pre0_recv, pre_send, pre_recv, ret_send, ret_recv,
    d_send, d_recv, r_send, r_recv,
    b_send, b_recv, q_send, q_recv, g_send, g_recv, f_send, f_recv, corr_st, h_send, h_recv,
    in_sem, out_sem, a2a_send_sem, a2a_recv_sem, m_send_sem, m_recv_sem, own_sem, w_sem, pre0_sem,
    pre_send_sem, pre_recv_sem, ret_send_sem, ret_recv_sem, d_sem, r_sem, b_sem,
    q_send_sem, q_recv_sem, g_sem, f_send_sem, f_recv_sem,
    h_send_sem, h_recv_sem, far_sem, half_sem, wf_sem, wy_send_sem, wy_recv_sem, fr_send_sem, fr_recv_sem,
):
    dp = lax.axis_index("dp")
    me = lax.axis_index("seq")
    ch = lax.axis_index("chan")
    other = 1 - ch
    plane = n // 2
    zl, spot = lax.div(me, plane), lax.rem(me, plane)
    nx = m_far.shape[0]
    group = 2 * nx
    ny = plane // nx
    y, x = lax.div(spot, nx), lax.rem(spot, nx)
    g = zl * nx + x
    far_cols = m_far.shape[2]

    def member(k):
        return lax.div(k, nx) * plane + y * nx + lax.rem(k, nx)

    width = w_ref.shape[0]
    cols = w_ref.shape[1] // 2
    half = cot_ref.shape[1]
    piece = LANES // SUB
    n_own = b_send.shape[1] // LANES
    extras = n_own - n // 2
    rows = t1_ref.shape[0] // 2
    a_chunks = -(-width // LANES)

    pairs = (
        (signal_hbm, signal_ref), (filt_hbm, filt_ref), (cot_hbm, cot_ref), (up_hbm, up_ref),
        (w_hbm, w_ref), (t1_hbm, t1_ref), (t2_hbm, t2_ref), (t2b_hbm, t2b_ref), (t1b_hbm, t1b_ref),
        (tc_hbm, tc_ref), (ts_hbm, ts_ref), (gating_hbm, gating_ref), (down_hbm, down_ref),
        (skip_hbm, skip_ref),
    )
    loads = [pltpu.make_async_copy(s, d, in_sem.at[i]) for i, (s, d) in enumerate(pairs)]
    for load in loads:
        load.start()

    barrier = pltpu.get_barrier_semaphore()
    for d in range(4):
        for z in range(2):
            for c in range(2):
                if d or c:
                    pl.semaphore_signal(
                        barrier, inc=1,
                        device_id=(lax.rem(dp + d, 4), lax.rem(zl + z, 2) * plane + spot, lax.rem(ch + c, 2)),
                        device_id_type=MESH,
                    )

    def greet(d, _):
        pl.semaphore_signal(
            barrier, inc=1, device_id=(dp, lax.rem(me + d, n), ch), device_id_type=MESH
        )
        return 0

    lax.fori_loop(1, n, greet, 0, unroll=9 if n == 64 else 1)
    for z in range(2):
        for k in range(1, nx):
            pl.semaphore_signal(
                barrier, inc=1, device_id=(dp, member(z * nx + lax.rem(x + k, nx)), other),
                device_id_type=MESH,
            )

    loads[0].wait()
    loads[1].wait()
    sig_t[...] = signal_ref[...].astype(F32).T
    filt_t = filt_ref[...].T
    for cc in range(PER):
        sf_send[pl.ds(cc, n, stride=8), :] = sig_t[cc * n:(cc + 1) * n, :]
        sf_send[pl.ds(PER + cc, n, stride=8), :] = filt_t[cc * n:(cc + 1) * n, :]
    real_length = length_ref[0]
    live_col = (me * LANES + lax.broadcasted_iota(jnp.int32, (LANES, 1), 0) < real_length).astype(F32)
    live_row = (me * LANES + lax.broadcasted_iota(jnp.int32, (1, LANES), 1) < real_length).astype(F32)
    pick1 = index_ref[0].astype(F32)
    pick0 = 1.0 - pick1

    pl.semaphore_wait(barrier, n - 1 + 14 + 2 * (nx - 1))

    def a2a_start(k, src, dst, at):
        def body(d, _):
            j = lax.rem(me + d, n)
            pltpu.make_async_remote_copy(
                src_ref=src.at[at(j)],
                dst_ref=dst.at[at(me)],
                send_sem=a2a_send_sem.at[k],
                recv_sem=a2a_recv_sem.at[k],
                device_id=(dp, j, ch),
                device_id_type=MESH,
            ).start()
            return 0

        lax.fori_loop(1, n, body, 0, unroll=9 if n == 64 else 1)
        pltpu.make_async_copy(src.at[at(me)], dst.at[at(me)], a2a_recv_sem.at[k]).start()

    def a2a_wait(k, dst):
        pltpu.make_async_copy(dst, dst, a2a_recv_sem.at[k]).wait()

    def a2a_wait_send(k, src, size):
        part = src.at[pl.ds(0, (n - 1) * size)]
        pltpu.make_async_copy(part, part, a2a_send_sem.at[k]).wait()

    def eight(j):
        return pl.ds(pl.multiple_of(j * 8, 8), 8)

    def block(j):
        return j

    a2a_start(0, sf_send, sf_recv, eight)

    def cot_copy(sub, qq, hh):
        q = 2 * ch + qq
        return pltpu.make_async_remote_copy(
            src_ref=cot_hbm.at[pl.ds(sub * piece, piece), pl.ds((2 * qq + hh) * cols, cols)],
            dst_ref=m_recv.at[sub, zl],
            send_sem=m_send_sem.at[sub, 2 * qq + hh],
            recv_sem=m_recv_sem.at[sub],
            device_id=(q, lax.div(lax.rem(q - dp + 4, 4), 3) * plane + spot, hh),
            device_id_type=MESH,
        )

    def own_copy(qq, hh):
        return pltpu.make_async_remote_copy(
            src_ref=cot_hbm.at[:, pl.ds((2 * qq + hh) * cols, cols)],
            dst_ref=m_own,
            send_sem=own_sem.at[0],
            recv_sem=own_sem.at[1],
            device_id=(dp, me, hh),
            device_id_type=MESH,
        )

    def to_other(qq):
        return lax.rem(2 * ch + qq - dp + 4, 2) == 1

    for sub in range(SUB):
        for qq in range(2):
            for hh in range(2):
                @pl.when(to_other(qq))
                def _():
                    cot_copy(sub, qq, hh).start()
    for qq in range(2):
        for hh in range(2):
            @pl.when((2 * ch + qq == dp) & (ch != hh))
            def _():
                own_copy(qq, hh).start()

            @pl.when((2 * ch + qq == dp) & (ch == hh))
            def _():
                pltpu.make_async_copy(
                    cot_hbm.at[:, pl.ds((2 * qq + hh) * cols, cols)], m_own, own_sem.at[1]
                ).start()

    far = lax.rem(dp + 2, 4)
    slice_rows = width // ny
    my_slice = pl.ds(pl.multiple_of(y * slice_rows, slice_rows), slice_rows)

    wf_copy = pltpu.make_async_remote_copy(
        src_ref=w_hbm.at[my_slice, pl.ds(pl.multiple_of(x * far_cols, far_cols), far_cols)],
        dst_ref=w_far.at[my_slice, :],
        send_sem=wf_sem.at[0], recv_sem=wf_sem.at[1], device_id=(far, me, ch), device_id_type=MESH,
    )
    wf_copy.start()

    half_rows = LANES // 2

    def rows_of_core(c):
        return pl.ds(pl.multiple_of(c * half_rows, half_rows), half_rows)

    def far_copy(d, c):
        k = lax.rem(x + d, nx)
        core = lax.rem(ch + c, 2)
        at = lax.rem(far, 2) * 2 * cols + k * far_cols
        src = cot_hbm.at[rows_of_core(core), pl.ds(pl.multiple_of(at, far_cols), far_cols)]
        dst = m_far.at[d, rows_of_core(core)]
        if d == 0 and c == 0:
            return pltpu.make_async_copy(src, dst, far_sem.at[1])
        return pltpu.make_async_remote_copy(
            src_ref=src, dst_ref=dst, send_sem=far_sem.at[0], recv_sem=far_sem.at[1],
            device_id=(dp, member(zl * nx + k), core), device_id_type=MESH,
        )

    holds_far = ch == lax.div(far, 2)

    @pl.when(holds_far)
    def _():
        for d in range(nx):
            for c in range(2):
                far_copy(d, c).start()

    def to_chan(src, dst, send_sem, recv_sem):
        return pltpu.make_async_remote_copy(
            src_ref=src, dst_ref=dst, send_sem=send_sem, recv_sem=recv_sem,
            device_id=(dp, me, other), device_id_type=MESH,
        )

    w_copy = to_chan(
        w_hbm.at[:, pl.ds(pl.multiple_of(other * cols, LANES), cols)], w_recv, w_sem.at[0], w_sem.at[1]
    )
    w_copy.start()

    wf_copy.wait_recv()
    wy_copies = []
    for k in range(1, ny):
        copy = pltpu.make_async_remote_copy(
            src_ref=w_far.at[my_slice, :], dst_ref=w_far.at[my_slice, :],
            send_sem=wy_send_sem.at[k], recv_sem=wy_recv_sem,
            device_id=(dp, zl * plane + lax.rem(y + k, ny) * nx + x, ch), device_id_type=MESH,
        )
        copy.start()
        wy_copies.append(copy)

    for load in loads[2:]:
        load.wait()
    masked[...] = (cot_ref[...].astype(F32) * live_col).astype(BF)
    up_sel = (up_ref[0].astype(F32) * pick0 + up_ref[1].astype(F32) * pick1).astype(BF)
    down_sel = (down_ref[0].astype(F32) * pick0 + down_ref[1].astype(F32) * pick1).astype(BF)
    max_rank = up_sel.shape[0]
    keep = (lax.broadcasted_iota(jnp.int32, (max_rank, LANES), 0) < rank_ref[0]).astype(F32)
    d_send[...] = dot_t(up_sel, masked[...])
    d_copy = to_chan(d_send, d_recv, d_sem.at[0], d_sem.at[1])
    d_copy.start()
    gate_t[...] = gating_ref[...].astype(F32).T
    skip_t = jnp.broadcast_to(skip_ref[...], (LANES, width)).T

    own_cols = pl.ds(pl.multiple_of(ch * cols, LANES), cols)
    pltpu.make_async_copy(m_own, m_own, own_sem.at[1]).wait()
    w_copy.wait_recv()
    pre0_send[...] = dot_t(m_own[...], w_recv[...]).astype(BF)
    pre0_copy = to_chan(pre0_send, pre0_recv, pre0_sem.at[0], pre0_sem.at[1])
    pre0_copy.start()
    own_part = dot_t(m_own[...], w_ref[:, own_cols])

    pre_copies, ret_copies = [], []

    def project(sub):
        pltpu.make_async_copy(m_recv.at[sub], m_recv.at[sub], m_recv_sem.at[sub]).wait()
        part = m_recv[sub].reshape(2 * piece, cols)
        pre_send[sub] = dot_t(part, w_recv[...]).astype(BF)
        copy = to_chan(pre_send.at[sub], pre_recv.at[sub], pre_send_sem.at[sub], pre_recv_sem.at[sub])
        copy.start()
        pre_copies.append(copy)
        return dot_t(part, w_ref[:, own_cols])

    def give_back(sub, mine):
        pre_copies[sub].wait_recv()
        ret_send[sub] = (mine + pre_recv[sub].astype(F32)).astype(BF)
        for slot in range(2):
            copy = pltpu.make_async_remote_copy(
                src_ref=ret_send.at[sub, pl.ds(slot * piece, piece)],
                dst_ref=ret_recv.at[zl, pl.ds(sub * piece, piece)],
                send_sem=ret_send_sem.at[sub, slot], recv_sem=ret_recv_sem,
                device_id=(lax.rem(dp + 3 - 2 * zl, 4), slot * plane + spot, ch), device_id_type=MESH,
            )
            copy.start()
            ret_copies.append(copy)

    tc, ts = tc_ref[...], ts_ref[...]

    def forward(load, store):
        x = jnp.concatenate([load(cc) for cc in range(PER)], axis=1)
        y = dot(t1_ref[...], split_data(x, 0))
        parts = []
        for cc in range(PER):
            re = y[:rows, cc * LANES:(cc + 1) * LANES]
            im = y[rows:, cc * LANES:(cc + 1) * LANES]
            parts.append(jnp.concatenate([re * tc + im * ts, im * tc - re * ts], axis=1))
        store[...] = dot(split_data(jnp.concatenate(parts, axis=0), 1), t2_ref[...])

    def inverse(re, im):
        q = dot(split_data(jnp.concatenate([re, im], axis=1), 1), t2b_ref[...])
        parts = []
        for cc in range(PER):
            qr = q[cc * rows:(cc + 1) * rows, :LANES]
            qi = q[cc * rows:(cc + 1) * rows, LANES:]
            parts.append(jnp.concatenate([qr * tc - qi * ts, qi * tc + qr * ts], axis=0))
        return dot(t1b_ref[...], split_data(jnp.concatenate(parts, axis=1), 0))

    def spread_channels(dst, values):
        for cc in range(PER):
            dst[:, cc, :] = values[:, cc * LANES:(cc + 1) * LANES]

    def gather_channels(src):
        return jnp.concatenate([src[:, cc, :] for cc in range(PER)], axis=0)

    part = m_far.at[:, pl.ds(0, half_rows)]
    pltpu.make_async_copy(part, part, far_sem.at[1]).wait()
    half_copy = to_chan(
        m_far.at[:, rows_of_core(ch)], m_far.at[:, rows_of_core(ch)], half_sem.at[0], half_sem.at[1]
    )
    half_copy.start()

    a2a_wait(0, sf_recv)
    forward(lambda cc: sf_recv[pl.ds(cc, n, stride=8), :], spec_s)
    forward(lambda cc: sf_recv[pl.ds(PER + cc, n, stride=8), :], spec_f)
    s_re, s_im = spec_s[:, :LANES], spec_s[:, LANES:]
    f_re, f_im = spec_f[:, :LANES], spec_f[:, LANES:]
    spread_channels(c_send, inverse(s_re * f_re - s_im * f_im, s_re * f_im + s_im * f_re))
    a2a_start(1, c_send, c_recv, block)

    d_copy.wait()
    back_rank = (2.0 * (d_send[...] + d_recv[...]) * keep).astype(BF)

    half_copy.wait_recv()
    if ny > 1:
        rest = w_far.at[pl.ds(0, (ny - 1) * slice_rows), :]
        pltpu.make_async_copy(rest, rest, wy_recv_sem).wait()
    far_part = dot_t(m_far[...].reshape(nx * LANES, far_cols), w_far[...])
    far_send[...] = far_part[LANES:].astype(BF)
    own_part = own_part + far_part[:LANES]
    far_copies = []
    for d in range(1, nx):
        copy = pltpu.make_async_remote_copy(
            src_ref=far_send.at[pl.ds((d - 1) * LANES, LANES), :], dst_ref=far_recv.at[d - 1],
            send_sem=fr_send_sem.at[d], recv_sem=fr_recv_sem,
            device_id=(dp, member(zl * nx + lax.rem(x + nx - d, nx)), ch), device_id_type=MESH,
        )
        copy.start()
        far_copies.append(copy)

    mine = project(0)
    for sub in range(1, SUB):
        after = project(sub)
        give_back(sub - 1, mine)
        mine = after
    give_back(SUB - 1, mine)

    a2a_wait(1, c_recv)
    inner_t = gather_channels(c_recv) + skip_t * sig_t[...]
    gated_t = (gate_t[...] * inner_t).astype(BF)
    r_send[...] = dot(down_sel, gated_t)
    r_copy = to_chan(r_send, r_recv, r_sem.at[0], r_sem.at[1])
    r_copy.start()
    b_send[:, half:half + width] = dot_t(back_rank, gated_t).astype(BF)

    grad_y = own_part + received(pre0_copy, pre0_recv)
    pltpu.make_async_copy(ret_recv, ret_recv, ret_recv_sem).wait()
    pltpu.make_async_copy(far_recv, far_recv, fr_recv_sem).wait()
    for k in range(2):
        grad_y = grad_y + ret_recv[k].astype(F32)
    for k in range(nx - 1):
        grad_y = grad_y + far_recv[k].astype(F32)
    grad_y = grad_y.T * live_row + dot_0(down_sel, back_rank)
    grad_u = grad_y * gate_t[...]
    gradu_t[...] = grad_u
    for cc in range(PER):
        u_stage[:, cc, :] = gradu_t[cc * n:(cc + 1) * n, :]
    u_send[...] = u_stage[...].astype(BF)
    a2a_start(2, u_send, u_recv, block)
    r_copy.wait()
    fwd_rank = (2.0 * (r_send[...] + r_recv[...]) * keep).astype(BF)
    b_send[:, :half] = dot(fwd_rank, masked[...]).astype(BF)

    product = grad_u * sig_t[...]
    high = product.astype(BF)
    low = (product - high.astype(F32)).astype(BF)
    ones = jnp.ones((max_rank, LANES), BF)
    at = half + a_chunks * LANES
    b_send[:, at:at + width] = (dot_t(ones, high) + dot_t(ones, low)).astype(BF)

    def share(p, owner):
        src = b_send.at[:, pl.ds(pl.multiple_of(p * LANES, LANES), LANES)]
        dst = b_recv.at[pl.ds(pl.multiple_of(me * 16, 16), 16), :]

        @pl.when(owner != me)
        def _():
            pltpu.make_async_remote_copy(
                src_ref=src, dst_ref=dst, send_sem=b_sem.at[0], recv_sem=b_sem.at[1],
                device_id=(dp, owner, ch), device_id_type=MESH,
            ).start()

        @pl.when(owner == me)
        def _():
            pltpu.make_async_copy(src, dst, b_sem.at[1]).start()

    def share_main(d, _):
        p = lax.rem(me + d, plane)
        share(p, p)
        return 0

    for k in range(extras):
        share(plane + k, plane + (k % ny) * nx + k // ny)
    lax.fori_loop(0, plane, share_main, 0, unroll=4 if n == 64 else 1)

    ggat_ref[...] = (grad_y * inner_t).T.astype(BF)
    outs = [
        pltpu.make_async_copy(s, d, out_sem.at[i])
        for i, (s, d) in enumerate((
            (ggat_ref, ggat_hbm), (gsig_ref, gsig_hbm), (gfilt_ref, gfilt_hbm), (g_recv, gbank_hbm),
        ))
    ]
    outs[0].start()

    a2a_wait(2, u_recv)
    u_back[...] = u_recv[...].astype(F32)
    forward(lambda cc: u_back[:, cc, :], spec_g)
    g_re, g_im = spec_g[:, :LANES], spec_g[:, LANES:]
    s_re, s_im = spec_s[:, :LANES], spec_s[:, LANES:]
    spread_channels(ks_stage, inverse(g_re * s_re + g_im * s_im, g_im * s_re - g_re * s_im))
    ks_send[...] = ks_stage[...].astype(BF)
    a2a_start(3, ks_send, ks_recv, block)

    column = zl * plane + x * ny
    is_owner = column + y < n_own

    def q_copy(step):
        return pltpu.make_async_remote_copy(
            src_ref=q_send, dst_ref=q_recv.at[step - 1], send_sem=q_send_sem.at[step],
            recv_sem=q_recv_sem, device_id=(lax.rem(dp + step, 4), me, ch), device_id_type=MESH,
        )

    @pl.when(is_owner)
    def _():
        pltpu.make_async_copy(b_recv, b_recv, b_sem.at[1]).wait()
        acc = b_recv[0:16, :].astype(F32)
        for i in range(1, n):
            acc = acc + b_recv[16 * i:16 * (i + 1), :].astype(F32)
        q_send[...] = jnp.concatenate([acc * pick0, acc * pick1], axis=0)
        for step in (1, 3, 2):
            q_copy(step).start()

    f_re, f_im = spec_f[:, :LANES], spec_f[:, LANES:]
    spread_channels(kf_stage, inverse(g_re * f_re + g_im * f_im, g_im * f_re - g_re * f_im))
    kf_send[...] = kf_stage[...].astype(BF)
    a2a_start(4, kf_send, kf_recv, block)

    g_size = 2 * max_rank
    bank_rows = pl.ds(pl.multiple_of((column + y) * g_size, g_size), g_size)

    @pl.when(is_owner)
    def _():
        pltpu.make_async_copy(q_recv, q_recv, q_recv_sem).wait()
        g_send[...] = (q_send[...] + q_recv[0] + q_recv[1] + q_recv[2]).astype(BF)
        for k in range(1, ny):
            pltpu.make_async_remote_copy(
                src_ref=g_send, dst_ref=g_recv.at[bank_rows, :], send_sem=g_sem.at[0], recv_sem=g_sem.at[1],
                device_id=(dp, zl * plane + lax.rem(y + k, ny) * nx + x, ch), device_id_type=MESH,
            ).start()
        pltpu.make_async_copy(g_send, g_recv.at[bank_rows, :], g_sem.at[1]).start()

    a2a_wait(3, ks_recv)
    quarter = width // 4
    ks_back[...] = ks_recv[...].astype(F32)
    corr_st[...] = gather_channels(ks_back)
    f_send[...] = corr_st[...].astype(BF)
    f_copies = []
    for step in (1, 3, 2):
        q = lax.rem(dp + step, 4)
        copy = pltpu.make_async_remote_copy(
            src_ref=f_send.at[pl.ds(pl.multiple_of(q * quarter, quarter), quarter), :],
            dst_ref=f_recv.at[step - 1], send_sem=f_send_sem.at[step], recv_sem=f_recv_sem,
            device_id=(q, me, ch), device_id_type=MESH,
        )
        copy.start()
        f_copies.append(copy)

    columns = [(zl == 0, ny)] + [
        ((zl == 1) & (x == k), max(0, min(ny, extras - k * ny))) for k in range(nx)
    ]

    def block_copy(k, count):
        rows_of = pl.ds(pl.multiple_of(column * g_size, g_size), count * g_size)
        return pltpu.make_async_remote_copy(
            src_ref=g_recv.at[rows_of, :], dst_ref=g_recv.at[rows_of, :],
            send_sem=g_sem.at[2], recv_sem=g_sem.at[3],
            device_id=(dp, member(lax.rem(g + k, group)), ch), device_id_type=MESH,
        )

    for here, count in columns:
        if count:
            @pl.when(here)
            def _():
                part = g_recv.at[pl.ds(0, count * g_size), :]
                pltpu.make_async_copy(part, part, g_sem.at[1]).wait()
                for k in range(1, group):
                    block_copy(k, count).start()

    a2a_wait(4, kf_recv)
    kf_back[...] = kf_recv[...].astype(F32)
    gsig_ref[...] = (gather_channels(kf_back) + skip_t * gradu_t[...]).T.astype(BF)
    outs[1].start()

    pltpu.make_async_copy(f_recv, f_recv, f_recv_sem).wait()
    my_quarter = pl.ds(pl.multiple_of(dp * quarter, quarter), quarter)
    sums = corr_st[my_quarter, :]
    for k in range(3):
        sums = sums + f_recv[k].astype(F32)
    h_send[...] = sums.astype(BF)
    h_copies = []
    for step in (1, 3, 2):
        copy = pltpu.make_async_remote_copy(
            src_ref=h_send, dst_ref=h_recv.at[my_quarter, :], send_sem=h_send_sem.at[step],
            recv_sem=h_recv_sem, device_id=(lax.rem(dp + step, 4), me, ch), device_id_type=MESH,
        )
        copy.start()
        h_copies.append(copy)
    pltpu.make_async_copy(h_send, h_recv.at[my_quarter, :], h_recv_sem).start()

    pltpu.make_async_copy(h_recv, h_recv, h_recv_sem).wait()
    gfilt_ref[...] = h_recv[...].astype(F32).T
    outs[2].start()

    for here, count in columns:
        @pl.when(here)
        def _():
            part = g_recv.at[pl.ds(0, (n_own - count) * g_size), :]
            pltpu.make_async_copy(part, part, g_sem.at[3]).wait()
    outs[3].start()

    for sub in range(SUB):
        for qq in range(2):
            for hh in range(2):
                @pl.when(to_other(qq))
                def _():
                    cot_copy(sub, qq, hh).wait_send()
    for qq in range(2):
        for hh in range(2):
            @pl.when((2 * ch + qq == dp) & (ch != hh))
            def _():
                own_copy(qq, hh).wait_send()
    a2a_wait_send(0, sf_send, 8)
    for k, src in ((1, c_send), (2, u_send), (3, ks_send), (4, kf_send)):
        a2a_wait_send(k, src, 1)
    w_copy.wait_send()
    pre0_copy.wait_send()
    wf_copy.wait_send()
    half_copy.wait_send()
    for copy in wy_copies + far_copies + pre_copies + ret_copies + f_copies + h_copies:
        copy.wait_send()

    @pl.when(holds_far)
    def _():
        def sent(d, _):
            part = m_far.at[0, pl.ds(0, half_rows)]
            pltpu.make_async_copy(part, part, far_sem.at[0]).wait()
            return 0

        lax.fori_loop(1, 2 * nx, sent, 0)

    def b_sent(count):
        part = b_send.at[:, pl.ds(0, count * LANES)]
        pltpu.make_async_copy(part, part, b_sem.at[0]).wait()

    @pl.when(is_owner)
    def _():
        b_sent(n_own - 1)
        for step in (1, 3, 2):
            q_copy(step).wait_send()
        for _ in range(1, ny):
            pltpu.make_async_copy(g_send, g_send, g_sem.at[0]).wait()

    @pl.when(jnp.logical_not(is_owner))
    def _():
        b_sent(n_own)

    for here, count in columns:
        if count:
            @pl.when(here)
            def _():
                for k in range(1, group):
                    block_copy(k, count).wait_send()

    for out in outs:
        out.wait()


def received(copy, ref):
    copy.wait_recv()
    return ref[...].astype(F32)


def finish_kernel(
    ny,
    gsig_in, ggat_in, gfilt_in, gbank_in,
    gsig_out, ggat_out, gfilt_out, gskip_out, ga_out, gb_out,
    gsig_ref, ggat_ref, gfilt_ref, gbank_ref, gskip_ref, ga_ref, gb_ref, in_sem, out_sem,
):
    max_rank, half = gb_ref.shape[1:]
    width = ga_ref.shape[2]
    g_size = 2 * max_rank
    up_chunks = half // LANES
    nx = up_chunks // ny
    a_chunks = -(-width // LANES)
    pairs = ((gbank_in, gbank_ref), (gfilt_in, gfilt_ref), (gsig_in, gsig_ref), (ggat_in, ggat_ref))
    loads = [pltpu.make_async_copy(s, d, in_sem.at[i]) for i, (s, d) in enumerate(pairs)]
    for load in loads:
        load.start()
    pairs = (
        (gb_ref, gb_out), (gfilt_ref, gfilt_out), (gsig_ref, gsig_out), (ggat_ref, ggat_out),
        (gskip_ref, gskip_out), (ga_ref, ga_out),
    )
    stores = [pltpu.make_async_copy(s, d, out_sem.at[i]) for i, (s, d) in enumerate(pairs)]
    loads[0].wait()
    for p in range(up_chunks):
        at = ((p % nx) * ny + p // nx) * g_size
        block = gbank_ref[at:at + g_size, :].astype(F32)
        gb_ref[0, :, p * LANES:(p + 1) * LANES] = block[:max_rank]
        gb_ref[1, :, p * LANES:(p + 1) * LANES] = block[max_rank:]
    stores[0].start()
    for k in range(1, 4):
        loads[k].wait()
        stores[k].start()
    size = min(LANES, width)
    for k in range(a_chunks):
        at = (up_chunks + k) * g_size
        block = gbank_ref[at:at + g_size, :].astype(F32)
        ga_ref[0, :, k * size:(k + 1) * size] = block[:max_rank, :size]
        ga_ref[1, :, k * size:(k + 1) * size] = block[max_rank:, :size]
        at = (up_chunks + a_chunks + k) * g_size
        block = gbank_ref[at:at + g_size, :].astype(F32)
        gskip_ref[:, k * size:(k + 1) * size] = (block[0:1] + block[max_rank:max_rank + 1])[:, :size]
    stores[4].start()
    stores[5].start()
    for store in stores:
        store.wait()


def local(
    signal, gating, cotangent, filt, skip, output_projection,
    adapter_down_bank, adapter_up_bank, adapter_index, sequence_rank, real_length,
):
    n = lax.axis_size("seq")
    width = signal.shape[2]
    half = cotangent.shape[2]
    cols = output_projection.shape[1] // 2
    max_rank = adapter_up_bank.shape[1]
    a_chunks = -(-width // LANES)
    n_own = half // LANES + 2 * a_chunks
    piece = LANES // SUB
    nx = min(4, n // 2)
    far_cols = 2 * cols // nx
    consts = [jnp.asarray(t) for t in tables(n)]
    rows = consts[4].shape[0]
    vmem = pl.BlockSpec(memory_space=pltpu.VMEM)
    smem = pl.BlockSpec(memory_space=pltpu.SMEM)
    hbm = pl.BlockSpec(memory_space=pltpu.HBM)
    dma = pltpu.SemaphoreType.DMA
    arrays = [
        signal[0], gating[0], cotangent[0], filt, skip[None], output_projection,
        jnp.swapaxes(adapter_down_bank, 1, 2), adapter_up_bank, *consts,
    ]
    block = pltpu.VMEM((n, PER, LANES), F32)
    narrow = pltpu.VMEM((n, PER, LANES), BF)
    eight = pltpu.VMEM((8 * n, LANES), F32)
    wide = pltpu.VMEM((width, LANES), F32)
    spec = pltpu.VMEM((PER * rows, 2 * LANES), F32)
    rank = pltpu.VMEM((max_rank, LANES), F32)
    outs = pl.pallas_call(
        functools.partial(kernel, n),
        out_shape=(
            jax.ShapeDtypeStruct((LANES, width), BF),
            jax.ShapeDtypeStruct((LANES, width), BF),
            jax.ShapeDtypeStruct((LANES, width), F32),
            jax.ShapeDtypeStruct((2 * max_rank * n_own, LANES), BF),
        ),
        in_specs=[smem] * 3 + [hbm] * len(arrays),
        out_specs=(hbm,) * 4,
        scratch_shapes=[
            pltpu.VMEM((LANES, width), BF),
            pltpu.VMEM((LANES, width), BF),
            pltpu.VMEM((LANES, width), F32),
        ] + [pltpu.VMEM(a.shape, a.dtype) for a in arrays] + [
            pltpu.VMEM((LANES, half), BF),
            wide, wide, wide, spec, spec, spec,
            eight, eight, block, block, narrow, narrow, narrow, narrow, narrow, narrow,
            block, block, block, block, block, block,
            pltpu.VMEM((LANES, cols), BF),
            pltpu.VMEM((SUB, 2, piece, cols), BF),
            pltpu.VMEM((nx, LANES, far_cols), BF),
            pltpu.VMEM((width, far_cols), BF),
            pltpu.VMEM(((nx - 1) * LANES, width), BF),
            pltpu.VMEM((nx - 1, LANES, width), BF),
            pltpu.VMEM((width, cols), BF),
            pltpu.VMEM((LANES, width), BF),
            pltpu.VMEM((LANES, width), BF),
            pltpu.VMEM((SUB, 2 * piece, width), BF),
            pltpu.VMEM((SUB, 2 * piece, width), BF),
            pltpu.VMEM((SUB, 2 * piece, width), BF),
            pltpu.VMEM((2, LANES, width), BF),
            rank, rank, rank, rank,
            pltpu.VMEM((max_rank, n_own * LANES), BF),
            pltpu.VMEM((16 * n, LANES), BF),
            pltpu.VMEM((2 * max_rank, LANES), F32),
            pltpu.VMEM((3, 2 * max_rank, LANES), F32),
            pltpu.VMEM((2 * max_rank, LANES), BF),
            pltpu.VMEM((2 * max_rank * n_own, LANES), BF),
            pltpu.VMEM((width, LANES), BF),
            pltpu.VMEM((3, width // 4, LANES), BF),
            wide,
            pltpu.VMEM((width // 4, LANES), BF),
            pltpu.VMEM((width, LANES), BF),
            dma((len(arrays),)), dma((4,)), dma((5,)), dma((5,)), dma((SUB, 4)), dma((SUB,)), dma((2,)), dma((2,)),
            dma((2,)), dma((SUB,)), dma((SUB,)), dma((SUB, 4)), dma, dma((2,)), dma((2,)), dma((2,)),
            dma((4,)), dma, dma((4,)), dma((4,)), dma,
            dma((4,)), dma, dma((2,)), dma((2,)), dma((2,)), dma((8,)), dma, dma((nx,)), dma,
        ],
        compiler_params=pltpu.CompilerParams(
            collective_id=0, has_side_effects=True, vmem_limit_bytes=VMEM_LIMIT
        ),
    )(adapter_index, sequence_rank, real_length, *arrays)
    grad_signal, grad_gating, grad_filt, grad_skip, grad_a, grad_b = pl.pallas_call(
        functools.partial(finish_kernel, n // (2 * nx)),
        out_shape=(
            jax.ShapeDtypeStruct((LANES, width), BF),
            jax.ShapeDtypeStruct((LANES, width), BF),
            jax.ShapeDtypeStruct((LANES, width), F32),
            jax.ShapeDtypeStruct((1, width), F32),
            jax.ShapeDtypeStruct((2, max_rank, width), F32),
            jax.ShapeDtypeStruct((2, max_rank, half), F32),
        ),
        in_specs=[hbm] * 4,
        out_specs=(hbm,) * 6,
        scratch_shapes=[
            pltpu.VMEM((LANES, width), BF), pltpu.VMEM((LANES, width), BF), pltpu.VMEM((LANES, width), F32),
            pltpu.VMEM((2 * max_rank * n_own, LANES), BF), pltpu.VMEM((1, width), F32),
            pltpu.VMEM((2, max_rank, width), F32), pltpu.VMEM((2, max_rank, half), F32),
            dma((4,)), dma((6,)),
        ],
        compiler_params=pltpu.CompilerParams(vmem_limit_bytes=VMEM_LIMIT),
    )(*outs)
    return (grad_signal[None], grad_gating[None], grad_filt, grad_skip[0], jnp.swapaxes(grad_a, 1, 2), grad_b)


def solution(mesh):
    placed = (
        P("dp", "seq", "chan"), P("dp", "seq", "chan"), P("dp", "seq", "chan"), P("seq", "chan"),
        P("chan"), P("chan", "dp"), P(None, "chan", None), P(None, None, "chan"),
        P("dp"), P("dp"), P("dp"),
    )
    return jax.shard_map(
        local,
        mesh=mesh,
        in_specs=placed,
        out_specs=(
            P("dp", "seq", "chan"), P("dp", "seq", "chan"), P("seq", "chan"), P("chan"),
            P(None, "chan", None), P(None, None, "chan"),
        ),
        check_vma=False,
    )
```

```python
import functools
import math

import jax
import jax.numpy as jnp
import ml_dtypes
import numpy as np
from jax import lax
from jax.experimental import pallas as pl
from jax.experimental.pallas import tpu as pltpu
from jax.sharding import PartitionSpec as P

MESH = pl.DeviceIdType.MESH
BF = jnp.bfloat16
F32 = jnp.float32
LANES = 128
PER = 4
VMEM_LIMIT = 62 * 1024 * 1024
SUB = 2


def split3(table, axis, order):
    high = table.astype(ml_dtypes.bfloat16)
    low = (table - high.astype(np.float64)).astype(ml_dtypes.bfloat16)
    return np.concatenate([high if o else low for o in order], axis=axis)


def tables(n):
    rows = -(-(n + 1) // 8) * 8
    k1 = np.arange(rows)
    used = (k1 <= n).astype(np.float64)
    i = np.arange(n)
    a = np.arange(LANES)
    period = 2 * n * LANES
    th1 = 2 * math.pi * (k1[:, None] * i[None, :] % (2 * n)) / (2 * n)
    first = np.concatenate([np.cos(th1) * used[:, None], -np.sin(th1) * used[:, None]], 0)
    thw = 2 * math.pi * (k1[:, None] * a[None, :] % period) / period
    tw_cos, tw_sin = np.cos(thw), np.sin(thw)
    th2 = 2 * math.pi * (a[:, None] * a[None, :] % LANES) / LANES
    c2, s2 = np.cos(th2), np.sin(th2)
    second = np.block([[c2, -s2], [s2, c2]])
    second_back = np.block([[c2, s2], [-s2, c2]])
    weight = used * np.where((k1 == 0) | (k1 == n), 1.0, 2.0) / period
    last = np.concatenate([np.cos(th1).T * weight, -np.sin(th1).T * weight], 1)
    return (
        split3(first, 1, (1, 1, 0)),
        split3(second, 0, (1, 1, 0)),
        split3(second_back, 0, (1, 1, 0)),
        split3(last, 1, (1, 1, 0)),
        tw_cos.astype(np.float32),
        tw_sin.astype(np.float32),
    )


def split_data(x, axis):
    high = x.astype(BF)
    low = (x - high.astype(F32)).astype(BF)
    return jnp.concatenate([high, low, high], axis=axis)


def dot(a, b):
    return jnp.dot(a, b, preferred_element_type=F32)


def dot_t(a, b):
    return lax.dot_general(a, b, (((1,), (1,)), ((), ())), preferred_element_type=F32)


def dot_0(a, b):
    return lax.dot_general(a, b, (((0,), (0,)), ((), ())), preferred_element_type=F32)


def kernel(
    n,
    index_ref, rank_ref, length_ref,
    signal_hbm, gating_hbm, cot_hbm, filt_hbm, skip_hbm, w_hbm, down_hbm, up_hbm,
    t1_hbm, t2_hbm, t2b_hbm, t1b_hbm, tc_hbm, ts_hbm,
    gsig_hbm, ggat_hbm, gfilt_hbm, gbank_hbm,
    gsig_ref, ggat_ref, gfilt_ref,
    signal_ref, gating_ref, cot_ref, filt_ref, skip_ref, w_ref, down_ref, up_ref,
    t1_ref, t2_ref, t2b_ref, t1b_ref, tc_ref, ts_ref,
    masked, sig_t, gate_t, gradu_t, spec_s, spec_f, spec_g,
    sf_send, sf_recv, c_send, c_recv, u_send, u_recv, ks_send, ks_recv, kf_send, kf_recv,
    u_stage, u_back, ks_stage, ks_back, kf_stage, kf_back,
    m_own, m_recv, m_far, w_far, far_send, far_recv, w_recv, pre0_send, pre0_recv, pre_send, pre_recv, ret_send, ret_recv,
    d_send, d_recv, r_send, r_recv,
    b_send, b_recv, q_send, q_recv, g_send, g_recv, f_send, f_recv, corr_st, h_send, h_recv,
    in_sem, out_sem, a2a_send_sem, a2a_recv_sem, m_send_sem, m_recv_sem, own_sem, w_sem, pre0_sem,
    pre_send_sem, pre_recv_sem, ret_send_sem, ret_recv_sem, d_sem, r_sem, b_sem,
    q_send_sem, q_recv_sem, g_sem, f_send_sem, f_recv_sem,
    h_send_sem, h_recv_sem, far_sem, wf_sem, wy_send_sem, wy_recv_sem, fr_send_sem, fr_recv_sem,
):
    dp = lax.axis_index("dp")
    me = lax.axis_index("seq")
    ch = lax.axis_index("chan")
    other = 1 - ch
    plane = n // 2
    zl, spot = lax.div(me, plane), lax.rem(me, plane)
    nx = m_far.shape[0]
    group = 2 * nx
    ny = plane // nx
    y, x = lax.div(spot, nx), lax.rem(spot, nx)
    g = zl * nx + x
    far_cols = m_far.shape[2]

    def member(k):
        return lax.div(k, nx) * plane + y * nx + lax.rem(k, nx)

    width = w_ref.shape[0]
    cols = w_ref.shape[1] // 2
    half = cot_ref.shape[1]
    piece = LANES // SUB
    n_own = b_send.shape[1] // LANES
    extras = n_own - n // 2
    rows = t1_ref.shape[0] // 2
    a_chunks = -(-width // LANES)

    pairs = (
        (signal_hbm, signal_ref), (filt_hbm, filt_ref), (cot_hbm, cot_ref), (up_hbm, up_ref),
        (w_hbm, w_ref), (t1_hbm, t1_ref), (t2_hbm, t2_ref), (t2b_hbm, t2b_ref), (t1b_hbm, t1b_ref),
        (tc_hbm, tc_ref), (ts_hbm, ts_ref), (gating_hbm, gating_ref), (down_hbm, down_ref),
        (skip_hbm, skip_ref),
    )
    loads = [pltpu.make_async_copy(s, d, in_sem.at[i]) for i, (s, d) in enumerate(pairs)]
    for load in loads:
        load.start()

    barrier = pltpu.get_barrier_semaphore()
    for d in range(4):
        for z in range(2):
            for c in range(2):
                if d or c:
                    pl.semaphore_signal(
                        barrier, inc=1,
                        device_id=(lax.rem(dp + d, 4), lax.rem(zl + z, 2) * plane + spot, lax.rem(ch + c, 2)),
                        device_id_type=MESH,
                    )

    def greet(d, _):
        pl.semaphore_signal(
            barrier, inc=1, device_id=(dp, lax.rem(me + d, n), ch), device_id_type=MESH
        )
        return 0

    lax.fori_loop(1, n, greet, 0, unroll=9 if n == 64 else 1)
    for z in range(2):
        for k in range(1, nx):
            pl.semaphore_signal(
                barrier, inc=1, device_id=(dp, member(z * nx + lax.rem(x + k, nx)), other),
                device_id_type=MESH,
            )

    loads[0].wait()
    loads[1].wait()
    sig_t[...] = signal_ref[...].astype(F32).T
    filt_t = filt_ref[...].T
    for cc in range(PER):
        sf_send[pl.ds(cc, n, stride=8), :] = sig_t[cc * n:(cc + 1) * n, :]
        sf_send[pl.ds(PER + cc, n, stride=8), :] = filt_t[cc * n:(cc + 1) * n, :]
    real_length = length_ref[0]
    live_col = (me * LANES + lax.broadcasted_iota(jnp.int32, (LANES, 1), 0) < real_length).astype(F32)
    live_row = (me * LANES + lax.broadcasted_iota(jnp.int32, (1, LANES), 1) < real_length).astype(F32)
    pick1 = index_ref[0].astype(F32)
    pick0 = 1.0 - pick1

    pl.semaphore_wait(barrier, n - 1 + 14 + 2 * (nx - 1))

    def a2a_start(k, src, dst, at):
        def body(d, _):
            j = lax.rem(me + d, n)
            pltpu.make_async_remote_copy(
                src_ref=src.at[at(j)],
                dst_ref=dst.at[at(me)],
                send_sem=a2a_send_sem.at[k],
                recv_sem=a2a_recv_sem.at[k],
                device_id=(dp, j, ch),
                device_id_type=MESH,
            ).start()
            return 0

        lax.fori_loop(1, n, body, 0, unroll=9 if n == 64 else 1)
        pltpu.make_async_copy(src.at[at(me)], dst.at[at(me)], a2a_recv_sem.at[k]).start()

    def a2a_wait(k, dst):
        pltpu.make_async_copy(dst, dst, a2a_recv_sem.at[k]).wait()

    def a2a_wait_send(k, src, size):
        part = src.at[pl.ds(0, (n - 1) * size)]
        pltpu.make_async_copy(part, part, a2a_send_sem.at[k]).wait()

    def eight(j):
        return pl.ds(pl.multiple_of(j * 8, 8), 8)

    def block(j):
        return j

    def cot_copy(sub, qq, hh):
        q = 2 * ch + qq
        return pltpu.make_async_remote_copy(
            src_ref=cot_hbm.at[pl.ds(sub * piece, piece), pl.ds((2 * qq + hh) * cols, cols)],
            dst_ref=m_recv.at[sub, zl],
            send_sem=m_send_sem.at[sub, 2 * qq + hh],
            recv_sem=m_recv_sem.at[sub],
            device_id=(q, lax.div(lax.rem(q - dp + 4, 4), 3) * plane + spot, hh),
            device_id_type=MESH,
        )

    def own_copy(qq, hh):
        return pltpu.make_async_remote_copy(
            src_ref=cot_hbm.at[:, pl.ds((2 * qq + hh) * cols, cols)],
            dst_ref=m_own,
            send_sem=own_sem.at[0],
            recv_sem=own_sem.at[1],
            device_id=(dp, me, hh),
            device_id_type=MESH,
        )

    def to_other(qq):
        return lax.rem(2 * ch + qq - dp + 4, 2) == 1

    for sub in range(SUB):
        for qq in range(2):
            for hh in range(2):
                @pl.when(to_other(qq))
                def _():
                    cot_copy(sub, qq, hh).start()
    a2a_start(0, sf_send, sf_recv, eight)

    for qq in range(2):
        for hh in range(2):
            @pl.when((2 * ch + qq == dp) & (ch != hh))
            def _():
                own_copy(qq, hh).start()

            @pl.when((2 * ch + qq == dp) & (ch == hh))
            def _():
                pltpu.make_async_copy(
                    cot_hbm.at[:, pl.ds((2 * qq + hh) * cols, cols)], m_own, own_sem.at[1]
                ).start()

    far = lax.rem(dp + 2, 4)
    slice_rows = width // ny
    my_slice = pl.ds(pl.multiple_of(y * slice_rows, slice_rows), slice_rows)

    wf_copy = pltpu.make_async_remote_copy(
        src_ref=w_hbm.at[my_slice, pl.ds(pl.multiple_of(x * far_cols, far_cols), far_cols)],
        dst_ref=w_far.at[my_slice, :],
        send_sem=wf_sem.at[0], recv_sem=wf_sem.at[1], device_id=(far, me, ch), device_id_type=MESH,
    )
    wf_copy.start()

    def far_copy(d, c):
        k = lax.rem(x + d, nx)
        at = lax.rem(far, 2) * 2 * cols + k * far_cols
        src = cot_hbm.at[:, pl.ds(pl.multiple_of(at, far_cols), far_cols)]
        if d == 0 and c == 0:
            return pltpu.make_async_copy(src, m_far.at[d], far_sem.at[1])
        return pltpu.make_async_remote_copy(
            src_ref=src, dst_ref=m_far.at[d], send_sem=far_sem.at[0], recv_sem=far_sem.at[1],
            device_id=(dp, member(zl * nx + k), lax.rem(ch + c, 2)), device_id_type=MESH,
        )

    holds_far = ch == lax.div(far, 2)

    @pl.when(holds_far)
    def _():
        for d in range(nx):
            for c in range(2):
                far_copy(d, c).start()

    def to_chan(src, dst, send_sem, recv_sem):
        return pltpu.make_async_remote_copy(
            src_ref=src, dst_ref=dst, send_sem=send_sem, recv_sem=recv_sem,
            device_id=(dp, me, other), device_id_type=MESH,
        )

    w_copy = to_chan(
        w_hbm.at[:, pl.ds(pl.multiple_of(other * cols, LANES), cols)], w_recv, w_sem.at[0], w_sem.at[1]
    )
    w_copy.start()

    wf_copy.wait_recv()
    wy_copies = []
    for k in range(1, ny):
        copy = pltpu.make_async_remote_copy(
            src_ref=w_far.at[my_slice, :], dst_ref=w_far.at[my_slice, :],
            send_sem=wy_send_sem.at[k], recv_sem=wy_recv_sem,
            device_id=(dp, zl * plane + lax.rem(y + k, ny) * nx + x, ch), device_id_type=MESH,
        )
        copy.start()
        wy_copies.append(copy)

    for load in loads[2:]:
        load.wait()
    masked[...] = (cot_ref[...].astype(F32) * live_col).astype(BF)
    up_sel = (up_ref[0].astype(F32) * pick0 + up_ref[1].astype(F32) * pick1).astype(BF)
    down_sel = (down_ref[0].astype(F32) * pick0 + down_ref[1].astype(F32) * pick1).astype(BF)
    max_rank = up_sel.shape[0]
    keep = (lax.broadcasted_iota(jnp.int32, (max_rank, LANES), 0) < rank_ref[0]).astype(F32)
    d_send[...] = dot_t(up_sel, masked[...])
    d_copy = to_chan(d_send, d_recv, d_sem.at[0], d_sem.at[1])
    d_copy.start()
    gate_t[...] = gating_ref[...].astype(F32).T
    skip_t = jnp.broadcast_to(skip_ref[...], (LANES, width)).T

    own_cols = pl.ds(pl.multiple_of(ch * cols, LANES), cols)
    pltpu.make_async_copy(m_own, m_own, own_sem.at[1]).wait()
    w_copy.wait_recv()
    pre0_send[...] = dot_t(m_own[...], w_recv[...]).astype(BF)
    pre0_copy = to_chan(pre0_send, pre0_recv, pre0_sem.at[0], pre0_sem.at[1])
    pre0_copy.start()
    own_part = dot_t(m_own[...], w_ref[:, own_cols])

    pre_copies, ret_copies = [], []

    def project(sub):
        pltpu.make_async_copy(m_recv.at[sub], m_recv.at[sub], m_recv_sem.at[sub]).wait()
        part = m_recv[sub].reshape(2 * piece, cols)
        pre_send[sub] = dot_t(part, w_recv[...]).astype(BF)
        copy = to_chan(pre_send.at[sub], pre_recv.at[sub], pre_send_sem.at[sub], pre_recv_sem.at[sub])
        copy.start()
        pre_copies.append(copy)
        return dot_t(part, w_ref[:, own_cols])

    def give_back(sub, mine):
        pre_copies[sub].wait_recv()
        ret_send[sub] = (mine + pre_recv[sub].astype(F32)).astype(BF)
        for slot in range(2):
            copy = pltpu.make_async_remote_copy(
                src_ref=ret_send.at[sub, pl.ds(slot * piece, piece)],
                dst_ref=ret_recv.at[zl, pl.ds(sub * piece, piece)],
                send_sem=ret_send_sem.at[sub, slot], recv_sem=ret_recv_sem,
                device_id=(lax.rem(dp + 3 - 2 * zl, 4), slot * plane + spot, ch), device_id_type=MESH,
            )
            copy.start()
            ret_copies.append(copy)

    tc, ts = tc_ref[...], ts_ref[...]

    def forward(load, store):
        x = jnp.concatenate([load(cc) for cc in range(PER)], axis=1)
        y = dot(t1_ref[...], split_data(x, 0))
        parts = []
        for cc in range(PER):
            re = y[:rows, cc * LANES:(cc + 1) * LANES]
            im = y[rows:, cc * LANES:(cc + 1) * LANES]
            parts.append(jnp.concatenate([re * tc + im * ts, im * tc - re * ts], axis=1))
        store[...] = dot(split_data(jnp.concatenate(parts, axis=0), 1), t2_ref[...])

    def inverse(re, im):
        q = dot(split_data(jnp.concatenate([re, im], axis=1), 1), t2b_ref[...])
        parts = []
        for cc in range(PER):
            qr = q[cc * rows:(cc + 1) * rows, :LANES]
            qi = q[cc * rows:(cc + 1) * rows, LANES:]
            parts.append(jnp.concatenate([qr * tc - qi * ts, qi * tc + qr * ts], axis=0))
        return dot(t1b_ref[...], split_data(jnp.concatenate(parts, axis=1), 0))

    def spread_channels(dst, values):
        for cc in range(PER):
            dst[:, cc, :] = values[:, cc * LANES:(cc + 1) * LANES]

    def gather_channels(src):
        return jnp.concatenate([src[:, cc, :] for cc in range(PER)], axis=0)

    a2a_wait(0, sf_recv)
    forward(lambda cc: sf_recv[pl.ds(cc, n, stride=8), :], spec_s)
    forward(lambda cc: sf_recv[pl.ds(PER + cc, n, stride=8), :], spec_f)
    s_re, s_im = spec_s[:, :LANES], spec_s[:, LANES:]
    f_re, f_im = spec_f[:, :LANES], spec_f[:, LANES:]
    spread_channels(c_send, inverse(s_re * f_re - s_im * f_im, s_re * f_im + s_im * f_re))
    a2a_start(1, c_send, c_recv, block)

    d_copy.wait()
    back_rank = (2.0 * (d_send[...] + d_recv[...]) * keep).astype(BF)

    pltpu.make_async_copy(m_far, m_far, far_sem.at[1]).wait()
    if ny > 1:
        rest = w_far.at[pl.ds(0, (ny - 1) * slice_rows), :]
        pltpu.make_async_copy(rest, rest, wy_recv_sem).wait()
    far_part = dot_t(m_far[...].reshape(nx * LANES, far_cols), w_far[...])
    far_send[...] = far_part[LANES:].astype(BF)
    own_part = own_part + far_part[:LANES]
    far_copies = []
    for d in range(1, nx):
        copy = pltpu.make_async_remote_copy(
            src_ref=far_send.at[pl.ds((d - 1) * LANES, LANES), :], dst_ref=far_recv.at[d - 1],
            send_sem=fr_send_sem.at[d], recv_sem=fr_recv_sem,
            device_id=(dp, member(zl * nx + lax.rem(x + nx - d, nx)), ch), device_id_type=MESH,
        )
        copy.start()
        far_copies.append(copy)

    mine = project(0)
    for sub in range(1, SUB):
        after = project(sub)
        give_back(sub - 1, mine)
        mine = after
    give_back(SUB - 1, mine)

    a2a_wait(1, c_recv)
    inner_t = gather_channels(c_recv) + skip_t * sig_t[...]
    gated_t = (gate_t[...] * inner_t).astype(BF)
    r_send[...] = dot(down_sel, gated_t)
    r_copy = to_chan(r_send, r_recv, r_sem.at[0], r_sem.at[1])
    r_copy.start()
    b_send[:, half:half + width] = dot_t(back_rank, gated_t).astype(BF)

    grad_y = own_part + received(pre0_copy, pre0_recv)
    pltpu.make_async_copy(ret_recv, ret_recv, ret_recv_sem).wait()
    pltpu.make_async_copy(far_recv, far_recv, fr_recv_sem).wait()
    for k in range(2):
        grad_y = grad_y + ret_recv[k].astype(F32)
    for k in range(nx - 1):
        grad_y = grad_y + far_recv[k].astype(F32)
    grad_y = grad_y.T * live_row + dot_0(down_sel, back_rank)
    grad_u = grad_y * gate_t[...]
    gradu_t[...] = grad_u
    for cc in range(PER):
        u_stage[:, cc, :] = gradu_t[cc * n:(cc + 1) * n, :]
    u_send[...] = u_stage[...].astype(BF)
    a2a_start(2, u_send, u_recv, block)
    r_copy.wait()
    fwd_rank = (2.0 * (r_send[...] + r_recv[...]) * keep).astype(BF)
    b_send[:, :half] = dot(fwd_rank, masked[...]).astype(BF)

    product = grad_u * sig_t[...]
    high = product.astype(BF)
    low = (product - high.astype(F32)).astype(BF)
    ones = jnp.ones((max_rank, LANES), BF)
    at = half + a_chunks * LANES
    b_send[:, at:at + width] = (dot_t(ones, high) + dot_t(ones, low)).astype(BF)

    def share(p, owner):
        src = b_send.at[:, pl.ds(pl.multiple_of(p * LANES, LANES), LANES)]
        dst = b_recv.at[pl.ds(pl.multiple_of(me * 16, 16), 16), :]

        @pl.when(owner != me)
        def _():
            pltpu.make_async_remote_copy(
                src_ref=src, dst_ref=dst, send_sem=b_sem.at[0], recv_sem=b_sem.at[1],
                device_id=(dp, owner, ch), device_id_type=MESH,
            ).start()

        @pl.when(owner == me)
        def _():
            pltpu.make_async_copy(src, dst, b_sem.at[1]).start()

    def share_main(d, _):
        p = lax.rem(me + d, plane)
        share(p, p)
        return 0

    for k in range(extras):
        share(plane + k, plane + (k % ny) * nx + k // ny)
    lax.fori_loop(0, plane, share_main, 0, unroll=4 if n == 64 else 1)

    ggat_ref[...] = (grad_y * inner_t).T.astype(BF)
    outs = [
        pltpu.make_async_copy(s, d, out_sem.at[i])
        for i, (s, d) in enumerate((
            (ggat_ref, ggat_hbm), (gsig_ref, gsig_hbm), (gfilt_ref, gfilt_hbm), (g_recv, gbank_hbm),
        ))
    ]
    outs[0].start()

    a2a_wait(2, u_recv)
    u_back[...] = u_recv[...].astype(F32)
    forward(lambda cc: u_back[:, cc, :], spec_g)
    g_re, g_im = spec_g[:, :LANES], spec_g[:, LANES:]
    s_re, s_im = spec_s[:, :LANES], spec_s[:, LANES:]
    spread_channels(ks_stage, inverse(g_re * s_re + g_im * s_im, g_im * s_re - g_re * s_im))
    ks_send[...] = ks_stage[...].astype(BF)
    a2a_start(3, ks_send, ks_recv, block)

    column = zl * plane + x * ny
    is_owner = column + y < n_own

    def q_copy(step):
        return pltpu.make_async_remote_copy(
            src_ref=q_send, dst_ref=q_recv.at[step - 1], send_sem=q_send_sem.at[step],
            recv_sem=q_recv_sem, device_id=(lax.rem(dp + step, 4), me, ch), device_id_type=MESH,
        )

    @pl.when(is_owner)
    def _():
        pltpu.make_async_copy(b_recv, b_recv, b_sem.at[1]).wait()
        acc = b_recv[0:16, :].astype(F32)
        for i in range(1, n):
            acc = acc + b_recv[16 * i:16 * (i + 1), :].astype(F32)
        q_send[...] = jnp.concatenate([acc * pick0, acc * pick1], axis=0)
        for step in (1, 3, 2):
            q_copy(step).start()

    f_re, f_im = spec_f[:, :LANES], spec_f[:, LANES:]
    spread_channels(kf_stage, inverse(g_re * f_re + g_im * f_im, g_im * f_re - g_re * f_im))
    kf_send[...] = kf_stage[...].astype(BF)
    a2a_start(4, kf_send, kf_recv, block)

    g_size = 2 * max_rank
    bank_rows = pl.ds(pl.multiple_of((column + y) * g_size, g_size), g_size)

    @pl.when(is_owner)
    def _():
        pltpu.make_async_copy(q_recv, q_recv, q_recv_sem).wait()
        g_send[...] = (q_send[...] + q_recv[0] + q_recv[1] + q_recv[2]).astype(BF)
        for k in range(1, ny):
            pltpu.make_async_remote_copy(
                src_ref=g_send, dst_ref=g_recv.at[bank_rows, :], send_sem=g_sem.at[0], recv_sem=g_sem.at[1],
                device_id=(dp, zl * plane + lax.rem(y + k, ny) * nx + x, ch), device_id_type=MESH,
            ).start()
        pltpu.make_async_copy(g_send, g_recv.at[bank_rows, :], g_sem.at[1]).start()

    a2a_wait(3, ks_recv)
    quarter = width // 4
    ks_back[...] = ks_recv[...].astype(F32)
    corr_st[...] = gather_channels(ks_back)
    f_send[...] = corr_st[...].astype(BF)
    f_copies = []
    for step in (1, 3, 2):
        q = lax.rem(dp + step, 4)
        copy = pltpu.make_async_remote_copy(
            src_ref=f_send.at[pl.ds(pl.multiple_of(q * quarter, quarter), quarter), :],
            dst_ref=f_recv.at[step - 1], send_sem=f_send_sem.at[step], recv_sem=f_recv_sem,
            device_id=(q, me, ch), device_id_type=MESH,
        )
        copy.start()
        f_copies.append(copy)

    columns = [(zl == 0, ny)] + [
        ((zl == 1) & (x == k), max(0, min(ny, extras - k * ny))) for k in range(nx)
    ]

    def block_copy(k, count):
        rows_of = pl.ds(pl.multiple_of(column * g_size, g_size), count * g_size)
        return pltpu.make_async_remote_copy(
            src_ref=g_recv.at[rows_of, :], dst_ref=g_recv.at[rows_of, :],
            send_sem=g_sem.at[2], recv_sem=g_sem.at[3],
            device_id=(dp, member(lax.rem(g + k, group)), ch), device_id_type=MESH,
        )

    for here, count in columns:
        if count:
            @pl.when(here)
            def _():
                part = g_recv.at[pl.ds(0, count * g_size), :]
                pltpu.make_async_copy(part, part, g_sem.at[1]).wait()
                for k in range(1, group):
                    block_copy(k, count).start()

    a2a_wait(4, kf_recv)
    kf_back[...] = kf_recv[...].astype(F32)
    gsig_ref[...] = (gather_channels(kf_back) + skip_t * gradu_t[...]).T.astype(BF)
    outs[1].start()

    pltpu.make_async_copy(f_recv, f_recv, f_recv_sem).wait()
    my_quarter = pl.ds(pl.multiple_of(dp * quarter, quarter), quarter)
    sums = corr_st[my_quarter, :]
    for k in range(3):
        sums = sums + f_recv[k].astype(F32)
    h_send[...] = sums.astype(BF)
    h_copies = []
    for step in (1, 3, 2):
        copy = pltpu.make_async_remote_copy(
            src_ref=h_send, dst_ref=h_recv.at[my_quarter, :], send_sem=h_send_sem.at[step],
            recv_sem=h_recv_sem, device_id=(lax.rem(dp + step, 4), me, ch), device_id_type=MESH,
        )
        copy.start()
        h_copies.append(copy)
    pltpu.make_async_copy(h_send, h_recv.at[my_quarter, :], h_recv_sem).start()

    pltpu.make_async_copy(h_recv, h_recv, h_recv_sem).wait()
    gfilt_ref[...] = h_recv[...].astype(F32).T
    outs[2].start()

    for here, count in columns:
        @pl.when(here)
        def _():
            part = g_recv.at[pl.ds(0, (n_own - count) * g_size), :]
            pltpu.make_async_copy(part, part, g_sem.at[3]).wait()
    outs[3].start()

    for sub in range(SUB):
        for qq in range(2):
            for hh in range(2):
                @pl.when(to_other(qq))
                def _():
                    cot_copy(sub, qq, hh).wait_send()
    for qq in range(2):
        for hh in range(2):
            @pl.when((2 * ch + qq == dp) & (ch != hh))
            def _():
                own_copy(qq, hh).wait_send()
    a2a_wait_send(0, sf_send, 8)
    for k, src in ((1, c_send), (2, u_send), (3, ks_send), (4, kf_send)):
        a2a_wait_send(k, src, 1)
    w_copy.wait_send()
    pre0_copy.wait_send()
    wf_copy.wait_send()
    for copy in wy_copies + far_copies + pre_copies + ret_copies + f_copies + h_copies:
        copy.wait_send()

    @pl.when(holds_far)
    def _():
        def sent(d, _):
            pltpu.make_async_copy(m_far.at[0], m_far.at[0], far_sem.at[0]).wait()
            return 0

        lax.fori_loop(1, 2 * nx, sent, 0)

    def b_sent(count):
        part = b_send.at[:, pl.ds(0, count * LANES)]
        pltpu.make_async_copy(part, part, b_sem.at[0]).wait()

    @pl.when(is_owner)
    def _():
        b_sent(n_own - 1)
        for step in (1, 3, 2):
            q_copy(step).wait_send()
        for _ in range(1, ny):
            pltpu.make_async_copy(g_send, g_send, g_sem.at[0]).wait()

    @pl.when(jnp.logical_not(is_owner))
    def _():
        b_sent(n_own)

    for here, count in columns:
        if count:
            @pl.when(here)
            def _():
                for k in range(1, group):
                    block_copy(k, count).wait_send()

    for out in outs:
        out.wait()


def received(copy, ref):
    copy.wait_recv()
    return ref[...].astype(F32)


def finish_kernel(
    ny,
    gsig_in, ggat_in, gfilt_in, gbank_in,
    gsig_out, ggat_out, gfilt_out, gskip_out, ga_out, gb_out,
    gsig_ref, ggat_ref, gfilt_ref, gbank_ref, gskip_ref, ga_ref, gb_ref, in_sem, out_sem,
):
    max_rank, half = gb_ref.shape[1:]
    width = ga_ref.shape[2]
    g_size = 2 * max_rank
    up_chunks = half // LANES
    nx = up_chunks // ny
    a_chunks = -(-width // LANES)
    pairs = ((gbank_in, gbank_ref), (gfilt_in, gfilt_ref), (gsig_in, gsig_ref), (ggat_in, ggat_ref))
    loads = [pltpu.make_async_copy(s, d, in_sem.at[i]) for i, (s, d) in enumerate(pairs)]
    for load in loads:
        load.start()
    pairs = (
        (gb_ref, gb_out), (gfilt_ref, gfilt_out), (gsig_ref, gsig_out), (ggat_ref, ggat_out),
        (gskip_ref, gskip_out), (ga_ref, ga_out),
    )
    stores = [pltpu.make_async_copy(s, d, out_sem.at[i]) for i, (s, d) in enumerate(pairs)]
    loads[0].wait()
    for p in range(up_chunks):
        at = ((p % nx) * ny + p // nx) * g_size
        block = gbank_ref[at:at + g_size, :].astype(F32)
        gb_ref[0, :, p * LANES:(p + 1) * LANES] = block[:max_rank]
        gb_ref[1, :, p * LANES:(p + 1) * LANES] = block[max_rank:]
    stores[0].start()
    for k in range(1, 4):
        loads[k].wait()
        stores[k].start()
    size = min(LANES, width)
    for k in range(a_chunks):
        at = (up_chunks + k) * g_size
        block = gbank_ref[at:at + g_size, :].astype(F32)
        ga_ref[0, :, k * size:(k + 1) * size] = block[:max_rank, :size]
        ga_ref[1, :, k * size:(k + 1) * size] = block[max_rank:, :size]
        at = (up_chunks + a_chunks + k) * g_size
        block = gbank_ref[at:at + g_size, :].astype(F32)
        gskip_ref[:, k * size:(k + 1) * size] = (block[0:1] + block[max_rank:max_rank + 1])[:, :size]
    stores[4].start()
    stores[5].start()
    for store in stores:
        store.wait()


def local(
    signal, gating, cotangent, filt, skip, output_projection,
    adapter_down_bank, adapter_up_bank, adapter_index, sequence_rank, real_length,
):
    n = lax.axis_size("seq")
    width = signal.shape[2]
    half = cotangent.shape[2]
    cols = output_projection.shape[1] // 2
    max_rank = adapter_up_bank.shape[1]
    a_chunks = -(-width // LANES)
    n_own = half // LANES + 2 * a_chunks
    piece = LANES // SUB
    nx = min(4, n // 2)
    far_cols = 2 * cols // nx
    consts = [jnp.asarray(t) for t in tables(n)]
    rows = consts[4].shape[0]
    vmem = pl.BlockSpec(memory_space=pltpu.VMEM)
    smem = pl.BlockSpec(memory_space=pltpu.SMEM)
    hbm = pl.BlockSpec(memory_space=pltpu.HBM)
    dma = pltpu.SemaphoreType.DMA
    arrays = [
        signal[0], gating[0], cotangent[0], filt, skip[None], output_projection,
        jnp.swapaxes(adapter_down_bank, 1, 2), adapter_up_bank, *consts,
    ]
    block = pltpu.VMEM((n, PER, LANES), F32)
    narrow = pltpu.VMEM((n, PER, LANES), BF)
    eight = pltpu.VMEM((8 * n, LANES), F32)
    wide = pltpu.VMEM((width, LANES), F32)
    spec = pltpu.VMEM((PER * rows, 2 * LANES), F32)
    rank = pltpu.VMEM((max_rank, LANES), F32)
    outs = pl.pallas_call(
        functools.partial(kernel, n),
        out_shape=(
            jax.ShapeDtypeStruct((LANES, width), BF),
            jax.ShapeDtypeStruct((LANES, width), BF),
            jax.ShapeDtypeStruct((LANES, width), F32),
            jax.ShapeDtypeStruct((2 * max_rank * n_own, LANES), BF),
        ),
        in_specs=[smem] * 3 + [hbm] * len(arrays),
        out_specs=(hbm,) * 4,
        scratch_shapes=[
            pltpu.VMEM((LANES, width), BF),
            pltpu.VMEM((LANES, width), BF),
            pltpu.VMEM((LANES, width), F32),
        ] + [pltpu.VMEM(a.shape, a.dtype) for a in arrays] + [
            pltpu.VMEM((LANES, half), BF),
            wide, wide, wide, spec, spec, spec,
            eight, eight, block, block, narrow, narrow, narrow, narrow, narrow, narrow,
            block, block, block, block, block, block,
            pltpu.VMEM((LANES, cols), BF),
            pltpu.VMEM((SUB, 2, piece, cols), BF),
            pltpu.VMEM((nx, LANES, far_cols), BF),
            pltpu.VMEM((width, far_cols), BF),
            pltpu.VMEM(((nx - 1) * LANES, width), BF),
            pltpu.VMEM((nx - 1, LANES, width), BF),
            pltpu.VMEM((width, cols), BF),
            pltpu.VMEM((LANES, width), BF),
            pltpu.VMEM((LANES, width), BF),
            pltpu.VMEM((SUB, 2 * piece, width), BF),
            pltpu.VMEM((SUB, 2 * piece, width), BF),
            pltpu.VMEM((SUB, 2 * piece, width), BF),
            pltpu.VMEM((2, LANES, width), BF),
            rank, rank, rank, rank,
            pltpu.VMEM((max_rank, n_own * LANES), BF),
            pltpu.VMEM((16 * n, LANES), BF),
            pltpu.VMEM((2 * max_rank, LANES), F32),
            pltpu.VMEM((3, 2 * max_rank, LANES), F32),
            pltpu.VMEM((2 * max_rank, LANES), BF),
            pltpu.VMEM((2 * max_rank * n_own, LANES), BF),
            pltpu.VMEM((width, LANES), BF),
            pltpu.VMEM((3, width // 4, LANES), BF),
            wide,
            pltpu.VMEM((width // 4, LANES), BF),
            pltpu.VMEM((width, LANES), BF),
            dma((len(arrays),)), dma((4,)), dma((5,)), dma((5,)), dma((SUB, 4)), dma((SUB,)), dma((2,)), dma((2,)),
            dma((2,)), dma((SUB,)), dma((SUB,)), dma((SUB, 4)), dma, dma((2,)), dma((2,)), dma((2,)),
            dma((4,)), dma, dma((4,)), dma((4,)), dma,
            dma((4,)), dma, dma((2,)), dma((2,)), dma((8,)), dma, dma((nx,)), dma,
        ],
        compiler_params=pltpu.CompilerParams(
            collective_id=0, has_side_effects=True, vmem_limit_bytes=VMEM_LIMIT
        ),
    )(adapter_index, sequence_rank, real_length, *arrays)
    grad_signal, grad_gating, grad_filt, grad_skip, grad_a, grad_b = pl.pallas_call(
        functools.partial(finish_kernel, n // (2 * nx)),
        out_shape=(
            jax.ShapeDtypeStruct((LANES, width), BF),
            jax.ShapeDtypeStruct((LANES, width), BF),
            jax.ShapeDtypeStruct((LANES, width), F32),
            jax.ShapeDtypeStruct((1, width), F32),
            jax.ShapeDtypeStruct((2, max_rank, width), F32),
            jax.ShapeDtypeStruct((2, max_rank, half), F32),
        ),
        in_specs=[hbm] * 4,
        out_specs=(hbm,) * 6,
        scratch_shapes=[
            pltpu.VMEM((LANES, width), BF), pltpu.VMEM((LANES, width), BF), pltpu.VMEM((LANES, width), F32),
            pltpu.VMEM((2 * max_rank * n_own, LANES), BF), pltpu.VMEM((1, width), F32),
            pltpu.VMEM((2, max_rank, width), F32), pltpu.VMEM((2, max_rank, half), F32),
            dma((4,)), dma((6,)),
        ],
        compiler_params=pltpu.CompilerParams(vmem_limit_bytes=VMEM_LIMIT),
    )(*outs)
    return (grad_signal[None], grad_gating[None], grad_filt, grad_skip[0], jnp.swapaxes(grad_a, 1, 2), grad_b)


def solution(mesh):
    placed = (
        P("dp", "seq", "chan"), P("dp", "seq", "chan"), P("dp", "seq", "chan"), P("seq", "chan"),
        P("chan"), P("chan", "dp"), P(None, "chan", None), P(None, None, "chan"),
        P("dp"), P("dp"), P("dp"),
    )
    return jax.shard_map(
        local,
        mesh=mesh,
        in_specs=placed,
        out_specs=(
            P("dp", "seq", "chan"), P("dp", "seq", "chan"), P("seq", "chan"), P("chan"),
            P(None, "chan", None), P(None, None, "chan"),
        ),
        check_vma=False,
    )
```
